32 devices in a mesh: seq: 8 (over z, y), wt: 4 (over x, core).
Axes of the slice: x: 2, y: 2, z: 4, core: 2. Of those that a mesh axis runs over, the one named last changes fastest.
Arguments:
- tokens: bfloat16 [4, 2048, 2048], P('wt', 'seq'), may hold values from -6 to 6
- in_proj: bfloat16 [3, 2048, 2048], P(None, None, 'wt'), may hold values from -0.125 to 0.125
- out_proj: bfloat16 [2048, 2048], P('wt'), may hold values from -0.125 to 0.125
- gate_up: bfloat16 [2, 2048, 5632], P(None, None, 'wt'), may hold values from -0.125 to 0.125
- down: bfloat16 [5632, 2048], P('wt'), may hold values from -0.078125 to 0.078125
- norm1_gain: float32 [2048], replicated, may hold values from 0.5 to 1.5
- mixer_gain: float32 [2048], replicated, may hold values from 0.5 to 1.5
- norm2_gain: float32 [2048], replicated, may hold values from 0.5 to 1.5
- lower_bound: float32 [2048], replicated, may hold values from 0.9 to 1
- cotangent: bfloat16 [4, 2048, 2048], P('wt', 'seq'), may hold values from -6 to 6
Outputs:
- block_out: bfloat16 [4, 2048, 2048], P('wt', 'seq')
- input_grad: float32 [4, 2048, 2048], P('wt', 'seq')
- in_proj_grad: float32 [3, 2048, 2048], P(None, 'seq', 'wt')
- out_proj_grad: float32 [2048, 2048], P('wt', 'seq')
- gate_up_grad: float32 [2, 2048, 5632], P(None, 'seq', 'wt')
- down_grad: float32 [5632, 2048], P('wt', 'seq')
- norm1_grad: float32 [2048], P('wt')
- mixer_grad: float32 [2048], P('wt')
- norm2_grad: float32 [2048], P('wt')
- bound_grad: float32 [2048], P('wt')
The draws below stay inside these ranges and needn't reach their ends.
All inputs are finite; a program needn't handle non-finite values.
Results may differ from the reference program's by a relative error of at most 0.015.
Values may be sent and summed in bfloat16 or wider, within the bound.
No kernel may reach another device: no remote copies, remote signals or barrier semaphores. Data moves between devices by JAX's collectives and lax.ppermute only.
A program may use at most 320 MiB of HBM per device.

```python
import jax
import jax.numpy as jnp
from jax import lax

D = 2048
FF = 5632
SEQS = 4
LENGTH = 2048


def draw_lower_bound(key, part):
    pick_key, slow_key, fast_key = jax.random.split(key, 3)
    share = 0.5
    slow = jax.random.uniform(pick_key, (D,)) < share
    length = float(LENGTH)
    slow_rate = jnp.exp(jax.random.uniform(slow_key, (D,), minval=jnp.log(0.25 / length), maxval=jnp.log(4.0 / length)))
    fast_rate = jnp.exp(jax.random.uniform(fast_key, (D,), minval=jnp.log(0.02), maxval=jnp.log(0.08)))
    return (1.0 - jnp.where(slow, slow_rate, fast_rate)).astype(jnp.float32)


def shard_levels(key, extent, shards, low, top_value):
    level, own = 1.0, jax.random.fold_in(key, 6)
    for position, shards_of in shards:
        steps = jnp.exp(jax.random.uniform(jax.random.fold_in(own, position), (shards_of,), jnp.float32, low / len(shards), top_value / len(shards)))
        level = level * jnp.repeat(steps, extent[position] // shards_of).reshape([-1 if axis == position else 1 for axis in range(len(extent))])
    return level


def centred(rng, dims, scale, bound, shards=(), kind=jnp.bfloat16):
    level = shard_levels(rng, dims, shards, -0.22, 0.18) if shards else 1.0
    array = jax.random.normal(rng, dims, jnp.float32) * scale * level
    return jnp.minimum(jnp.maximum(array, -bound), bound).astype(kind)


def setup_inputs(seed: int = 0) -> dict:
    streams_of = jax.random.split(jax.random.key(seed), 11)
    return {
        "tokens": centred(streams_of[0], (SEQS, LENGTH, D), 1.0, 6.0, ((0, 4), (1, 8))),
        "in_proj": centred(streams_of[1], (3, D, D), D ** -0.5, 0.125, ((2, 4),)),
        "out_proj": centred(streams_of[2], (D, D), D ** -0.5, 0.125, ((0, 4),)),
        "gate_up": centred(streams_of[3], (2, D, FF), D ** -0.5, 0.125, ((2, 4),)),
        "down": centred(streams_of[4], (FF, D), FF ** -0.5, 0.078125, ((0, 4),)),
        "norm1_gain": jnp.clip(1.0 + 0.1 * jax.random.normal(streams_of[5], (D,), jnp.float32), 0.5, 1.5),
        "mixer_gain": jnp.clip(1.0 + 0.1 * jax.random.normal(streams_of[6], (D,), jnp.float32), 0.5, 1.5),
        "norm2_gain": jnp.clip(1.0 + 0.1 * jax.random.normal(streams_of[7], (D,), jnp.float32), 0.5, 1.5),
        "lower_bound": draw_lower_bound(jax.random.fold_in(streams_of[10], 71), 0),
        "cotangent": centred(streams_of[9], (SEQS, LENGTH, D), 1.0, 6.0, ((0, 4), (1, 8))),
    }


EPS = 1e-06

@jax.custom_vjp
def low(v):
    return lax.optimization_barrier(v.astype(jnp.bfloat16)).astype(jnp.float32)

@jax.custom_vjp
def low_back(v):
    return v

def low_keep(v):
    return (low(v), None)

def low_pass(kept, grad):
    return (grad,)

def back_keep(v):
    return (v, None)

def back_low(kept, grad):
    return (low(grad),)
low.defvjp(low_keep, low_pass)
low_back.defvjp(back_keep, back_low)

def rms_scale(values):
    return lax.rsqrt(lax.optimization_barrier(jnp.mean(values * values, axis=-1, keepdims=True)) + EPS)

def combine_chain(earlier, later):
    return (earlier[0] * later[0], later[0] * earlier[1] + later[1])

def highest(left, right):
    return jnp.dot(left, right, precision=lax.Precision.HIGHEST, preferred_element_type=jnp.float32)

def layer(inputs, in_proj, out_proj, gate_up, down, norm1_gain, mixer_gain, norm2_gain, lower_bound):
    normed = low(inputs * rms_scale(inputs) * norm1_gain)
    pre_input = low_back(highest(normed, in_proj[0]))
    pre_forget = low_back(highest(normed, in_proj[1]))
    pre_gate = low_back(highest(normed, in_proj[2]))
    forget = lower_bound + (1.0 - lower_bound) * jax.nn.sigmoid(pre_forget)
    drive = jax.nn.silu(pre_input) * (1.0 - forget)
    state = lax.associative_scan(combine_chain, (forget, drive), axis=0)[1]
    mixed = low(state * rms_scale(state) * mixer_gain * jax.nn.silu(pre_gate))
    middle = inputs + low_back(highest(mixed, out_proj))
    normed_two = low(middle * rms_scale(middle) * norm2_gain)
    gate_part = low_back(highest(normed_two, gate_up[0]))
    up_part = low_back(highest(normed_two, gate_up[1]))
    hidden = low(jax.nn.silu(gate_part) * up_part)
    return middle + low_back(highest(hidden, down))

def reference(tokens, in_proj, out_proj, gate_up, down, norm1_gain, mixer_gain, norm2_gain, lower_bound, cotangent):
    weights = (in_proj.astype(jnp.float32), out_proj.astype(jnp.float32), gate_up.astype(jnp.float32), down.astype(jnp.float32))
    gains = (norm1_gain, mixer_gain, norm2_gain, lower_bound)

    def forward(weight_set, gain_set, inputs):

        def single(sequence):
            return layer(sequence, weight_set[0], weight_set[1], weight_set[2], weight_set[3], gain_set[0], gain_set[1], gain_set[2], gain_set[3])
        return lax.map(single, inputs)
    outputs, pullback = jax.vjp(forward, weights, gains, tokens.astype(jnp.float32))
    grad_weights, grad_gains, grad_tokens = pullback(cotangent.astype(jnp.float32))
    return (outputs.astype(jnp.bfloat16), grad_tokens, grad_weights[0], grad_weights[1], grad_weights[2], grad_weights[3], grad_gains[0], grad_gains[1], grad_gains[2], grad_gains[3])
```

```python
import functools

import jax
import jax.numpy as jnp
from jax import lax
from jax.experimental import pallas as pl
from jax.experimental.pallas import tpu as pltpu
from jax.sharding import PartitionSpec as P

EPS = 1e-06
BF = jnp.bfloat16
F32 = jnp.float32
CHUNKS = 8


def swap(values, axis, bit):
    size = lax.axis_size(axis)
    return lax.ppermute(values, axis, [(i, i ^ bit) for i in range(size)])


def shift(values, axis, step):
    size = lax.axis_size(axis)
    pairs = [(i, i + step) for i in range(size) if 0 <= i + step < size]
    return lax.ppermute(values, axis, pairs)


def rms_scale(values):
    return lax.rsqrt(jnp.mean(values * values, axis=-1, keepdims=True) + EPS)


def norm_back(grad_normed, values, scale, weight):
    weighted = grad_normed * weight
    return scale * weighted - values * (scale * scale * scale) * jnp.mean(
        weighted * values, axis=-1, keepdims=True
    )


def sigmoid(v):
    return 1.0 / (1.0 + jnp.exp(-v))


def scan_local_kernel(pi_ref, pf_ref, lb_ref, loc_ref, cum_ref, tot_ref):
    rows = loc_ref.shape[1]
    steps = rows // CHUNKS
    lb = lb_ref[...]
    s = jnp.zeros((CHUNKS, loc_ref.shape[2]), F32)
    p = jnp.ones_like(s)
    for t in range(steps):
        at = pl.ds(t, CHUNKS, stride=steps)
        pi = pi_ref[0, 0, at, :]
        sig = sigmoid(pf_ref[0, 0, at, :])
        f = lb + (1.0 - lb) * sig
        d = pi * sigmoid(pi) * ((1.0 - lb) * (1.0 - sig))
        s = f * s + d
        p = p * f
        loc_ref[0, at, :] = s
        cum_ref[0, at, :] = p
    a = p[0:1]
    b = s[0:1]
    for c in range(1, CHUNKS):
        b = p[c : c + 1] * b + s[c : c + 1]
        a = a * p[c : c + 1]
    tot_ref[0, 0:1, :] = a
    tot_ref[0, 1:2, :] = b


def scan_mix_kernel(loc_ref, cum_ref, pg_ref, carry_ref, gain_ref, state_ref, mix_ref, sq_ref):
    rows = loc_ref.shape[1]
    steps = rows // CHUNKS
    first = pl.program_id(1) == 0
    gain = gain_ref[...]
    cin = carry_ref[0]
    for c in range(CHUNKS):
        at = pl.ds(c * steps, steps)
        st = loc_ref[0, at, :] + cum_ref[0, at, :] * cin
        cin = st[steps - 1 : steps]
        pg = pg_ref[0, 0, at, :]
        state_ref[0, at, :] = st
        mix_ref[0, at, :] = (st * gain * (pg * sigmoid(pg))).astype(BF)
        part = jnp.sum(st * st, axis=-1, keepdims=True)

        @pl.when(first)
        def _():
            sq_ref[0, at, :] = part

        @pl.when(jnp.logical_not(first))
        def _():
            sq_ref[0, at, :] += part


def back_local_kernel(
    width,
    gm_ref,
    pg_ref,
    pf_ref,
    state_ref,
    scale_ref,
    inner_ref,
    gain_ref,
    lb_ref,
    mixed_ref,
    gpg_ref,
    loc_ref,
    cum_ref,
    tot_ref,
    term_ref,
):
    rows = loc_ref.shape[1]
    steps = rows // CHUNKS
    gain = gain_ref[...]
    lb = lb_ref[...]
    term = jnp.zeros((1, loc_ref.shape[2]), F32)
    for c in range(CHUNKS):
        at = pl.ds(c * steps, steps)
        scale = scale_ref[0, at, :]
        coef = scale * scale * scale * inner_ref[0, at, :] * (1.0 / width)
        pg = pg_ref[0, 0, at, :]
        gm = gm_ref[0, at, :]
        st = state_ref[0, at, :]
        sig = sigmoid(pg)
        act = pg * sig
        unit = st * scale
        gact = gm * act
        mixed_ref[0, at, :] = (unit * gain * act).astype(BF)
        gpg_ref[0, at, :] = (gm * gain * unit * (sig * (1.0 + pg * (1.0 - sig)))).astype(BF)
        term = term + jnp.sum(gact * unit, axis=0, keepdims=True)
        loc_ref[0, at, :] = scale * (gact * gain) - st * coef
    term_ref[0] = term
    s = jnp.zeros((CHUNKS, loc_ref.shape[2]), F32)
    q = jnp.ones_like(s)
    for t in range(steps - 1, -1, -1):
        at = pl.ds(t, CHUNKS, stride=steps)
        f = lb + (1.0 - lb) * sigmoid(pf_ref[0, 0, at, :])
        adj = loc_ref[0, at, :] + s
        loc_ref[0, at, :] = adj
        cum_ref[0, at, :] = q
        s = f * adj
        q = q * f
    last = CHUNKS - 1
    a = q[last : last + 1]
    b = s[last : last + 1]
    for c in range(CHUNKS - 2, -1, -1):
        b = q[c : c + 1] * b + s[c : c + 1]
        a = a * q[c : c + 1]
    tot_ref[0, 0:1, :] = a
    tot_ref[0, 1:2, :] = b


def back_mix_kernel(
    loc_ref, cum_ref, state_ref, pi_ref, pf_ref, carry_ref, prior_ref, lb_ref, gpi_ref, gpf_ref, term_ref
):
    rows = loc_ref.shape[1]
    steps = rows // CHUNKS
    lb = lb_ref[...]
    rest = 1.0 - lb
    cin = carry_ref[0]
    term = jnp.zeros((1, loc_ref.shape[2]), F32)
    top = lax.broadcasted_iota(jnp.int32, (steps, loc_ref.shape[2]), 0) == 0
    for c in range(CHUNKS - 1, -1, -1):
        at = pl.ds(c * steps, steps)
        adj = loc_ref[0, at, :] + cum_ref[0, at, :] * cin
        pi = pi_ref[0, 0, at, :]
        sig = sigmoid(pf_ref[0, 0, at, :])
        cin = (lb + rest * sig[0:1]) * adj[0:1]
        st = state_ref[0, at, :]
        before = prior_ref[0] if c == 0 else state_ref[0, pl.ds(c * steps - 1, 1), :]
        prev = jnp.where(top, before, pltpu.roll(st, 1, 0))
        sig_in = sigmoid(pi)
        total = adj * (prev - pi * sig_in)
        left = 1.0 - sig
        gpi_ref[0, at, :] = (adj * (rest * left) * (sig_in * (1.0 + pi * (1.0 - sig_in)))).astype(BF)
        gpf_ref[0, at, :] = (total * rest * sig * left).astype(BF)
        term = term + jnp.sum(total * left, axis=0, keepdims=True)
    term_ref[0] = term


def tile_of(chans):
    return 128 if chans % 128 == 0 else chans


def sds(shape, dtype=F32):
    return jax.ShapeDtypeStruct(shape, dtype)


def piece_specs(rows, tile):
    full = pl.BlockSpec((1, rows, tile), lambda g, c: (g, 0, c))
    row = pl.BlockSpec((1, tile), lambda g, c: (0, c))
    per = pl.BlockSpec((1, 1, tile), lambda g, c: (g, 0, c))
    tot = pl.BlockSpec((1, 2, tile), lambda g, c: (g, 0, c))
    col = pl.BlockSpec((1, rows, 1), lambda g, c: (g, 0, 0))

    def pick(k):
        return pl.BlockSpec((1, 1, rows, tile), lambda g, c: (k, g, 0, c))

    return full, row, per, tot, col, pick


def cost(elements, arrays):
    return pl.CostEstimate(
        flops=20 * elements, bytes_accessed=4 * arrays * elements, transcendentals=2 * elements
    )


def scan_local(project, lower):
    _, groups, rows, chans = project.shape
    tile = tile_of(chans)
    full, row, per, tot, col, pick = piece_specs(rows, tile)
    return pl.pallas_call(
        scan_local_kernel,
        grid=(groups, chans // tile),
        in_specs=[pick(0), pick(1), row],
        out_specs=[full, full, tot],
        out_shape=[sds((groups, rows, chans)), sds((groups, rows, chans)), sds((groups, 2, chans))],
        cost_estimate=cost(groups * rows * chans, 4),
        name="scan_local",
    )(project, project, lower)


def scan_mix(loc, cum, project, carry, gain):
    groups, rows, chans = loc.shape
    tile = tile_of(chans)
    full, row, per, tot, col, pick = piece_specs(rows, tile)
    return pl.pallas_call(
        scan_mix_kernel,
        grid=(groups, chans // tile),
        in_specs=[full, full, pick(2), per, row],
        out_specs=[full, full, col],
        out_shape=[
            sds((groups, rows, chans)),
            sds((groups, rows, chans), BF),
            sds((groups, rows, 1)),
        ],
        cost_estimate=cost(groups * rows * chans, 5),
        name="scan_mix",
    )(loc, cum, project, carry, gain)


def back_local(width, grad_mixed, project, state, scale, inner, gain, lower):
    groups, rows, chans = state.shape
    tile = tile_of(chans)
    full, row, per, tot, col, pick = piece_specs(rows, tile)
    shape = (groups, rows, chans)
    return pl.pallas_call(
        functools.partial(back_local_kernel, width),
        grid=(groups, chans // tile),
        in_specs=[full, pick(2), pick(1), full, col, col, row, row],
        out_specs=[full, full, full, full, tot, per],
        out_shape=[
            sds(shape, BF),
            sds(shape, BF),
            sds(shape),
            sds(shape),
            sds((groups, 2, chans)),
            sds((groups, 1, chans)),
        ],
        cost_estimate=cost(groups * rows * chans, 7),
        name="back_local",
    )(grad_mixed, project, project, state, scale, inner, gain, lower)


def back_mix(loc, cum, state, project, carry, prior, lower):
    groups, rows, chans = state.shape
    tile = tile_of(chans)
    full, row, per, tot, col, pick = piece_specs(rows, tile)
    shape = (groups, rows, chans)
    return pl.pallas_call(
        back_mix_kernel,
        grid=(groups, chans // tile),
        in_specs=[full, full, full, pick(0), pick(1), per, per, row],
        out_specs=[full, full, per],
        out_shape=[sds(shape, BF), sds(shape, BF), sds((groups, 1, chans))],
        cost_estimate=cost(groups * rows * chans, 6),
        name="back_mix",
    )(loc, cum, state, project, project, carry, prior, lower)


def chain_carry(total, reverse):
    size = lax.axis_size("seq")
    odd = (lax.axis_index("seq") % 2) == 1
    other = swap(total, "seq", 1)
    low_a, low_b = jnp.where(odd, other[:, 0], total[:, 0]), jnp.where(odd, other[:, 1], total[:, 1])
    high_a, high_b = jnp.where(odd, total[:, 0], other[:, 0]), jnp.where(odd, total[:, 1], other[:, 1])
    if reverse:
        pair = jnp.stack([low_a * high_a, low_a * high_b + low_b], axis=1)
    else:
        pair = jnp.stack([low_a * high_a, high_a * low_b + high_b], axis=1)
    sign = -1 if reverse else 1
    reached = [shift(pair, "seq", 2 * sign * d) for d in range(1, size // 2)]
    enter = jnp.zeros_like(total[:, 0])
    for got in reversed(reached):
        enter = got[:, 0] * enter + got[:, 1]
    if reverse:
        enter = jnp.where(odd, enter, high_a * enter + high_b)
    else:
        enter = jnp.where(odd, low_a * enter + low_b, enter)
    return enter[:, None]


def far_of(own):
    step = swap(own, "wt", 2)
    return step, swap(step, "wt", 1)


def sum_to_owner(near, far):
    across = far[0].astype(F32) + swap(far[1], "wt", 1).astype(F32)
    moved = swap(across.astype(near.dtype), "wt", 2)
    own = near[0].astype(F32) + swap(near[1], "wt", 1).astype(F32)
    return own + moved.astype(F32)


def block_order(bits, count):
    order = [0]
    for bit in reversed(bits):
        order = order + [j ^ bit for j in order]
    return order


def reordered(values, axis, order, count):
    me = lax.axis_index("seq")
    size = values.shape[axis] // count
    return [lax.dynamic_slice_in_dim(values, (me ^ j) * size, size, axis) for j in order]


def halving(send, keep, bits, axis):
    for n, bit in enumerate(bits):
        got = swap(send, "seq", bit)
        total = keep.astype(F32) + got.astype(F32)
        if n == len(bits) - 1:
            return total
        total = total.astype(BF)
        half = total.shape[axis] // 2
        keep = lax.slice_in_dim(total, 0, half, axis=axis)
        send = lax.slice_in_dim(total, half, 2 * half, axis=axis)


def seq_bits():
    size = lax.axis_size("seq")
    bits = []
    bit = 1
    while bit < size:
        bits.append(bit)
        bit *= 2
    return bits


def left_product(left, right):
    return lax.dot_general(left, right, (((0,), (0,)), ((), ())), preferred_element_type=F32)


def right_product(left, right):
    return lax.dot_general(left, right, (((1,), (1,)), ((), ())), preferred_element_type=F32)


def reduced_left(left, right, bits):
    count = lax.axis_size("seq")
    blocks = reordered(left, 1, block_order(bits, count), count)
    half = count // 2
    send = left_product(jnp.concatenate(blocks[half:], axis=1), right).astype(BF)
    keep = left_product(jnp.concatenate(blocks[:half], axis=1), right).astype(BF)
    return halving(send, keep, bits, 0)


def reduced_right(left, right, bits):
    count = lax.axis_size("seq")
    blocks = reordered(right, 1, block_order(bits, count), count)
    half = count // 2
    send = left_product(left, jnp.concatenate(blocks[half:], axis=1)).astype(BF)
    keep = left_product(left, jnp.concatenate(blocks[:half], axis=1)).astype(BF)
    return halving(send, keep, bits, 1)


def on_device(
    tokens,
    in_proj,
    out_proj,
    gate_up,
    down,
    norm1_gain,
    mixer_gain,
    norm2_gain,
    lower_bound,
    cotangent,
):
    width = in_proj.shape[1]
    chans = in_proj.shape[2]
    inputs = tokens[0].astype(F32)
    grad_out = cotangent[0]
    upstream = grad_out.astype(F32)
    rows = inputs.shape[0]
    bits = seq_bits()
    y_first = bits
    z_first = bits[1:] + bits[:1]

    offset = lax.axis_index("wt") * chans
    lower_use = lax.dynamic_slice_in_dim(lower_bound, offset, chans)[None]
    mixer_use = lax.dynamic_slice_in_dim(mixer_gain, offset, chans)[None]

    def pair(one, two):
        return jnp.concatenate([one, two], axis=0)

    def grouped(values):
        return values.reshape(2, rows, values.shape[-1])

    scale_one = rms_scale(inputs)
    normed = (inputs * scale_one * norm1_gain).astype(BF)
    normed_near = pair(normed, swap(normed, "wt", 1))
    normed_far = pair(*far_of(normed))
    grad_near = pair(grad_out, swap(grad_out, "wt", 1))
    grad_far = pair(*far_of(grad_out))

    def project(piece):
        return jnp.einsum("rd,kdc->krc", piece, in_proj, preferred_element_type=F32).reshape(
            3, 2, rows, chans
        )

    def forward(piece):
        pre = project(piece)
        loc, cum, total = scan_local(pre, lower_use)
        enter = chain_carry(total, False)
        state, mix, squares = scan_mix(loc, cum, pre, enter, mixer_use)
        branch = jnp.dot(mix.reshape(2 * rows, chans), out_proj, preferred_element_type=F32)
        return pre, enter, state, squares, grouped(branch.astype(BF))

    pre_n, enter_n, state_n, squares_n, branch_n = forward(normed_near)
    pre_f, enter_f, state_f, squares_f, branch_f = forward(normed_far)
    branch_raw = sum_to_owner(branch_n, branch_f)
    squares = sum_to_owner(squares_n.reshape(2, 1, rows), squares_f.reshape(2, 1, rows))
    scale_two = lax.rsqrt(squares / width + EPS)
    middle = inputs + branch_raw * scale_two.reshape(rows, 1)

    scale_three = rms_scale(middle)
    normed_two = (middle * scale_three * norm2_gain).astype(BF)
    two_near = pair(normed_two, swap(normed_two, "wt", 1))
    two_far = pair(*far_of(normed_two))

    def feed(piece, grad_rows):
        grad_hidden = right_product(grad_rows, down)
        gate_part = jnp.dot(piece, gate_up[0], preferred_element_type=F32)
        up_part = jnp.dot(piece, gate_up[1], preferred_element_type=F32)
        sig = sigmoid(gate_part)
        act = gate_part * sig
        hidden = (act * up_part).astype(BF)
        grad_gate = (grad_hidden * up_part * sig * (1.0 + gate_part * (1.0 - sig))).astype(BF)
        grad_up = (grad_hidden * act).astype(BF)
        back = right_product(grad_gate, gate_up[0]) + right_product(grad_up, gate_up[1])
        return hidden, grad_gate, grad_up, grouped(back.astype(BF))

    hidden_n, gg_n, gu_n, back_n = feed(two_near, grad_near)
    hidden_f, gg_f, gu_f, back_f = feed(two_far, grad_far)
    grad_normed_two = sum_to_owner(back_n, back_f)

    grad_middle = upstream + norm_back(grad_normed_two, middle, scale_three, norm2_gain)
    norm2_term = jnp.sum(grad_normed_two * middle * scale_three, axis=0)

    grad_branch = grad_middle.astype(BF)
    inner = jnp.sum(grad_branch.astype(F32) * branch_raw, axis=-1)
    small = jnp.stack([scale_two.reshape(rows), inner])[None]
    small_near = pair(small, swap(small, "wt", 1))
    small_far = pair(*far_of(small))
    gb_near = pair(grad_branch, swap(grad_branch, "wt", 1))
    gb_far = pair(*far_of(grad_branch))

    def backward(gb, small_piece, pre, state, enter):
        grad_mixed = grouped(right_product(gb, out_proj))
        scale = small_piece[:, 0, :, None]
        inner_piece = small_piece[:, 1, :, None]
        mixed, gpg, loc, cum, total, mixer_term = back_local(
            width, grad_mixed, pre, state, scale, inner_piece, mixer_use, lower_use
        )
        carry = chain_carry(total, True)
        gpi, gpf, bound_term = back_mix(loc, cum, state, pre, carry, enter, lower_use)
        flat = [v.reshape(2 * rows, chans) for v in (gpi, gpf, gpg)]
        back = (
            right_product(flat[0], in_proj[0])
            + right_product(flat[1], in_proj[1])
            + right_product(flat[2], in_proj[2])
        )
        return (
            mixed.reshape(2 * rows, chans),
            flat,
            jnp.sum(mixer_term, axis=(0, 1)),
            jnp.sum(bound_term, axis=(0, 1)),
            grouped(back.astype(BF)),
        )

    mixed_n, flat_n, mixer_n, bound_n, down_n = backward(gb_near, small_near, pre_n, state_n, enter_n)
    mixed_f, flat_f, mixer_f, bound_f, down_f = backward(gb_far, small_far, pre_f, state_f, enter_f)
    grad_normed = sum_to_owner(down_n, down_f)
    norm1_term = jnp.sum(grad_normed * inputs * scale_one, axis=0)
    grad_inputs = grad_middle + norm_back(grad_normed, inputs, scale_one, norm1_gain)

    ffn_n = grouped(jnp.dot(hidden_n, down, preferred_element_type=F32).astype(BF))
    ffn_f = grouped(jnp.dot(hidden_f, down, preferred_element_type=F32).astype(BF))
    result = middle + sum_to_owner(ffn_n, ffn_f)

    two_rows = pair(two_near, two_far)
    gate_grad = reduced_left(two_rows, pair(gg_n, gg_f), y_first)
    up_grad = reduced_left(two_rows, pair(gu_n, gu_f), y_first)
    down_grad = reduced_right(pair(hidden_n, hidden_f), pair(grad_near, grad_far), y_first)
    out_grad = reduced_right(pair(mixed_n, mixed_f), pair(gb_near, gb_far), z_first)
    normed_rows = pair(normed_near, normed_far)
    in_grads = [
        reduced_left(normed_rows, pair(flat_n[k], flat_f[k]), z_first if k == 2 else y_first)
        for k in range(3)
    ]

    me = lax.axis_index("wt")

    def block(values, j):
        return lax.dynamic_slice_in_dim(values, (me ^ j) * chans, chans, values.ndim - 1)

    norm_terms = jnp.stack([norm1_term, norm2_term])
    low = jnp.stack([block(norm_terms, 0), block(norm_terms, 1)])
    high = jnp.stack([block(norm_terms, 2), block(norm_terms, 3)])
    norms = sum_to_owner(low, high)
    gains = jnp.stack([norms[0], mixer_n + mixer_f, norms[1], bound_n + bound_f])
    for bit in bits:
        gains = gains + swap(gains, "seq", bit)

    return (
        result.astype(BF)[None],
        grad_inputs[None],
        jnp.stack(in_grads),
        out_grad,
        jnp.stack([gate_grad, up_grad]),
        down_grad,
        gains[0],
        gains[1],
        gains[2],
        gains[3],
    )


def solution(mesh):
    placed = (
        P("wt", "seq", None),
        P(None, None, "wt"),
        P("wt", None),
        P(None, None, "wt"),
        P("wt", None),
        P(),
        P(),
        P(),
        P(),
        P("wt", "seq", None),
    )
    return jax.shard_map(
        on_device,
        mesh=mesh,
        in_specs=placed,
        out_specs=(
            P("wt", "seq", None),
            P("wt", "seq", None),
            P(None, "seq", "wt"),
            P("wt", "seq"),
            P(None, "seq", "wt"),
            P("wt", "seq"),
            P("wt"),
            P("wt"),
            P("wt"),
            P("wt"),
        ),
        check_vma=False,
    )
```

```python
import functools

import jax
import jax.numpy as jnp
from jax import lax
from jax.experimental import pallas as pl
from jax.experimental.pallas import tpu as pltpu
from jax.sharding import PartitionSpec as P

EPS = 1e-06
BF = jnp.bfloat16
F32 = jnp.float32
CHUNKS = 8


def swap(values, axis, bit):
    size = lax.axis_size(axis)
    return lax.ppermute(values, axis, [(i, i ^ bit) for i in range(size)])


def shift(values, axis, step):
    size = lax.axis_size(axis)
    pairs = [(i, i + step) for i in range(size) if 0 <= i + step < size]
    return lax.ppermute(values, axis, pairs)


def rms_scale(values):
    return lax.rsqrt(jnp.mean(values * values, axis=-1, keepdims=True) + EPS)


def norm_back(grad_normed, values, scale, weight):
    weighted = grad_normed * weight
    return scale * weighted - values * (scale * scale * scale) * jnp.mean(
        weighted * values, axis=-1, keepdims=True
    )


def sigmoid(v):
    return 0.5 * jnp.tanh(0.5 * v) + 0.5


ANYWHERE = pl.BlockSpec(memory_space=pl.ANY)
EXTRA = 16
VMEM_LIMIT = 60 * 1024 * 1024


def sds(shape, dtype=F32):
    return jax.ShapeDtypeStruct(shape, dtype)


def call(kernel, name, grid, inputs, outputs, flops=0, after=(), scratch=(), blocks=None):
    in_specs = [pl.BlockSpec(block, index) for _, block, index in inputs]
    in_specs += [ANYWHERE] * len(after)
    out_specs = [pl.BlockSpec(block, index) for _, _, block, index in outputs]
    count = len(inputs)
    skip = len(after)
    lead = 0 if blocks is None else 1

    def body(*refs):
        kernel(*refs[: lead + count], *refs[lead + count + skip :])

    settings = dict(
        out_shape=[sds(shape, dtype) for shape, dtype, _, _ in outputs],
        compiler_params=pltpu.CompilerParams(vmem_limit_bytes=VMEM_LIMIT),
        cost_estimate=pl.CostEstimate(flops=0, bytes_accessed=0, transcendentals=0),
        name=name,
    )
    operands = [a for a, _, _ in inputs] + list(after)
    if blocks is None:
        got = pl.pallas_call(
            body, grid=grid, in_specs=in_specs, out_specs=out_specs, scratch_shapes=list(scratch), **settings
        )(*operands)
    else:
        spec = pltpu.PrefetchScalarGridSpec(
            num_scalar_prefetch=1,
            grid=grid,
            in_specs=in_specs,
            out_specs=out_specs,
            scratch_shapes=list(scratch),
        )
        got = pl.pallas_call(body, grid_spec=spec, **settings)(blocks, *operands)
    return got[0] if len(outputs) == 1 else got


def fixed(array):
    zeros = (0,) * array.ndim
    return (array, array.shape, lambda *_: zeros)


def hold_kernel(*refs):
    pass


def after(value, *earlier):
    return pl.pallas_call(
        hold_kernel,
        in_specs=[ANYWHERE] * (1 + len(earlier)),
        out_specs=ANYWHERE,
        out_shape=jax.ShapeDtypeStruct(value.shape, value.dtype),
        input_output_aliases={0: 0},
        cost_estimate=pl.CostEstimate(flops=0, bytes_accessed=0, transcendentals=0),
        name="hold",
    )(value, *earlier)


def dot(left, right):
    return jnp.dot(left, right, preferred_element_type=F32)


def dot_last(left, right):
    return lax.dot_general(left, right, (((1,), (1,)), ((), ())), preferred_element_type=F32)


def dot_first(left, right):
    return lax.dot_general(left, right, (((0,), (0,)), ((), ())), preferred_element_type=F32)


def wide(column):
    return jnp.broadcast_to(column, (column.shape[0], 128))


def upright(row):
    return jnp.broadcast_to(row, (128, row.shape[1])).T


def stack(*refs):
    return jnp.concatenate([r[...] for r in refs], axis=0)


def tile_of(size, most):
    best = size
    for tile in range(128, most + 1, 128):
        if size % tile == 0:
            best = tile
    return best


def project_kernel(x0, x1, w, lb_ref, *refs):
    pi_ref, pf_ref, pg_ref, loc_ref, cum_ref, tot_ref = refs[-6:]
    groups, rows, tile = loc_ref.shape
    steps = rows // CHUNKS
    y = dot(stack(x0, x1), jnp.concatenate([w[0], w[1], w[2]], axis=1))
    lb = lb_ref[...]
    for g in range(groups):
        part = y[g * rows : (g + 1) * rows]
        pi_ref[g] = part[:, :tile]
        pf_ref[g] = part[:, tile : 2 * tile]
        pg_ref[g] = part[:, 2 * tile :]
    for g in range(groups):
        s = jnp.zeros((CHUNKS, tile), F32)
        p = jnp.ones_like(s)
        for t in range(steps):
            at = pl.ds(t, CHUNKS, stride=steps)
            pi = pi_ref[g, at, :]
            sig = sigmoid(pf_ref[g, at, :])
            f = lb + (1.0 - lb) * sig
            s = f * s + pi * sigmoid(pi) * ((1.0 - lb) * (1.0 - sig))
            p = p * f
            loc_ref[g, at, :] = s
            cum_ref[g, at, :] = p
        a = p[0:1]
        b = s[0:1]
        for c in range(1, CHUNKS):
            b = p[c : c + 1] * b + s[c : c + 1]
            a = a * p[c : c + 1]
        put_total(tot_ref, g, a, b, refs[:-6])


def put_total(tot_ref, g, a, b, prior):
    at = g
    if prior:
        at = g + prior[0].shape[1]
        if g == 0:
            tot_ref[:, : prior[0].shape[1], :] = prior[0][...]
    tot_ref[0, at : at + 1, :] = a
    tot_ref[1, at : at + 1, :] = b


def total_blocks(prior, chans, tile):
    count = 2 + sum(p.shape[1] for p in prior)
    inputs = [(p, (2, p.shape[1], tile), lambda c: (0, 0, c)) for p in prior]
    return inputs, ((2, count, chans), F32, (2, count, tile), lambda c: (0, 0, c))


def project(x0, x1, in_proj, lower, prior=(), after=()):
    rows, width = x0.shape
    chans = in_proj.shape[2]
    tile = tile_of(chans, 128)
    full = ((2, rows, chans), F32, (2, rows, tile), lambda c: (0, 0, c))
    before, total = total_blocks(prior, chans, tile)
    return call(
        project_kernel,
        "project",
        (chans // tile,),
        [
            fixed(x0),
            fixed(x1),
            (in_proj, (3, width, tile), lambda c: (0, 0, c)),
            (lower, (1, tile), lambda c: (0, c)),
            *before,
        ],
        [full] * 5 + [total],
        flops=12 * rows * width * chans,
        after=after,
    )


def mix_kernel(loc_ref, cum_ref, pg_ref, carry_ref, gain_ref, w_ref, state_ref, b0, b1, q0, q1, mix_ref, sq_ref):
    rows = loc_ref.shape[1]
    steps = rows // CHUNKS
    gain = gain_ref[...]
    cin = carry_ref[0]
    for c in range(CHUNKS):
        at = pl.ds(c * steps, steps)
        st = loc_ref[0, at, :] + cum_ref[0, at, :] * cin
        cin = st[steps - 1 : steps]
        pg = pg_ref[0, at, :]
        state_ref[0, at, :] = st
        mix_ref[at, :] = (st * gain * (pg * sigmoid(pg))).astype(BF)
        sq_ref[at, :] = wide(jnp.sum(st * st, axis=-1, keepdims=True))
    out = dot(mix_ref[...], w_ref[...]).astype(BF)
    first = pl.program_id(0) == 0

    @pl.when(first)
    def _():
        b0[...] = out
        q0[...] = sq_ref[...]

    @pl.when(jnp.logical_not(first))
    def _():
        b1[...] = out
        q1[...] = sq_ref[...]


def mix(loc, cum, pg, carry, shift, gain, out_proj, after=()):
    _, rows, chans = loc.shape
    width = out_proj.shape[1]
    piece = ((1, rows, chans), lambda g: (g, 0, 0))
    whole = ((rows, width), BF, (rows, width), lambda g: (0, 0))
    return call(
        mix_kernel,
        "mix",
        (2,),
        [
            (loc, *piece),
            (cum, *piece),
            (pg, *piece),
            (carry, (1, 1, chans), lambda g: (g + shift, 0, 0)),
            fixed(gain),
            fixed(out_proj),
        ],
        [
            (loc.shape, F32, *piece),
            whole,
            whole,
            ((rows, 128), F32, (rows, 128), lambda g: (0, 0)),
            ((rows, 128), F32, (rows, 128), lambda g: (0, 0)),
        ],
        flops=4 * rows * chans * width,
        after=after,
        scratch=[pltpu.VMEM((rows, chans), BF), pltpu.VMEM((rows, 128), F32)],
    )


def hidden_grad_kernel(g0, g1, w, out):
    out[...] = dot_last(stack(g0, g1), w[...])


def hidden_grad(g0, g1, down, after=()):
    rows, width = g0.shape
    units = down.shape[0]
    tile = min(256, units)
    return call(
        hidden_grad_kernel,
        "hidden_grad",
        (pl.cdiv(units, tile),),
        [fixed(g0), fixed(g1), (down, (tile, width), lambda n: (n, 0))],
        [((2 * rows, units), F32, (2 * rows, tile), lambda n: (0, n))],
        flops=4 * rows * width * units,
        after=after,
    )


def feed_kernel(x0, x1, w, gh_ref, hidden, gg, gu):
    x = stack(x0, x1)
    gate = dot(x, w[0])
    up = dot(x, w[1])
    gh = gh_ref[...]
    sig = sigmoid(gate)
    act = gate * sig
    hidden[...] = (act * up).astype(BF)
    gg[...] = (gh * up * (sig * (1.0 + gate * (1.0 - sig)))).astype(BF)
    gu[...] = (gh * act).astype(BF)


def feed(x0, x1, gate_up, gh, after=()):
    rows, width = x0.shape
    units = gate_up.shape[2]
    tile = min(256, units)
    col = ((2 * rows, tile), lambda n: (0, n))
    return call(
        feed_kernel,
        "feed",
        (pl.cdiv(units, tile),),
        [
            fixed(x0),
            fixed(x1),
            (gate_up, (2, width, tile), lambda n: (0, 0, n)),
            (gh, *col),
        ],
        [((2 * rows, units), BF, *col)] * 3,
        flops=8 * rows * width * units,
        after=after,
    )


def feed_back_kernel(gg, gu, w, b0, b1):
    rows = b0.shape[0]
    out = (dot_last(gg[...], w[0]) + dot_last(gu[...], w[1])).astype(BF)
    b0[...] = out[:rows]
    b1[...] = out[rows:]


def feed_back(gg, gu, gate_up, after=()):
    rows = gg.shape[0] // 2
    _, width, units = gate_up.shape
    tile = tile_of(width, 512)
    part = ((rows, width), BF, (rows, tile), lambda d: (0, d))
    return call(
        feed_back_kernel,
        "feed_back",
        (width // tile,),
        [fixed(gg), fixed(gu), (gate_up, (2, tile, units), lambda d: (0, d, 0))],
        [part, part],
        flops=8 * rows * width * units,
        after=after,
    )


def feed_out_kernel(h, w, b0, b1):
    rows = b0.shape[0]
    out = dot(h[...], w[...]).astype(BF)
    b0[...] = out[:rows]
    b1[...] = out[rows:]


def feed_out(hidden, down, after=()):
    rows = hidden.shape[0] // 2
    units, width = down.shape
    tile = tile_of(width, 512)
    part = ((rows, width), BF, (rows, tile), lambda d: (0, d))
    return call(
        feed_out_kernel,
        "feed_out",
        (width // tile,),
        [fixed(hidden), (down, (units, tile), lambda d: (0, d))],
        [part, part],
        flops=4 * rows * width * units,
        after=after,
    )


def back_local_kernel(
    width, g0, g1, w, pg_ref, pf_ref, state_ref, gain_ref, lb_ref, *refs
):
    mixed_ref, gpg_ref, loc_ref, cum_ref, tot_ref, term_ref = refs[-6:]
    groups, rows, tile = loc_ref.shape
    steps = rows // CHUNKS
    gain = gain_ref[...]
    lb = lb_ref[...]
    grads = dot_last(jnp.concatenate([g0[:rows], g1[:rows]], axis=0), w[...])
    term = jnp.zeros((1, tile), F32)
    for g in range(groups):
        extra = (g1 if g else g0)[rows:, :rows].astype(F32)
        scales = upright(extra[0:1] + extra[1:2])
        inners = upright(extra[2:3] + extra[3:4])
        for c in range(CHUNKS):
            at = pl.ds(c * steps, steps)
            part = slice(c * steps, (c + 1) * steps)
            scale = scales[part, :1]
            coef = scale * scale * scale * inners[part, :1] * (1.0 / width)
            pg = pg_ref[g, at, :]
            gm = grads[g * rows + c * steps : g * rows + (c + 1) * steps]
            st = state_ref[g, at, :]
            sig = sigmoid(pg)
            act = pg * sig
            unit = st * scale
            gact = gm * act
            mixed_ref[g, at, :] = (unit * gain * act).astype(BF)
            gpg_ref[g, at, :] = (gm * gain * unit * (sig * (1.0 + pg * (1.0 - sig)))).astype(BF)
            term = term + jnp.sum(gact * unit, axis=0, keepdims=True)
            loc_ref[g, at, :] = scale * (gact * gain) - st * coef
    term_ref[...] = term
    for g in range(groups):
        s = jnp.zeros((CHUNKS, tile), F32)
        q = jnp.ones_like(s)
        for t in range(steps - 1, -1, -1):
            at = pl.ds(t, CHUNKS, stride=steps)
            f = lb + (1.0 - lb) * sigmoid(pf_ref[g, at, :])
            adj = loc_ref[g, at, :] + s
            loc_ref[g, at, :] = adj
            cum_ref[g, at, :] = q
            s = f * adj
            q = q * f
        last = CHUNKS - 1
        a = q[last : last + 1]
        b = s[last : last + 1]
        for c in range(CHUNKS - 2, -1, -1):
            b = q[c : c + 1] * b + s[c : c + 1]
            a = a * q[c : c + 1]
        put_total(tot_ref, g, a, b, refs[:-6])


def back_local(g0, g1, out_proj, pg, pf, state, gain, lower, prior=(), after=()):
    rows, width = pg.shape[1], g0.shape[1]
    chans = out_proj.shape[0]
    tile = tile_of(chans, 128)
    piece = ((2, rows, tile), lambda c: (0, 0, c))
    row = ((1, tile), lambda c: (0, c))
    shape = (2, rows, chans)
    before, total = total_blocks(prior, chans, tile)
    return call(
        functools.partial(back_local_kernel, width),
        "back_local",
        (chans // tile,),
        [
            fixed(g0),
            fixed(g1),
            (out_proj, (tile, width), lambda c: (c, 0)),
            (pg, *piece),
            (pf, *piece),
            (state, *piece),
            (gain, *row),
            (lower, *row),
            *before,
        ],
        [
            (shape, BF, *piece),
            (shape, BF, *piece),
            (shape, F32, *piece),
            (shape, F32, *piece),
            total,
            ((1, chans), F32, *row),
        ],
        flops=4 * rows * width * chans,
        after=after,
    )


def back_mix_kernel(
    loc_ref, cum_ref, state_ref, pi_ref, pf_ref, gpg_ref, carry_ref, prior_ref, lb_ref, w,
    gpi_ref, gpf_ref, b0, b1, term_ref,
):
    rows = loc_ref.shape[1]
    steps = rows // CHUNKS
    lb = lb_ref[...]
    rest = 1.0 - lb
    cin = carry_ref[0]
    term = jnp.zeros((1, loc_ref.shape[2]), F32)
    top = lax.broadcasted_iota(jnp.int32, (steps, loc_ref.shape[2]), 0) == 0
    for c in range(CHUNKS - 1, -1, -1):
        at = pl.ds(c * steps, steps)
        adj = loc_ref[0, at, :] + cum_ref[0, at, :] * cin
        pi = pi_ref[0, at, :]
        sig = sigmoid(pf_ref[0, at, :])
        cin = (lb + rest * sig[0:1]) * adj[0:1]
        st = state_ref[0, at, :]
        before = prior_ref[0] if c == 0 else state_ref[0, pl.ds(c * steps - 1, 1), :]
        prev = jnp.where(top, before, pltpu.roll(st, 1, 0))
        sig_in = sigmoid(pi)
        total = adj * (prev - pi * sig_in)
        left = 1.0 - sig
        gpi_ref[0, at, :] = (adj * (rest * left) * (sig_in * (1.0 + pi * (1.0 - sig_in)))).astype(BF)
        gpf_ref[0, at, :] = (total * rest * sig * left).astype(BF)
        term = term + jnp.sum(total * left, axis=0, keepdims=True)
    term_ref[0] = term
    out = (
        dot_last(gpi_ref[0], w[0]) + dot_last(gpf_ref[0], w[1]) + dot_last(gpg_ref[0], w[2])
    ).astype(BF)
    first = pl.program_id(0) == 0

    @pl.when(first)
    def _():
        b0[...] = out

    @pl.when(jnp.logical_not(first))
    def _():
        b1[...] = out


def back_mix(loc, cum, state, pi, pf, gpg, carry, prior, shift, lower, in_proj, after=()):
    _, rows, chans = state.shape
    width = in_proj.shape[1]
    piece = ((1, rows, chans), lambda g: (g, 0, 0))
    per = ((1, 1, chans), lambda g: (g, 0, 0))
    moved = ((1, 1, chans), lambda g: (g + shift, 0, 0))
    whole = ((rows, width), BF, (rows, width), lambda g: (0, 0))
    return call(
        back_mix_kernel,
        "back_mix",
        (2,),
        [(v, *piece) for v in (loc, cum, state, pi, pf, gpg)]
        + [(carry, *moved), (prior, *moved), fixed(lower), fixed(in_proj)],
        [
            (state.shape, BF, *piece),
            (state.shape, BF, *piece),
            whole,
            whole,
            ((2, 1, chans), F32, *per),
        ],
        flops=12 * rows * width * chans,
        after=after,
    )


def product_kernel(me, x0, x1, x2, x3, near, far, out):
    out[...] = (dot_first(stack(x0, x1), near[...]) + dot_first(stack(x2, x3), far[...])).astype(BF)


def product_add_kernel(half, me, x0, x1, x2, x3, near, far, got, send, keep):
    total = dot_first(stack(x0, x1), near[...]) + dot_first(stack(x2, x3), far[...])
    total = (total + got[...].astype(F32)).astype(BF)
    early = pl.program_id(0) < half

    @pl.when(early)
    def _():
        send[...] = total

    @pl.when(jnp.logical_not(early))
    def _():
        keep[...] = total


def product(me, lefts, near, far, bits, size, got=None, after=()):
    levels = len(bits)
    count = 1 << (levels - 1)
    base = 0 if got is None else count
    top = 2 * count - 1 - base
    rows = near.shape[0] // 2
    units = near.shape[1]

    def place(j, me):
        turned = top - j
        block = me[0]
        for n, bit in enumerate(bits):
            block = block ^ (((turned >> (levels - 1 - n)) & 1) * bit)
        return (0, block)

    if size % 128:
        def ordered(x):
            parts = [
                lax.dynamic_slice_in_dim(x[:rows], place(j, me)[1] * size, size, 1)
                for j in range(count)
            ]
            return jnp.concatenate(parts, axis=1)

        lefts = [ordered(x) for x in lefts]
        count, size = count * size // 128, 128
        position = lambda j, me: (0, j)
    else:
        position = place
    inputs = [(x, (rows, size), position) for x in lefts]
    inputs += [fixed(near), fixed(far)]
    flops = 8 * rows * units * size * count
    if got is None:
        out = ((count * size, units), BF, (size, units), lambda j, me: (j, 0))
        return call(product_kernel, "product", (count,), inputs, [out], flops, after, blocks=me)
    half = count // 2
    inputs.append((got, (size, units), lambda j, me: (j, 0)))
    shape = (half * size, units)
    send = (shape, BF, (size, units), lambda j, me: (jnp.minimum(j, half - 1), 0))
    keep = (shape, BF, (size, units), lambda j, me: (jnp.maximum(j - half, 0), 0))
    return call(
        functools.partial(product_add_kernel, half),
        "product_add",
        (count,),
        inputs,
        [send, keep],
        flops,
        after,
        blocks=me,
    )


def halve_kernel(half, one, two, send, keep):
    total = (one[...].astype(F32) + two[...].astype(F32)).astype(BF)
    early = pl.program_id(0) < half

    @pl.when(early)
    def _():
        send[...] = total

    @pl.when(jnp.logical_not(early))
    def _():
        keep[...] = total


def halve(one, two, size, after=()):
    count = one.shape[0] // size
    half = count // 2
    units = one.shape[1]
    block = ((size, units), lambda j: (j, 0))
    shape = (half * size, units)
    return call(
        functools.partial(halve_kernel, half),
        "halve",
        (count,),
        [(one, *block), (two, *block)],
        [
            (shape, BF, (size, units), lambda j: (jnp.minimum(j, half - 1), 0)),
            (shape, BF, (size, units), lambda j: (jnp.maximum(j - half, 0), 0)),
        ],
        after=after,
    )


def finish_kernel(turned, *refs):
    out = refs[-1]
    for k in range(len(refs) // 2):
        total = refs[2 * k][...].astype(F32) + refs[2 * k + 1][...].astype(F32)
        if turned:
            out[...] = total.T
        else:
            out[k] = total


def finish(pairs, turned=False, after=()):
    rows, units = pairs[0][0].shape
    flat = [v for one in pairs for v in one]
    if turned:
        tile = 128 if rows % 128 == 0 else rows
        out = ((units, rows), F32, (units, tile), lambda n: (0, n))
    else:
        tile = 64 if rows % 64 == 0 else rows
        count = len(pairs)
        out = ((count, rows, units), F32, (count, tile, units), lambda n: (0, n, 0))
    return call(
        functools.partial(finish_kernel, turned),
        "finish",
        (rows // tile,),
        [(v, (tile, units), lambda n: (n, 0)) for v in flat],
        [out],
        after=after,
    )


def row_call(kernel, name, arrays, gains, outputs, sums=0, after=(), most=64, more=()):
    rows, width = arrays[0].shape[-2:]
    tile = most if rows % most == 0 else rows

    def block(shape):
        lead = len(shape) - 2
        return (*shape[:-2], tile, shape[-1]), lambda r: (*(0,) * lead, r, 0)

    inputs = [(a, *block(a.shape)) for a in arrays] + [fixed(g) for g in gains]
    results = [(shape, dtype, *block(shape)) for shape, dtype in outputs]
    results += [((1, width), F32, (1, width), lambda r: (0, 0))] * sums + list(more)
    return call(kernel, name, (rows // tile,), inputs, results, after=after)


def add_to(ref, term):
    first = pl.program_id(0) == 0

    @pl.when(first)
    def _():
        ref[...] = term

    @pl.when(jnp.logical_not(first))
    def _():
        ref[...] += term


def first_norm_kernel(x_ref, gain_ref, out):
    x = x_ref[...].astype(F32)
    out[...] = (x * rms_scale(x) * gain_ref[...]).astype(BF)


def plus_kernel(one, two, out):
    out[...] = (one[...].astype(F32) + two[...].astype(F32)).astype(BF)


def plus(one, two, after=()):
    return row_call(plus_kernel, "plus", [one, two], [], [(one.shape, BF)], after=after)


def middle_kernel(x, own, core, hop, q0, q1, q2, q3, gain, branch_ref, middle_ref, out, scale_ref):
    width = x.shape[1]
    branch = own[...].astype(F32) + core[...].astype(F32) + hop[...].astype(F32)
    scale = lax.rsqrt((q0[...] + q1[...] + q2[...] + q3[...]) / width + EPS)
    middle = x[...].astype(F32) + branch * scale[:, :1]
    branch_ref[...] = branch
    scale_ref[...] = scale
    middle_ref[...] = middle
    out[...] = (middle * rms_scale(middle) * gain[...]).astype(BF)


def turn_kernel(up, own, core, hop, middle_ref, branch, scale_ref, gain, grad_ref, term, out):
    tile = up.shape[0]
    step = pl.program_id(0)
    rows = out.shape[0] - EXTRA
    grad = own[...].astype(F32) + core[...].astype(F32) + hop[...].astype(F32)
    middle = middle_ref[...]
    scale = rms_scale(middle)
    total = up[...].astype(F32) + norm_back(grad, middle, scale, gain[...])
    low = total.astype(BF)
    grad_ref[...] = total
    out[pl.ds(pl.multiple_of(step * tile, tile), tile), :] = low
    inner = wide(jnp.sum(low.astype(F32) * branch[...], axis=-1, keepdims=True)).T[:EXTRA]
    outer = scale_ref[...].T[:EXTRA]
    high_outer = outer.astype(BF).astype(F32)
    high_inner = inner.astype(BF).astype(F32)
    which = lax.broadcasted_iota(jnp.int32, inner.shape, 0)
    both = jnp.where(which < 2, outer, inner)
    high = jnp.where(which < 2, high_outer, high_inner)
    extra = jnp.where(which % 2 == 0, high, both - high)

    @pl.when(step == 0)
    def _():
        out[rows:, :] = jnp.zeros((EXTRA, out.shape[1]), BF)

    out[rows:, pl.ds(pl.multiple_of(step * tile, tile), tile)] = extra.astype(BF)
    add_to(term, jnp.sum(grad * middle * scale, axis=0, keepdims=True))


def turn(up, own, core, hop, middle, branch, scale, gain, after=()):
    rows, width = up.shape
    shape = (rows + EXTRA, width)
    return row_call(
        turn_kernel, "turn", [up, own, core, hop, middle, branch, scale], [gain],
        [(up.shape, F32)], sums=1, after=after, most=128,
        more=[(shape, BF, shape, lambda r: (0, 0))],
    )


def last_kernel(x_ref, own, core, hop, grad_middle, gain, out, term):
    grad = own[...].astype(F32) + core[...].astype(F32) + hop[...].astype(F32)
    x = x_ref[...].astype(F32)
    scale = rms_scale(x)
    out[...] = grad_middle[...] + norm_back(grad, x, scale, gain[...])
    add_to(term, jnp.sum(grad * x * scale, axis=0, keepdims=True))


def result_kernel(middle, own, core, hop, out):
    out[...] = (
        middle[...] + (own[...].astype(F32) + core[...].astype(F32) + hop[...].astype(F32))
    ).astype(BF)


def in_order(me, total, other):
    odd = (me[0] % 2) == 1
    return (
        odd,
        jnp.where(odd, other[0], total[0]),
        jnp.where(odd, other[1], total[1]),
        jnp.where(odd, total[0], other[0]),
        jnp.where(odd, total[1], other[1]),
    )


def pair_kernel(reverse, me, total, other, pair):
    odd, low_a, low_b, high_a, high_b = in_order(me, total, other)
    pair[0] = low_a * high_a
    pair[1] = low_a * high_b + low_b if reverse else high_a * low_b + high_b


def enter_kernel(reverse, me, total, other, *refs):
    odd, low_a, low_b, high_a, high_b = in_order(me, total, other)
    enter = jnp.zeros_like(low_a)
    for got in reversed(refs[:-1]):
        enter = got[0] * enter + got[1]
    if reverse:
        enter = jnp.where(odd, enter, high_a * enter + high_b)
    else:
        enter = jnp.where(odd, low_a * enter + low_b, enter)
    for g in range(enter.shape[0]):
        refs[-1][g] = enter[g : g + 1]


def chain(me, total, reverse, between=None, beside=None):
    size = lax.axis_size("seq")
    _, groups, chans = total.shape
    other = swap(total, "seq", 1)
    got = between() if between else ()
    whole = (total.shape, F32, total.shape, lambda i, me: (0, 0, 0))
    pair = call(
        functools.partial(pair_kernel, reverse), "pair", (1,), [fixed(total), fixed(other)], [whole],
        after=got, blocks=me,
    )
    sign = -1 if reverse else 1
    reached = [shift(pair, "seq", 2 * sign * d) for d in range(1, size // 2)]
    shape = (groups, 1, chans)
    got = beside(pair) if beside else ()
    return call(
        functools.partial(enter_kernel, reverse), "enter", (1,),
        [fixed(total), fixed(other), *[fixed(r) for r in reached]],
        [(shape, F32, shape, lambda i, me: (0, 0, 0))],
        after=got,
        blocks=me,
    )


def seq_bits():
    size = lax.axis_size("seq")
    bits = []
    bit = 1
    while bit < size:
        bits.append(bit)
        bit *= 2
    return bits


class Weight:
    def __init__(self, me, lefts, near, far, bits, size):
        self.me, self.lefts, self.near, self.far = me, lefts, near, far
        self.bits, self.size, self.level = bits, size, 0

    def begin(self, *earlier):
        self.send = product(
            self.me, self.lefts, self.near, self.far, self.bits, self.size, after=earlier
        )
        return self.send

    def go(self, *earlier):
        send = after(self.send, *earlier) if earlier else self.send
        self.got = swap(send, "seq", self.bits[self.level])
        self.level += 1

    def step(self, *earlier):
        if self.level == 1:
            self.send, self.keep = product(
                self.me, self.lefts, self.near, self.far, self.bits, self.size, self.got, after=earlier
            )
        else:
            self.send, self.keep = halve(self.keep, self.got, self.size, after=earlier)
        return self.send

    def last(self):
        return self.level == len(self.bits)


def on_device(
    tokens,
    in_proj,
    out_proj,
    gate_up,
    down,
    norm1_gain,
    mixer_gain,
    norm2_gain,
    lower_bound,
    cotangent,
):
    width = in_proj.shape[1]
    chans = in_proj.shape[2]
    x = tokens[0]
    g0 = cotangent[0]
    rows = x.shape[0]
    bits = seq_bits()
    y_first = bits
    z_first = bits[1:] + bits[:1]
    block = width // lax.axis_size("seq")
    me = lax.axis_index("seq").reshape(1).astype(jnp.int32)

    offset = lax.axis_index("wt") * chans
    lower_use = lax.dynamic_slice_in_dim(lower_bound, offset, chans)[None]
    mixer_use = lax.dynamic_slice_in_dim(mixer_gain, offset, chans)[None]
    gain_one, gain_two = norm1_gain[None], norm2_gain[None]

    n0 = row_call(first_norm_kernel, "first_norm", [x], [gain_one], [(x.shape, BF)])
    hop = swap(n0, "wt", 2)
    n1 = swap(n0, "wt", 1)
    g1 = swap(g0, "wt", 1)
    grad_hop = swap(after(g0, n0), "wt", 2)
    pi_n, pf_n, pg_n, loc_n, cum_n, tot = project(n0, n1, in_proj, lower_use)
    gh_n = hidden_grad(g0, g1, down, after=(tot,))
    n2 = after(hop, gh_n)
    n3 = swap(n2, "wt", 1)
    pi_f, pf_f, pg_f, loc_f, cum_f, tot = project(n2, n3, in_proj, lower_use, (tot,))
    g2 = after(grad_hop, tot)
    g3 = swap(g2, "wt", 1)
    enter = chain(me, tot, False, lambda: (g2,))
    state_f, bf0, bf1, qf0, qf1 = mix(loc_f, cum_f, pg_f, enter, 2, mixer_use, out_proj)
    q2, q3 = swap(qf0, "wt", 2), swap(qf1, "wt", 3)
    state_n, bn0, bn1, q0, qn1 = mix(
        loc_n, cum_n, pg_n, enter, 0, mixer_use, out_proj, after=(bf0,)
    )
    across = plus(bf0, swap(bf1, "wt", 1), after=(bn0,))
    hop = swap(across, "wt", 2)
    q1 = swap(qn1, "wt", 1)
    core = swap(bn1, "wt", 1)
    gh_f = hidden_grad(g2, g3, down, after=(across,))
    branch, middle, t0, scale_two = row_call(
        middle_kernel,
        "middle",
        [x, bn0, core, hop, q0, q1, q2, q3],
        [gain_two],
        [(x.shape, F32), (x.shape, F32), (x.shape, BF), ((rows, 128), F32)],
        after=(gh_f,),
    )

    hop = swap(t0, "wt", 2)
    t1 = swap(t0, "wt", 1)
    hid_n, gg_n, gu_n = feed(t0, t1, gate_up, gh_n)
    kn0, kn1 = feed_back(gg_n, gu_n, gate_up)
    core = swap(kn1, "wt", 1)
    t2 = after(hop, kn0)
    t3 = swap(t2, "wt", 1)
    hid_f, gg_f, gu_f = feed(t2, t3, gate_up, gh_f)

    twos = (t0, t1, t2, t3)
    gate = Weight(me, twos, gg_n, gg_f, y_first, block)
    up = Weight(me, twos, gu_n, gu_f, y_first, block)
    lower = Weight(me, (g0, g1, g2, g3), hid_n, hid_f, z_first, block)
    kf0, kf1 = feed_back(gg_f, gu_f, gate_up)
    gate.begin(kf0)
    gate.go()
    across = plus(kf0, swap(kf1, "wt", 1), after=(gate.send,))
    hop = swap(across, "wt", 2)
    lower.begin(across)
    lower.go()
    up.begin(lower.send, across)
    ff0, ff1 = feed_out(hid_f, down, after=(up.send,))
    grad_middle, norm2_term, b0 = turn(
        g0, kn0, core, hop, middle, branch, scale_two, gain_two, after=(ff0,)
    )

    hop = swap(b0, "wt", 2)
    b1 = swap(b0, "wt", 1)
    mixed_n, gpg_n, bloc_n, bcum_n, btot, mixer_n = back_local(
        b0, b1, out_proj, pg_n, pf_n, state_n, mixer_use, lower_use
    )
    ffn_across = plus(ff0, swap(ff1, "wt", 1), after=(btot,))
    fn0, fn1 = feed_out(hid_n, down, after=(ffn_across,))
    ffn_core = swap(fn1, "wt", 1)
    b2 = after(hop, fn0)
    b3 = swap(b2, "wt", 1)
    gate.step(b2)
    ffn_hop = swap(after(ffn_across, b2), "wt", 2)
    mixed_f, gpg_f, bloc_f, bcum_f, btot, mixer_f = back_local(
        b2, b3, out_proj, pg_f, pf_f, state_f, mixer_use, lower_use, (btot,), after=(gate.send,)
    )
    leave = chain(me, btot, True, None, lambda pair: (lower.step(pair),))
    gate.go(leave)
    up.go(leave)
    lower.go(leave)
    gpi_f, gpf_f, df0, df1, bound_f = back_mix(
        bloc_f, bcum_f, state_f, pi_f, pf_f, gpg_f, leave, enter, 2, lower_use, in_proj
    )
    across = plus(df0, swap(df1, "wt", 1))
    hop = swap(across, "wt", 2)
    gpi_n, gpf_n, dn0, dn1, bound_n = back_mix(
        bloc_n, bcum_n, state_n, pi_n, pf_n, gpg_n, leave, enter, 0, lower_use, in_proj, after=(across,)
    )
    core = swap(dn1, "wt", 1)

    def flat(values):
        return values.reshape(2 * rows, chans)

    normals = (n0, n1, n2, n3)
    ins = [
        Weight(me, normals, flat(near), flat(far), y_first, block)
        for near, far in ((gpi_n, gpi_f), (gpf_n, gpf_f), (gpg_n, gpg_f))
    ]
    out = Weight(me, (b0, b1, b2, b3), flat(mixed_n), flat(mixed_f), y_first, block)
    token = gate.step(dn0)
    gate.go()
    for one in (out, ins[0]):
        token = one.begin(token)
        one.go()
    token = up.step(token)
    up.go()
    for one in ins[1:]:
        token = one.begin(token)
        one.go()
    token = out.step(token)
    out.go()
    result = row_call(
        result_kernel, "result", [middle, fn0, ffn_core, ffn_hop], [], [(x.shape, BF)], after=(token,)
    )
    grad_inputs, norm1_term = row_call(
        last_kernel,
        "last",
        [x, dn0, core, hop, grad_middle],
        [gain_one],
        [(x.shape, F32)],
        sums=1,
        after=(result,),
    )

    wt = lax.axis_index("wt")
    span = width // lax.axis_size("wt")
    norm_terms = jnp.concatenate([norm1_term, norm2_term])

    def part(j):
        return lax.dynamic_slice_in_dim(norm_terms, (wt ^ j) * span, span, 1)

    norms = part(0)
    for j in (1, 2, 3):
        norms = norms + swap(part(j), "wt", j)
    mixer_term = (mixer_n + mixer_f)[0]
    bound_term = jnp.sum(bound_n, axis=(0, 1)) + jnp.sum(bound_f, axis=(0, 1))
    gains = jnp.stack([norms[0], mixer_term, norms[1], bound_term])

    token = grad_inputs
    order = [lower, ins[0], up, out, *ins[1:]]
    while not all(one.last() for one in (gate, *order)):
        for one in (gate, *order):
            if not one.last():
                token = one.step(token)
                one.go()
    gate_up_grad = finish([(gate.keep, gate.got), (up.keep, up.got)])
    down_grad = finish([(lower.keep, lower.got)], True)
    out_grad = finish([(out.keep, out.got)], True)
    gains = after(gains, gate_up_grad)
    for bit in bits:
        gains = gains + swap(gains, "seq", bit)
    in_grad = finish([(one.keep, one.got) for one in ins])

    return (
        result[None],
        grad_inputs[None],
        in_grad,
        out_grad,
        gate_up_grad,
        down_grad,
        gains[0],
        gains[1],
        gains[2],
        gains[3],
    )


def solution(mesh):
    placed = (
        P("wt", "seq", None),
        P(None, None, "wt"),
        P("wt", None),
        P(None, None, "wt"),
        P("wt", None),
        P(),
        P(),
        P(),
        P(),
        P("wt", "seq", None),
    )
    return jax.shard_map(
        on_device,
        mesh=mesh,
        in_specs=placed,
        out_specs=(
            P("wt", "seq", None),
            P("wt", "seq", None),
            P(None, "seq", "wt"),
            P("wt", "seq"),
            P(None, "seq", "wt"),
            P("wt", "seq"),
            P("wt"),
            P("wt"),
            P("wt"),
            P("wt"),
        ),
        check_vma=False,
    )
```

```python
import functools

import jax
import jax.numpy as jnp
from jax import lax
from jax.experimental import pallas as pl
from jax.experimental.pallas import tpu as pltpu
from jax.sharding import PartitionSpec as P

EPS = 1e-06
BF = jnp.bfloat16
F32 = jnp.float32
CHUNKS = 8


def swap(values, axis, bit):
    size = lax.axis_size(axis)
    return lax.ppermute(values, axis, [(i, i ^ bit) for i in range(size)])


def shift(values, axis, step):
    size = lax.axis_size(axis)
    pairs = [(i, i + step) for i in range(size) if 0 <= i + step < size]
    return lax.ppermute(values, axis, pairs)


def rms_scale(values):
    return lax.rsqrt(jnp.mean(values * values, axis=-1, keepdims=True) + EPS)


def norm_back(grad_normed, values, scale, weight):
    weighted = grad_normed * weight
    return scale * weighted - values * (scale * scale * scale) * jnp.mean(
        weighted * values, axis=-1, keepdims=True
    )


def sigmoid(v):
    return 0.5 * jnp.tanh(0.5 * v) + 0.5


ANYWHERE = pl.BlockSpec(memory_space=pl.ANY)
EXTRA = 16
VMEM_LIMIT = 60 * 1024 * 1024


def sds(shape, dtype=F32):
    return jax.ShapeDtypeStruct(shape, dtype)


def call(kernel, name, grid, inputs, outputs, flops=0, after=(), scratch=(), blocks=None):
    in_specs = [pl.BlockSpec(block, index) for _, block, index in inputs]
    in_specs += [ANYWHERE] * len(after)
    out_specs = [pl.BlockSpec(block, index) for _, _, block, index in outputs]
    count = len(inputs)
    skip = len(after)
    lead = 0 if blocks is None else 1

    def body(*refs):
        kernel(*refs[: lead + count], *refs[lead + count + skip :])

    settings = dict(
        out_shape=[sds(shape, dtype) for shape, dtype, _, _ in outputs],
        compiler_params=pltpu.CompilerParams(vmem_limit_bytes=VMEM_LIMIT),
        cost_estimate=pl.CostEstimate(flops=0, bytes_accessed=0, transcendentals=0),
        name=name,
    )
    operands = [a for a, _, _ in inputs] + list(after)
    if blocks is None:
        got = pl.pallas_call(
            body, grid=grid, in_specs=in_specs, out_specs=out_specs, scratch_shapes=list(scratch), **settings
        )(*operands)
    else:
        spec = pltpu.PrefetchScalarGridSpec(
            num_scalar_prefetch=1,
            grid=grid,
            in_specs=in_specs,
            out_specs=out_specs,
            scratch_shapes=list(scratch),
        )
        got = pl.pallas_call(body, grid_spec=spec, **settings)(blocks, *operands)
    return got[0] if len(outputs) == 1 else got


def fixed(array):
    zeros = (0,) * array.ndim
    return (array, array.shape, lambda *_: zeros)


def hold_kernel(*refs):
    pass


def after(value, *earlier):
    return pl.pallas_call(
        hold_kernel,
        in_specs=[ANYWHERE] * (1 + len(earlier)),
        out_specs=ANYWHERE,
        out_shape=jax.ShapeDtypeStruct(value.shape, value.dtype),
        input_output_aliases={0: 0},
        cost_estimate=pl.CostEstimate(flops=0, bytes_accessed=0, transcendentals=0),
        name="hold",
    )(value, *earlier)


def dot(left, right):
    return jnp.dot(left, right, preferred_element_type=F32)


def dot_last(left, right):
    return lax.dot_general(left, right, (((1,), (1,)), ((), ())), preferred_element_type=F32)


def dot_first(left, right):
    return lax.dot_general(left, right, (((0,), (0,)), ((), ())), preferred_element_type=F32)


def wide(column):
    return jnp.broadcast_to(column, (column.shape[0], 128))


def in_two(values):
    which = lax.broadcasted_iota(jnp.int32, values.shape, 0)
    high = values.astype(BF).astype(F32)
    return jnp.where(which == 0, high, jnp.where(which == 1, values - high, 0.0)).astype(BF)


def upright(row):
    return jnp.broadcast_to(row, (128, row.shape[1])).T


def stack(*refs):
    return jnp.concatenate([r[...] for r in refs], axis=0)


def tile_of(size, most):
    best = size
    for tile in range(128, most + 1, 128):
        if size % tile == 0:
            best = tile
    return best


def project_kernel(x0, x1, w, lb_ref, *refs):
    pi_ref, pf_ref, pg_ref, loc_ref, cum_ref, tot_ref = refs[-6:]
    groups, rows, tile = loc_ref.shape
    steps = rows // CHUNKS
    y = dot(stack(x0, x1), jnp.concatenate([w[0], w[1], w[2]], axis=1))
    lb = lb_ref[...]
    for g in range(groups):
        part = y[g * rows : (g + 1) * rows]
        pi_ref[g] = part[:, :tile]
        pf_ref[g] = part[:, tile : 2 * tile]
        pg_ref[g] = part[:, 2 * tile :]
    for g in range(groups):
        s = jnp.zeros((CHUNKS, tile), F32)
        p = jnp.ones_like(s)
        for t in range(steps):
            at = pl.ds(t, CHUNKS, stride=steps)
            pi = pi_ref[g, at, :]
            sig = sigmoid(pf_ref[g, at, :])
            f = lb + (1.0 - lb) * sig
            s = f * s + pi * sigmoid(pi) * ((1.0 - lb) * (1.0 - sig))
            p = p * f
            loc_ref[g, at, :] = s
            cum_ref[g, at, :] = p
        a = p[0:1]
        b = s[0:1]
        for c in range(1, CHUNKS):
            b = p[c : c + 1] * b + s[c : c + 1]
            a = a * p[c : c + 1]
        put_total(tot_ref, g, a, b, refs[:-6])


def put_total(tot_ref, g, a, b, prior):
    at = g
    if prior:
        at = g + prior[0].shape[1]
        if g == 0:
            tot_ref[:, : prior[0].shape[1], :] = prior[0][...]
    tot_ref[0, at : at + 1, :] = a
    tot_ref[1, at : at + 1, :] = b


def total_blocks(prior, chans, tile):
    count = 2 + sum(p.shape[1] for p in prior)
    inputs = [(p, (2, p.shape[1], tile), lambda c: (0, 0, c)) for p in prior]
    return inputs, ((2, count, chans), F32, (2, count, tile), lambda c: (0, 0, c))


def project(x0, x1, in_proj, lower, prior=(), after=()):
    rows, width = x0.shape
    chans = in_proj.shape[2]
    tile = tile_of(chans, 128)
    full = ((2, rows, chans), F32, (2, rows, tile), lambda c: (0, 0, c))
    before, total = total_blocks(prior, chans, tile)
    return call(
        project_kernel,
        "project",
        (chans // tile,),
        [
            fixed(x0),
            fixed(x1),
            (in_proj, (3, width, tile), lambda c: (0, 0, c)),
            (lower, (1, tile), lambda c: (0, c)),
            *before,
        ],
        [full] * 5 + [total],
        flops=12 * rows * width * chans,
        after=after,
    )


def mix_kernel(loc_ref, cum_ref, pg_ref, carry_ref, gain_ref, w_ref, state_ref, b0, b1, mix_ref, sq_ref):
    rows = loc_ref.shape[1]
    steps = rows // CHUNKS
    gain = gain_ref[...]
    cin = carry_ref[0]
    for c in range(CHUNKS):
        at = pl.ds(c * steps, steps)
        st = loc_ref[0, at, :] + cum_ref[0, at, :] * cin
        cin = st[steps - 1 : steps]
        pg = pg_ref[0, at, :]
        state_ref[0, at, :] = st
        mix_ref[at, :] = (st * gain * (pg * sigmoid(pg))).astype(BF)
        sq_ref[at, :] = wide(jnp.sum(st * st, axis=-1, keepdims=True))
    out = dot(mix_ref[...], w_ref[...]).astype(BF)
    first = pl.program_id(0) == 0

    def put(ref):
        ref[:rows] = out
        ref[rows:] = jnp.zeros((EXTRA, out.shape[1]), BF)
        ref[rows:, :rows] = in_two(sq_ref[...].T[:EXTRA])

    @pl.when(first)
    def _():
        put(b0)

    @pl.when(jnp.logical_not(first))
    def _():
        put(b1)


def mix(loc, cum, pg, carry, shift, gain, out_proj, after=()):
    _, rows, chans = loc.shape
    width = out_proj.shape[1]
    piece = ((1, rows, chans), lambda g: (g, 0, 0))
    shape = (rows + EXTRA, width)
    whole = (shape, BF, shape, lambda g: (0, 0))
    return call(
        mix_kernel,
        "mix",
        (2,),
        [
            (loc, *piece),
            (cum, *piece),
            (pg, *piece),
            (carry, (1, 1, chans), lambda g: (g + shift, 0, 0)),
            fixed(gain),
            fixed(out_proj),
        ],
        [
            (loc.shape, F32, *piece),
            whole,
            whole,
        ],
        flops=4 * rows * chans * width,
        after=after,
        scratch=[pltpu.VMEM((rows, chans), BF), pltpu.VMEM((rows, 128), F32)],
    )


def hidden_grad_kernel(g0, g1, w, out):
    out[...] = dot_last(stack(g0, g1), w[...])


def hidden_grad(g0, g1, down, after=()):
    rows, width = g0.shape
    units = down.shape[0]
    tile = min(512, units)
    return call(
        hidden_grad_kernel,
        "hidden_grad",
        (pl.cdiv(units, tile),),
        [fixed(g0), fixed(g1), (down, (tile, width), lambda n: (n, 0))],
        [((2 * rows, units), F32, (2 * rows, tile), lambda n: (0, n))],
        flops=4 * rows * width * units,
        after=after,
    )


def feed_kernel(*refs):
    w, gh_ref, hidden, gg, gu = refs[-5:]
    x = stack(*refs[:-5])
    gate = dot(x, w[0])
    up = dot(x, w[1])
    gh = gh_ref[...]
    sig = sigmoid(gate)
    act = gate * sig
    hidden[...] = (act * up).astype(BF)
    gg[...] = (gh * up * (sig * (1.0 + gate * (1.0 - sig)))).astype(BF)
    gu[...] = (gh * act).astype(BF)


def feed(pieces, gate_up, gh, after=()):
    rows, width = gh.shape[0] // 2, gate_up.shape[1]
    units = gate_up.shape[2]
    tile = min(512, units)
    col = ((2 * rows, tile), lambda n: (0, n))
    return call(
        feed_kernel,
        "feed",
        (pl.cdiv(units, tile),),
        [
            *[fixed(x) for x in pieces],
            (gate_up, (2, width, tile), lambda n: (0, 0, n)),
            (gh, *col),
        ],
        [((2 * rows, units), BF, *col)] * 3,
        flops=8 * rows * width * units,
        after=after,
    )


def feed_back_kernel(gg, gu, w, b0, b1):
    rows = b0.shape[0]
    out = (dot_last(gg[...], w[0]) + dot_last(gu[...], w[1])).astype(BF)
    b0[...] = out[:rows]
    b1[...] = out[rows:]


def feed_back(gg, gu, gate_up, after=()):
    rows = gg.shape[0] // 2
    _, width, units = gate_up.shape
    tile = tile_of(width, 512)
    part = ((rows, width), BF, (rows, tile), lambda d: (0, d))
    return call(
        feed_back_kernel,
        "feed_back",
        (width // tile,),
        [fixed(gg), fixed(gu), (gate_up, (2, tile, units), lambda d: (0, d, 0))],
        [part, part],
        flops=8 * rows * width * units,
        after=after,
    )


def feed_out_kernel(h, w, b0, b1):
    rows = b0.shape[0]
    out = dot(h[...], w[...]).astype(BF)
    b0[...] = out[:rows]
    b1[...] = out[rows:]


def feed_out(hidden, down, after=()):
    rows = hidden.shape[0] // 2
    units, width = down.shape
    tile = tile_of(width, 512)
    part = ((rows, width), BF, (rows, tile), lambda d: (0, d))
    return call(
        feed_out_kernel,
        "feed_out",
        (width // tile,),
        [fixed(hidden), (down, (units, tile), lambda d: (0, d))],
        [part, part],
        flops=4 * rows * width * units,
        after=after,
    )


def back_local_kernel(
    width, g0, g1, w, pg_ref, pf_ref, state_ref, gain_ref, lb_ref, *refs
):
    mixed_ref, gpg_ref, loc_ref, cum_ref, tot_ref, term_ref = refs[-6:]
    groups, rows, tile = loc_ref.shape
    steps = rows // CHUNKS
    gain = gain_ref[...]
    lb = lb_ref[...]
    grads = dot_last(jnp.concatenate([g0[:rows], g1[:rows]], axis=0), w[...])
    term = jnp.zeros((1, tile), F32)
    for g in range(groups):
        extra = (g1 if g else g0)[rows:, :rows].astype(F32)
        scales = upright(extra[0:1] + extra[1:2])
        inners = upright(extra[2:3] + extra[3:4])
        for c in range(CHUNKS):
            at = pl.ds(c * steps, steps)
            part = slice(c * steps, (c + 1) * steps)
            scale = scales[part, :1]
            coef = scale * scale * scale * inners[part, :1] * (1.0 / width)
            pg = pg_ref[g, at, :]
            gm = grads[g * rows + c * steps : g * rows + (c + 1) * steps]
            st = state_ref[g, at, :]
            sig = sigmoid(pg)
            act = pg * sig
            unit = st * scale
            gact = gm * act
            mixed_ref[g, at, :] = (unit * gain * act).astype(BF)
            gpg_ref[g, at, :] = (gm * gain * unit * (sig * (1.0 + pg * (1.0 - sig)))).astype(BF)
            term = term + jnp.sum(gact * unit, axis=0, keepdims=True)
            loc_ref[g, at, :] = scale * (gact * gain) - st * coef
    term_ref[...] = term
    for g in range(groups):
        s = jnp.zeros((CHUNKS, tile), F32)
        q = jnp.ones_like(s)
        for t in range(steps - 1, -1, -1):
            at = pl.ds(t, CHUNKS, stride=steps)
            f = lb + (1.0 - lb) * sigmoid(pf_ref[g, at, :])
            adj = loc_ref[g, at, :] + s
            loc_ref[g, at, :] = adj
            cum_ref[g, at, :] = q
            s = f * adj
            q = q * f
        last = CHUNKS - 1
        a = q[last : last + 1]
        b = s[last : last + 1]
        for c in range(CHUNKS - 2, -1, -1):
            b = q[c : c + 1] * b + s[c : c + 1]
            a = a * q[c : c + 1]
        put_total(tot_ref, g, a, b, refs[:-6])


def back_local(g0, g1, out_proj, pg, pf, state, gain, lower, prior=(), after=()):
    rows, width = pg.shape[1], g0.shape[1]
    chans = out_proj.shape[0]
    tile = tile_of(chans, 128)
    piece = ((2, rows, tile), lambda c: (0, 0, c))
    row = ((1, tile), lambda c: (0, c))
    shape = (2, rows, chans)
    before, total = total_blocks(prior, chans, tile)
    return call(
        functools.partial(back_local_kernel, width),
        "back_local",
        (chans // tile,),
        [
            fixed(g0),
            fixed(g1),
            (out_proj, (tile, width), lambda c: (c, 0)),
            (pg, *piece),
            (pf, *piece),
            (state, *piece),
            (gain, *row),
            (lower, *row),
            *before,
        ],
        [
            (shape, BF, *piece),
            (shape, BF, *piece),
            (shape, F32, *piece),
            (shape, F32, *piece),
            total,
            ((1, chans), F32, *row),
        ],
        flops=4 * rows * width * chans,
        after=after,
    )


def back_mix_kernel(
    loc_ref, cum_ref, state_ref, pi_ref, pf_ref, gpg_ref, carry_ref, prior_ref, lb_ref, w,
    both_ref, b0, b1, term_ref,
):
    _, rows, chans = loc_ref.shape
    steps = rows // CHUNKS
    lb = lb_ref[...]
    rest = 1.0 - lb
    cin = carry_ref[0]
    term = jnp.zeros((1, loc_ref.shape[2]), F32)
    top = lax.broadcasted_iota(jnp.int32, (steps, loc_ref.shape[2]), 0) == 0
    for c in range(CHUNKS - 1, -1, -1):
        at = pl.ds(c * steps, steps)
        adj = loc_ref[0, at, :] + cum_ref[0, at, :] * cin
        pi = pi_ref[0, at, :]
        sig = sigmoid(pf_ref[0, at, :])
        cin = (lb + rest * sig[0:1]) * adj[0:1]
        st = state_ref[0, at, :]
        before = prior_ref[0] if c == 0 else state_ref[0, pl.ds(c * steps - 1, 1), :]
        prev = jnp.where(top, before, pltpu.roll(st, 1, 0))
        sig_in = sigmoid(pi)
        total = adj * (prev - pi * sig_in)
        left = 1.0 - sig
        slope = sig_in * (1.0 + pi * (1.0 - sig_in))
        both_ref[0, at, :chans] = (adj * (rest * left) * slope).astype(BF)
        both_ref[0, at, chans:] = (total * rest * sig * left).astype(BF)
        term = term + jnp.sum(total * left, axis=0, keepdims=True)
    term_ref[0] = term
    out = (
        dot_last(both_ref[0, :, :chans], w[0])
        + dot_last(both_ref[0, :, chans:], w[1])
        + dot_last(gpg_ref[0], w[2])
    ).astype(BF)
    first = pl.program_id(0) == 0

    @pl.when(first)
    def _():
        b0[...] = out

    @pl.when(jnp.logical_not(first))
    def _():
        b1[...] = out


def back_mix(loc, cum, state, pi, pf, gpg, carry, prior, shift, lower, in_proj, after=()):
    _, rows, chans = state.shape
    width = in_proj.shape[1]
    piece = ((1, rows, chans), lambda g: (g, 0, 0))
    per = ((1, 1, chans), lambda g: (g, 0, 0))
    moved = ((1, 1, chans), lambda g: (g + shift, 0, 0))
    whole = ((rows, width), BF, (rows, width), lambda g: (0, 0))
    return call(
        back_mix_kernel,
        "back_mix",
        (2,),
        [(v, *piece) for v in (loc, cum, state, pi, pf, gpg)]
        + [(carry, *moved), (prior, *moved), fixed(lower), fixed(in_proj)],
        [
            ((2, rows, 2 * chans), BF, (1, rows, 2 * chans), lambda g: (g, 0, 0)),
            whole,
            whole,
            ((2, 1, chans), F32, *per),
        ],
        flops=12 * rows * width * chans,
        after=after,
    )


def total_product(near_count, refs):
    lefts, (near, far) = refs[:-2], refs[-2:]
    return dot_first(stack(*lefts[:near_count]), near[...]) + dot_first(
        stack(*lefts[near_count:]), far[...]
    )


def product_kernel(near_count, me, *refs):
    refs[-1][...] = total_product(near_count, refs[:-1]).astype(BF)


def product_add_kernel(near_count, half, me, *refs):
    got, send, keep = refs[-3:]
    total = (total_product(near_count, refs[:-3]) + got[...].astype(F32)).astype(BF)
    early = pl.program_id(0) < half

    @pl.when(early)
    def _():
        send[...] = total

    @pl.when(jnp.logical_not(early))
    def _():
        keep[...] = total


def product(me, lefts, near, far, bits, size, got=None, after=()):
    levels = len(bits)
    count = 1 << (levels - 1)
    base = 0 if got is None else count
    top = 2 * count - 1 - base
    units = near.shape[1]
    near_count = len(lefts[0])
    lefts = [*lefts[0], *lefts[1]]

    def place(j, me):
        turned = top - j
        block = me[0]
        for n, bit in enumerate(bits):
            block = block ^ (((turned >> (levels - 1 - n)) & 1) * bit)
        return (0, block)

    if size % 128:
        def ordered(x, rows):
            parts = [
                lax.dynamic_slice_in_dim(x[:rows], place(j, me)[1] * size, size, 1)
                for j in range(count)
            ]
            return jnp.concatenate(parts, axis=1), rows

        lefts = [ordered(*x) for x in lefts]
        count, size = count * size // 128, 128
        position = lambda j, me: (0, j)
    else:
        position = place
    inputs = [(x, (rows, size), position) for x, rows in lefts]
    inputs += [fixed(near), fixed(far)]
    flops = 0
    if got is None:
        out = ((count * size, units), BF, (size, units), lambda j, me: (j, 0))
        return call(
            functools.partial(product_kernel, near_count),
            "product", (count,), inputs, [out], flops, after, blocks=me,
        )
    half = count // 2
    inputs.append((got, (size, units), lambda j, me: (j, 0)))
    shape = (half * size, units)
    send = (shape, BF, (size, units), lambda j, me: (jnp.minimum(j, half - 1), 0))
    keep = (shape, BF, (size, units), lambda j, me: (jnp.maximum(j - half, 0), 0))
    return call(
        functools.partial(product_add_kernel, near_count, half),
        "product_add",
        (count,),
        inputs,
        [send, keep],
        flops,
        after,
        blocks=me,
    )


def halve_kernel(half, one, two, send, keep):
    total = (one[...].astype(F32) + two[...].astype(F32)).astype(BF)
    early = pl.program_id(0) < half

    @pl.when(early)
    def _():
        send[...] = total

    @pl.when(jnp.logical_not(early))
    def _():
        keep[...] = total


def halve(one, two, size, after=()):
    count = one.shape[0] // size
    half = count // 2
    units = one.shape[1]
    block = ((size, units), lambda j: (j, 0))
    shape = (half * size, units)
    return call(
        functools.partial(halve_kernel, half),
        "halve",
        (count,),
        [(one, *block), (two, *block)],
        [
            (shape, BF, (size, units), lambda j: (jnp.minimum(j, half - 1), 0)),
            (shape, BF, (size, units), lambda j: (jnp.maximum(j - half, 0), 0)),
        ],
        after=after,
    )


def finish_kernel(turned, one, two, *refs):
    out = refs[-1]
    total = one[...].astype(F32) + two[...].astype(F32)
    if turned:
        out[...] = total.T
    else:
        parts, _, units = out.shape
        for part in range(parts):
            out[part] = total[:, part * units : (part + 1) * units]


def finish(one, two, turned=False, slot=0, parts=1, slots=1, into=None, after=()):
    rows, units = one.shape
    if turned:
        tile = 128 if rows % 128 == 0 else rows
        shape = (units, rows)
        out = pl.BlockSpec((units, tile), lambda n: (0, n))
    else:
        tile = 64 if rows % 64 == 0 else rows
        shape = (slots, rows, units // parts)
        out = pl.BlockSpec((parts, tile, units // parts), lambda n: (slot // parts, n, 0))
    block = pl.BlockSpec((tile, units), lambda n: (n, 0))
    held = [] if into is None else [into]
    waits = [*held, *after]
    count = len(waits)
    return pl.pallas_call(
        lambda one, two, *refs: finish_kernel(turned, one, two, *refs[count:]),
        grid=(rows // tile,),
        in_specs=[block, block] + [ANYWHERE] * count,
        out_specs=out,
        out_shape=sds(shape),
        input_output_aliases={2: 0} if held else {},
        compiler_params=pltpu.CompilerParams(vmem_limit_bytes=VMEM_LIMIT),
        cost_estimate=pl.CostEstimate(flops=0, bytes_accessed=0, transcendentals=0),
        name="finish",
    )(one, two, *waits)


def row_call(kernel, name, arrays, gains, outputs, sums=0, after=(), most=64, more=()):
    rows, width = arrays[0].shape[-2:]
    tile = most if rows % most == 0 else rows

    def block(shape):
        lead = len(shape) - 2
        return (*shape[:-2], tile, shape[-1]), lambda r: (*(0,) * lead, r, 0)

    inputs = [(a, *block(a.shape)) for a in arrays] + [fixed(g) for g in gains]
    results = [(shape, dtype, *block(shape)) for shape, dtype in outputs]
    results += [((1, width), F32, (1, width), lambda r: (0, 0))] * sums + list(more)
    return call(kernel, name, (rows // tile,), inputs, results, after=after)


def add_to(ref, term):
    first = pl.program_id(0) == 0

    @pl.when(first)
    def _():
        ref[...] = term

    @pl.when(jnp.logical_not(first))
    def _():
        ref[...] += term


def first_norm_kernel(x_ref, gain_ref, out):
    x = x_ref[...].astype(F32)
    out[...] = (x * rms_scale(x) * gain_ref[...]).astype(BF)


def plus_kernel(one, two, out):
    out[...] = (one[...].astype(F32) + two[...].astype(F32)).astype(BF)


def plus(one, two, after=()):
    return row_call(plus_kernel, "plus", [one, two], [], [(one.shape, BF)], after=after)


def join_kernel(one, two, top, bottom):
    half = bottom.shape[0]
    rows = 2 * half
    for out, at in ((top, 0), (bottom, half)):
        part = slice(at, at + half)
        out[:half] = (one[part].astype(F32) + two[part].astype(F32)).astype(BF)
    extra = one[rows:].astype(F32) + two[rows:].astype(F32)
    top[half:] = in_two(jnp.broadcast_to(extra[0:1] + extra[1:2], extra.shape))


def join(one, two, after=()):
    rows, width = one.shape[0] - EXTRA, one.shape[1]
    shapes = [(rows // 2 + EXTRA, width), (rows // 2, width)]
    return call(
        join_kernel, "join", (1,), [fixed(one), fixed(two)],
        [(s, BF, s, lambda i: (0, 0)) for s in shapes], after=after,
    )


def middle_kernel(half, x, own, core, hop, own_more, core_more, hop_more, gain, *refs):
    branch_ref, middle_ref, scale_ref, full, out = refs[-5:]
    rows, width = x.shape
    more = own_more[...].astype(F32) + core_more[...].astype(F32) + hop_more[...].astype(F32)
    squares = (more[0:1] + more[1:2])[:, half * rows : (half + 1) * rows]
    scale = lax.rsqrt(upright(squares) / width + EPS)
    branch = own[...].astype(F32) + core[...].astype(F32) + hop[...].astype(F32)
    middle = x[...].astype(F32) + branch * scale[:, :1]
    branch_ref[...] = branch
    scale_ref[...] = scale
    middle_ref[...] = middle
    low = (middle * rms_scale(middle) * gain[...]).astype(BF)
    full[...] = low
    out[...] = low


def middle_half(half, x, own, core, hop, top, gain, begun=(), after=()):
    total, width = x.shape
    rows = total // 2
    part = pl.BlockSpec((rows, width), lambda i: (half, 0))
    alone = pl.BlockSpec((rows, width), lambda i: (0, 0))
    more = pl.BlockSpec((EXTRA, width), lambda i: (total // EXTRA, 0))
    top_more = pl.BlockSpec((EXTRA, width), lambda i: (rows // EXTRA, 0))
    waits = [*begun, *after]
    return pl.pallas_call(
        functools.partial(middle_kernel, half),
        grid=(1,),
        in_specs=[part, part, part, alone, more, more, top_more, pl.BlockSpec((1, width), lambda i: (0, 0))]
        + [ANYWHERE] * len(waits),
        out_specs=[part, part, pl.BlockSpec((rows, 128), lambda i: (half, 0)), part, alone],
        out_shape=[
            sds((total, width)), sds((total, width)), sds((total, 128)), sds((total, width), BF),
            sds((rows, width), BF),
        ],
        input_output_aliases={8 + n: n for n in range(len(begun))},
        compiler_params=pltpu.CompilerParams(vmem_limit_bytes=VMEM_LIMIT),
        cost_estimate=pl.CostEstimate(flops=0, bytes_accessed=0, transcendentals=0),
        name="middle",
    )(x, own, core, hop, own, core, top, gain, *waits)


def turn_kernel(up, own, core, hop, middle_ref, branch, scale_ref, gain, grad_ref, term, out):
    tile = up.shape[0]
    step = pl.program_id(0)
    rows = out.shape[0] - EXTRA
    grad = own[...].astype(F32) + core[...].astype(F32) + hop[...].astype(F32)
    middle = middle_ref[...]
    scale = rms_scale(middle)
    total = up[...].astype(F32) + norm_back(grad, middle, scale, gain[...])
    low = total.astype(BF)
    grad_ref[...] = total
    out[pl.ds(pl.multiple_of(step * tile, tile), tile), :] = low
    inner = wide(jnp.sum(low.astype(F32) * branch[...], axis=-1, keepdims=True)).T[:EXTRA]
    outer = scale_ref[...].T[:EXTRA]
    high_outer = outer.astype(BF).astype(F32)
    high_inner = inner.astype(BF).astype(F32)
    which = lax.broadcasted_iota(jnp.int32, inner.shape, 0)
    both = jnp.where(which < 2, outer, inner)
    high = jnp.where(which < 2, high_outer, high_inner)
    extra = jnp.where(which % 2 == 0, high, both - high)

    @pl.when(step == 0)
    def _():
        out[rows:, :] = jnp.zeros((EXTRA, out.shape[1]), BF)

    out[rows:, pl.ds(pl.multiple_of(step * tile, tile), tile)] = extra.astype(BF)
    add_to(term, jnp.sum(grad * middle * scale, axis=0, keepdims=True))


def turn(up, own, core, hop, middle, branch, scale, gain, after=()):
    rows, width = up.shape
    shape = (rows + EXTRA, width)
    return row_call(
        turn_kernel, "turn", [up, own, core, hop, middle, branch, scale], [gain],
        [(up.shape, F32)], sums=1, after=after, most=128,
        more=[(shape, BF, shape, lambda r: (0, 0))],
    )


def last_kernel(x_ref, own, core, hop, grad_middle, gain, out, term):
    grad = own[...].astype(F32) + core[...].astype(F32) + hop[...].astype(F32)
    x = x_ref[...].astype(F32)
    scale = rms_scale(x)
    out[...] = grad_middle[...] + norm_back(grad, x, scale, gain[...])
    add_to(term, jnp.sum(grad * x * scale, axis=0, keepdims=True))


def result_kernel(middle, own, core, hop, out):
    out[...] = (
        middle[...] + (own[...].astype(F32) + core[...].astype(F32) + hop[...].astype(F32))
    ).astype(BF)


def in_order(me, total, other):
    odd = (me[0] % 2) == 1
    return (
        odd,
        jnp.where(odd, other[0], total[0]),
        jnp.where(odd, other[1], total[1]),
        jnp.where(odd, total[0], other[0]),
        jnp.where(odd, total[1], other[1]),
    )


def pair_kernel(reverse, me, total, other, pair):
    odd, low_a, low_b, high_a, high_b = in_order(me, total, other)
    pair[0] = low_a * high_a
    pair[1] = low_a * high_b + low_b if reverse else high_a * low_b + high_b


def enter_kernel(reverse, me, total, other, *refs):
    odd, low_a, low_b, high_a, high_b = in_order(me, total, other)
    enter = jnp.zeros_like(low_a)
    for got in reversed(refs[:-1]):
        enter = got[0] * enter + got[1]
    if reverse:
        enter = jnp.where(odd, enter, high_a * enter + high_b)
    else:
        enter = jnp.where(odd, low_a * enter + low_b, enter)
    for g in range(enter.shape[0]):
        refs[-1][g] = enter[g : g + 1]


def chain(me, total, reverse, between=None, beside=None):
    size = lax.axis_size("seq")
    _, groups, chans = total.shape
    other = swap(total, "seq", 1)
    got = between() if between else ()
    whole = (total.shape, F32, total.shape, lambda i, me: (0, 0, 0))
    pair = call(
        functools.partial(pair_kernel, reverse), "pair", (1,), [fixed(total), fixed(other)], [whole],
        after=got, blocks=me,
    )
    sign = -1 if reverse else 1
    reached = [shift(pair, "seq", 2 * sign * d) for d in range(1, size // 2)]
    shape = (groups, 1, chans)
    got = beside(pair) if beside else ()
    return call(
        functools.partial(enter_kernel, reverse), "enter", (1,),
        [fixed(total), fixed(other), *[fixed(r) for r in reached]],
        [(shape, F32, shape, lambda i, me: (0, 0, 0))],
        after=got,
        blocks=me,
    )


def seq_bits():
    size = lax.axis_size("seq")
    bits = []
    bit = 1
    while bit < size:
        bits.append(bit)
        bit *= 2
    return bits


class Weight:
    def __init__(self, me, lefts, near, far, bits, size):
        self.me, self.lefts, self.near, self.far = me, lefts, near, far
        self.bits, self.size, self.level = bits, size, 0

    def begin(self, *earlier):
        self.send = product(
            self.me, self.lefts, self.near, self.far, self.bits, self.size, after=earlier
        )
        return self.send

    def go(self, *earlier):
        send = after(self.send, *earlier) if earlier else self.send
        self.got = swap(send, "seq", self.bits[self.level])
        self.level += 1

    def step(self, *earlier):
        if self.level == 1:
            self.send, self.keep = product(
                self.me, self.lefts, self.near, self.far, self.bits, self.size, self.got, after=earlier
            )
        else:
            self.send, self.keep = halve(self.keep, self.got, self.size, after=earlier)
        return self.send

    def last(self):
        return self.level == len(self.bits)


def gain_terms(norm1_term, norm2_term, mixer_term, bound_n, bound_f):
    wt = lax.axis_index("wt")
    span = norm1_term.shape[1] // lax.axis_size("wt")
    norm_terms = jnp.concatenate([norm1_term, norm2_term])

    def part(j):
        return lax.dynamic_slice_in_dim(norm_terms, (wt ^ j) * span, span, 1)

    norms = part(0)
    for j in (1, 2, 3):
        norms = norms + swap(part(j), "wt", j)
    bound_term = jnp.sum(bound_n, axis=(0, 1)) + jnp.sum(bound_f, axis=(0, 1))
    return jnp.stack([norms[0], mixer_term[0], norms[1], bound_term])


GATE_AT, LOWER_AT, UP_AT, LOWER_BITS = "before", "beside", "pair", "m"
ORDER = (
    ("-p", "-n", "gs", "bb", "us", "-l", "ob", "ls", "ab", "us", "-r", "gf")
    + ("bs", "os", "as", "lf", "bs", "uf", "as", "os", "bf", "af", "-t", "of")
)


def on_device(
    tokens,
    in_proj,
    out_proj,
    gate_up,
    down,
    norm1_gain,
    mixer_gain,
    norm2_gain,
    lower_bound,
    cotangent,
):
    width = in_proj.shape[1]
    chans = in_proj.shape[2]
    x = tokens[0]
    g0 = cotangent[0]
    rows = x.shape[0]
    bits = seq_bits()
    y_first = bits
    mixed_order = {"m": bits[1:2] + bits[:1] + bits[2:], "z": bits[1:] + bits[:1], "y": bits}[LOWER_BITS]
    block = width // lax.axis_size("seq")
    me = lax.axis_index("seq").reshape(1).astype(jnp.int32)

    offset = lax.axis_index("wt") * chans
    lower_use = lax.dynamic_slice_in_dim(lower_bound, offset, chans)[None]
    mixer_use = lax.dynamic_slice_in_dim(mixer_gain, offset, chans)[None]
    gain_one, gain_two = norm1_gain[None], norm2_gain[None]

    n0 = row_call(first_norm_kernel, "first_norm", [x], [gain_one], [(x.shape, BF)])
    hop = swap(n0, "wt", 2)
    n1 = swap(n0, "wt", 1)
    g1 = swap(g0, "wt", 1)
    grad_hop = swap(after(g0, n0), "wt", 2)
    pi_n, pf_n, pg_n, loc_n, cum_n, tot = project(n0, n1, in_proj, lower_use)
    gh_n = hidden_grad(g0, g1, down, after=(tot,))
    n2 = after(hop, gh_n)
    n3 = swap(n2, "wt", 1)
    pi_f, pf_f, pg_f, loc_f, cum_f, tot = project(n2, n3, in_proj, lower_use, (tot,))
    g2 = after(grad_hop, tot)
    g3 = swap(g2, "wt", 1)
    enter = chain(me, tot, False, lambda: (g2,))
    state_f, bf0, bf1 = mix(loc_f, cum_f, pg_f, enter, 2, mixer_use, out_proj)
    state_n, bn0, bn1 = mix(loc_n, cum_n, pg_n, enter, 0, mixer_use, out_proj, after=(bf0,))
    across = join(bf0, swap(bf1, "wt", 1), after=(bn0,))
    hops = [swap(part, "wt", 2) for part in across]
    core = swap(bn1, "wt", 1)
    gh_f = hidden_grad(g2, g3, down, after=(across[1],))
    *begun, half0 = middle_half(0, x, bn0, core, hops[0], hops[0], gain_two, after=(gh_f,))
    branch, middle, scale_two, t0, half1 = middle_half(
        1, x, bn0, core, hops[1], hops[0], gain_two, begun
    )

    hops = [swap(half, "wt", 2) for half in (half0, half1)]
    t2 = [after(hops[0], t0)]
    t1 = [after(swap(half, "wt", 1), t2[0]) for half in (half0, half1)]
    hid_n, gg_n, gu_n = feed((t0, *t1), gate_up, gh_n)
    kn0, kn1 = feed_back(gg_n, gu_n, gate_up)
    core = swap(kn1, "wt", 1)
    t2.append(after(hops[1], kn0))
    t3 = [swap(half, "wt", 1) for half in t2]
    hid_f, gg_f, gu_f = feed((*t2, *t3), gate_up, gh_f)

    def pieces(*arrays):
        return [(v, min(rows, v.shape[0])) for v in arrays]

    twos = (pieces(t0, *t1), pieces(*t2, *t3))
    gate = Weight(me, twos, gg_n, gg_f, y_first, block)
    up = Weight(me, twos, gu_n, gu_f, y_first, block)
    lower = Weight(me, (pieces(g0, g1), pieces(g2, g3)), hid_n, hid_f, mixed_order, block)
    kf0, kf1 = feed_back(gg_f, gu_f, gate_up)
    gate.begin(kf0)
    gate.go()
    across = plus(kf0, swap(kf1, "wt", 1), after=(gate.send,))
    hop = swap(across, "wt", 2)
    lower.begin(across)
    lower.go()
    up.begin(lower.send, across)
    ff0, ff1 = feed_out(hid_f, down, after=(up.send,))
    grad_middle, norm2_term, b0 = turn(
        g0, kn0, core, hop, middle, branch, scale_two, gain_two, after=(ff0,)
    )

    hop = swap(b0, "wt", 2)
    b1 = swap(b0, "wt", 1)
    mixed_n, gpg_n, bloc_n, bcum_n, btot, mixer_n = back_local(
        b0, b1, out_proj, pg_n, pf_n, state_n, mixer_use, lower_use
    )
    ffn_across = plus(ff0, swap(ff1, "wt", 1), after=(btot,))
    fn0, fn1 = feed_out(hid_n, down, after=(ffn_across,))
    ffn_core = swap(fn1, "wt", 1)
    b2 = after(hop, fn0)
    b3 = swap(b2, "wt", 1)
    early = (gate.step(b2),) if GATE_AT == "before" else ()
    mixed_f, gpg_f, bloc_f, bcum_f, btot, mixer_f = back_local(
        b2, b3, out_proj, pg_f, pf_f, state_f, mixer_use, lower_use, (btot,), after=early
    )

    def beside(pair):
        if UP_AT == "pair":
            up.go(pair)
        for one, place in ((gate, GATE_AT), (lower, LOWER_AT)):
            if place == "beside":
                pair = one.step(pair)
        return (pair,)

    leave = chain(me, btot, True, None, beside)
    if UP_AT == "leave":
        up.go(leave)
    if GATE_AT == "after":
        gate.step(leave)
        gate.go()
    else:
        gate.go(leave)
    if LOWER_AT == "beside":
        if LOWER_BITS == "z":
            lower.go(leave)
        else:
            lower.go()
    both_f, df0, df1, bound_f = back_mix(
        bloc_f, bcum_f, state_f, pi_f, pf_f, gpg_f, leave, enter, 2, lower_use, in_proj
    )

    def flat(values):
        return values.reshape(2 * rows, values.shape[2])

    normals = (pieces(n0, n1), pieces(n2, n3))
    last_in = Weight(me, normals, flat(gpg_n), flat(gpg_f), y_first, block)
    out = Weight(me, (pieces(b0, b1), pieces(b2, b3)), flat(mixed_n), flat(mixed_f), y_first, block)
    both_n, dn0, dn1, bound_n = None, None, None, None
    token = df0
    weights = {"g": gate, "u": up, "l": lower, "a": last_in, "o": out}
    rounds = list(bits)
    gate_up_grad = in_grad = None
    for kind, act in ORDER:
        if kind in weights:
            one = weights[kind]
            if act == "b":
                token = one.begin(token)
                one.go()
            elif act == "s":
                token = one.step(token)
                one.go()
                while one.level > 2 and not one.last():
                    token = one.step(token)
                    one.go()
            elif kind in "gu":
                slot = "gu".index(kind)
                token = gate_up_grad = finish(
                    one.keep, one.got, slot=slot, slots=2, into=gate_up_grad, after=(token,)
                )
            elif kind == "b":
                token = in_grad = finish(
                    one.keep, one.got, parts=2, slots=3, into=in_grad, after=(token,)
                )
            elif kind == "a":
                token = in_grad = finish(
                    one.keep, one.got, slot=2, slots=3, into=in_grad, after=(token,)
                )
            elif kind == "l":
                token = down_grad = finish(one.keep, one.got, True, after=(token,))
            else:
                token = out_grad = finish(one.keep, one.got, True, after=(token,))
        elif act == "p":
            token = plus(df0, swap(df1, "wt", 1), after=(token,))
            hop = swap(token, "wt", 2)
        elif act == "n":
            both_n, dn0, dn1, bound_n = back_mix(
                bloc_n, bcum_n, state_n, pi_n, pf_n, gpg_n, leave, enter, 0, lower_use, in_proj,
                after=(token,),
            )
            token = dn0
            core = swap(dn1, "wt", 1)
            weights["b"] = Weight(me, normals, flat(both_n), flat(both_f), y_first, block)
        elif act == "l":
            grad_inputs, norm1_term = row_call(
                last_kernel,
                "last",
                [x, dn0, core, hop, grad_middle],
                [gain_one],
                [(x.shape, F32)],
                sums=1,
                after=(token,),
            )
            token = grad_inputs
            ffn_hop = swap(after(ffn_across, token), "wt", 2)
            gains = gain_terms(norm1_term, norm2_term, mixer_n + mixer_f, bound_n, bound_f)
        elif act == "r":
            token = result = row_call(
                result_kernel, "result", [middle, fn0, ffn_core, ffn_hop], [], [(x.shape, BF)],
                after=(token,),
            )
        elif act == "t":
            for bit in rounds:
                gains = gains + after(swap(gains, "seq", bit), token)

    return (
        result[None],
        grad_inputs[None],
        in_grad,
        out_grad,
        gate_up_grad,
        down_grad,
        gains[0],
        gains[1],
        gains[2],
        gains[3],
    )


def solution(mesh):
    placed = (
        P("wt", "seq", None),
        P(None, None, "wt"),
        P("wt", None),
        P(None, None, "wt"),
        P("wt", None),
        P(),
        P(),
        P(),
        P(),
        P("wt", "seq", None),
    )
    return jax.shard_map(
        on_device,
        mesh=mesh,
        in_specs=placed,
        out_specs=(
            P("wt", "seq", None),
            P("wt", "seq", None),
            P(None, "seq", "wt"),
            P("wt", "seq"),
            P(None, "seq", "wt"),
            P("wt", "seq"),
            P("wt"),
            P("wt"),
            P("wt"),
            P("wt"),
        ),
        check_vma=False,
    )
```

```python
import functools

import jax
import jax.numpy as jnp
from jax import lax
from jax.experimental import pallas as pl
from jax.experimental.pallas import tpu as pltpu
from jax.sharding import PartitionSpec as P

EPS = 1e-06
BF = jnp.bfloat16
F32 = jnp.float32
CHUNKS = 8


def swap(values, axis, bit):
    size = lax.axis_size(axis)
    return lax.ppermute(values, axis, [(i, i ^ bit) for i in range(size)])


def shift(values, axis, step):
    size = lax.axis_size(axis)
    pairs = [(i, i + step) for i in range(size) if 0 <= i + step < size]
    return lax.ppermute(values, axis, pairs)


def rms_scale(values):
    return lax.rsqrt(jnp.mean(values * values, axis=-1, keepdims=True) + EPS)


def norm_back(grad_normed, values, scale, weight):
    weighted = grad_normed * weight
    return scale * weighted - values * (scale * scale * scale) * jnp.mean(
        weighted * values, axis=-1, keepdims=True
    )


def sigmoid(v):
    return 0.5 * jnp.tanh(0.5 * v) + 0.5


ANYWHERE = pl.BlockSpec(memory_space=pl.ANY)
EXTRA = 16
VMEM_LIMIT = 63 * 1024 * 1024


def sds(shape, dtype=F32):
    return jax.ShapeDtypeStruct(shape, dtype)


def call(kernel, name, grid, inputs, outputs, flops=0, after=(), scratch=(), blocks=None):
    in_specs = [pl.BlockSpec(block, index) for _, block, index in inputs]
    in_specs += [ANYWHERE] * len(after)
    out_specs = [pl.BlockSpec(block, index) for _, _, block, index in outputs]
    count = len(inputs)
    skip = len(after)
    lead = 0 if blocks is None else 1

    def body(*refs):
        kernel(*refs[: lead + count], *refs[lead + count + skip :])

    settings = dict(
        out_shape=[sds(shape, dtype) for shape, dtype, _, _ in outputs],
        compiler_params=pltpu.CompilerParams(vmem_limit_bytes=VMEM_LIMIT),
        cost_estimate=pl.CostEstimate(flops=0, bytes_accessed=0, transcendentals=0),
        name=name,
    )
    operands = [a for a, _, _ in inputs] + list(after)
    if blocks is None:
        got = pl.pallas_call(
            body, grid=grid, in_specs=in_specs, out_specs=out_specs, scratch_shapes=list(scratch), **settings
        )(*operands)
    else:
        spec = pltpu.PrefetchScalarGridSpec(
            num_scalar_prefetch=1,
            grid=grid,
            in_specs=in_specs,
            out_specs=out_specs,
            scratch_shapes=list(scratch),
        )
        got = pl.pallas_call(body, grid_spec=spec, **settings)(blocks, *operands)
    return got[0] if len(outputs) == 1 else got


def fixed(array):
    zeros = (0,) * array.ndim
    return (array, array.shape, lambda *_: zeros)


def hold_kernel(*refs):
    pass


def after(value, *earlier):
    return pl.pallas_call(
        hold_kernel,
        in_specs=[ANYWHERE] * (1 + len(earlier)),
        out_specs=ANYWHERE,
        out_shape=jax.ShapeDtypeStruct(value.shape, value.dtype),
        input_output_aliases={0: 0},
        cost_estimate=pl.CostEstimate(flops=0, bytes_accessed=0, transcendentals=0),
        name="hold",
    )(value, *earlier)


def dot(left, right):
    return jnp.dot(left, right, preferred_element_type=F32)


def dot_last(left, right):
    return lax.dot_general(left, right, (((1,), (1,)), ((), ())), preferred_element_type=F32)


def dot_first(left, right):
    return lax.dot_general(left, right, (((0,), (0,)), ((), ())), preferred_element_type=F32)


def wide(column):
    return jnp.broadcast_to(column, (column.shape[0], 128))


def in_two(values):
    which = lax.broadcasted_iota(jnp.int32, values.shape, 0)
    high = values.astype(BF).astype(F32)
    return jnp.where(which == 0, high, jnp.where(which == 1, values - high, 0.0)).astype(BF)


def upright(row):
    return jnp.broadcast_to(row, (128, row.shape[1])).T


def stack(*refs):
    return jnp.concatenate([r[...] for r in refs], axis=0)


def tile_of(size, most):
    best = size
    for tile in range(128, most + 1, 128):
        if size % tile == 0:
            best = tile
    return best


def project_kernel(x0, x1, w, lb_ref, *refs):
    pi_ref, pf_ref, pg_ref, loc_ref, cum_ref, tot_ref = refs[-6:]
    groups, rows, tile = loc_ref.shape
    steps = rows // CHUNKS
    y = dot(stack(x0, x1), jnp.concatenate([w[0], w[1], w[2]], axis=1))
    lb = lb_ref[...]
    for g in range(groups):
        part = y[g * rows : (g + 1) * rows]
        pi_ref[g] = part[:, :tile]
        pf_ref[g] = part[:, tile : 2 * tile]
        pg_ref[g] = part[:, 2 * tile :]
    for g in range(groups):
        s = jnp.zeros((CHUNKS, tile), F32)
        p = jnp.ones_like(s)
        for t in range(steps):
            at = pl.ds(t, CHUNKS, stride=steps)
            pi = pi_ref[g, at, :]
            sig = sigmoid(pf_ref[g, at, :])
            f = lb + (1.0 - lb) * sig
            s = f * s + pi * sigmoid(pi) * ((1.0 - lb) * (1.0 - sig))
            p = p * f
            loc_ref[g, at, :] = s
            cum_ref[g, at, :] = p
        a = p[0:1]
        b = s[0:1]
        for c in range(1, CHUNKS):
            b = p[c : c + 1] * b + s[c : c + 1]
            a = a * p[c : c + 1]
        put_total(tot_ref, g, a, b, refs[:-6])


def put_total(tot_ref, g, a, b, prior):
    at = g
    if prior:
        at = g + prior[0].shape[1]
        if g == 0:
            tot_ref[:, : prior[0].shape[1], :] = prior[0][...]
    tot_ref[0, at : at + 1, :] = a
    tot_ref[1, at : at + 1, :] = b


def total_blocks(prior, chans, tile):
    count = 2 + sum(p.shape[1] for p in prior)
    inputs = [(p, (2, p.shape[1], tile), lambda c: (0, 0, c)) for p in prior]
    return inputs, ((2, count, chans), F32, (2, count, tile), lambda c: (0, 0, c))


def project(x0, x1, in_proj, lower, prior=(), after=()):
    rows, width = x0.shape
    chans = in_proj.shape[2]
    tile = tile_of(chans, 128)
    full = ((2, rows, chans), F32, (2, rows, tile), lambda c: (0, 0, c))
    before, total = total_blocks(prior, chans, tile)
    return call(
        project_kernel,
        "project",
        (chans // tile,),
        [
            fixed(x0),
            fixed(x1),
            (in_proj, (3, width, tile), lambda c: (0, 0, c)),
            (lower, (1, tile), lambda c: (0, c)),
            *before,
        ],
        [full] * 5 + [total],
        flops=12 * rows * width * chans,
        after=after,
    )


def mix_kernel(loc_ref, cum_ref, pg_ref, carry_ref, gain_ref, w_ref, state_ref, b0, b1, mix_ref, sq_ref):
    rows = loc_ref.shape[1]
    steps = rows // CHUNKS
    gain = gain_ref[...]
    cin = carry_ref[0]
    for c in range(CHUNKS):
        at = pl.ds(c * steps, steps)
        st = loc_ref[0, at, :] + cum_ref[0, at, :] * cin
        cin = st[steps - 1 : steps]
        pg = pg_ref[0, at, :]
        state_ref[0, at, :] = st
        mix_ref[at, :] = (st * gain * (pg * sigmoid(pg))).astype(BF)
        sq_ref[at, :] = wide(jnp.sum(st * st, axis=-1, keepdims=True))
    out = dot(mix_ref[...], w_ref[...]).astype(BF)
    first = pl.program_id(0) == 0

    def put(ref):
        ref[:rows] = out
        ref[rows:] = jnp.zeros((EXTRA, out.shape[1]), BF)
        ref[rows:, :rows] = in_two(sq_ref[...].T[:EXTRA])

    @pl.when(first)
    def _():
        put(b0)

    @pl.when(jnp.logical_not(first))
    def _():
        put(b1)


def mix(loc, cum, pg, carry, shift, gain, out_proj, after=()):
    _, rows, chans = loc.shape
    width = out_proj.shape[1]
    piece = ((1, rows, chans), lambda g: (g, 0, 0))
    shape = (rows + EXTRA, width)
    whole = (shape, BF, shape, lambda g: (0, 0))
    return call(
        mix_kernel,
        "mix",
        (2,),
        [
            (loc, *piece),
            (cum, *piece),
            (pg, *piece),
            (carry, (1, 1, chans), lambda g: (g + shift, 0, 0)),
            fixed(gain),
            fixed(out_proj),
        ],
        [
            (loc.shape, F32, *piece),
            whole,
            whole,
        ],
        flops=4 * rows * chans * width,
        after=after,
        scratch=[pltpu.VMEM((rows, chans), BF), pltpu.VMEM((rows, 128), F32)],
    )


def hidden_grad_kernel(g0, g1, w, out):
    out[...] = dot_last(stack(g0, g1), w[...])


def hidden_grad(g0, g1, down, after=()):
    rows, width = g0.shape
    units = down.shape[0]
    tile = min(512, units)
    return call(
        hidden_grad_kernel,
        "hidden_grad",
        (pl.cdiv(units, tile),),
        [fixed(g0), fixed(g1), (down, (tile, width), lambda n: (n, 0))],
        [((2 * rows, units), F32, (2 * rows, tile), lambda n: (0, n))],
        flops=4 * rows * width * units,
        after=after,
    )


def feed_kernel(*refs):
    w, gh_ref, hidden, gg, gu = refs[-5:]
    x = stack(*refs[:-5])
    gate = dot(x, w[0])
    up = dot(x, w[1])
    gh = gh_ref[...]
    sig = sigmoid(gate)
    act = gate * sig
    hidden[...] = (act * up).astype(BF)
    gg[...] = (gh * up * (sig * (1.0 + gate * (1.0 - sig)))).astype(BF)
    gu[...] = (gh * act).astype(BF)


def feed(pieces, gate_up, gh, after=()):
    rows, width = gh.shape[0] // 2, gate_up.shape[1]
    units = gate_up.shape[2]
    tile = min(512, units)
    col = ((2 * rows, tile), lambda n: (0, n))
    return call(
        feed_kernel,
        "feed",
        (pl.cdiv(units, tile),),
        [
            *[(x, (min(x.shape[0], rows) // 128 * 128, width), lambda n: (0, 0)) for x in pieces],
            (gate_up, (2, width, tile), lambda n: (0, 0, n)),
            (gh, *col),
        ],
        [((2 * rows, units), BF, *col)] * 3,
        flops=8 * rows * width * units,
        after=after,
    )


def feed_back_kernel(gg, gu, w, b0, b1):
    rows = b0.shape[0]
    out = (dot_last(gg[...], w[0]) + dot_last(gu[...], w[1])).astype(BF)
    b0[...] = out[:rows]
    b1[...] = out[rows:]


def feed_back(gg, gu, gate_up, after=()):
    rows = gg.shape[0] // 2
    _, width, units = gate_up.shape
    tile = tile_of(width, 512)
    part = ((rows, width), BF, (rows, tile), lambda d: (0, d))
    return call(
        feed_back_kernel,
        "feed_back",
        (width // tile,),
        [fixed(gg), fixed(gu), (gate_up, (2, tile, units), lambda d: (0, d, 0))],
        [part, part],
        flops=8 * rows * width * units,
        after=after,
    )


def feed_out_kernel(h, w, b0, b1):
    rows = b0.shape[0]
    out = dot(h[...], w[...]).astype(BF)
    b0[...] = out[:rows]
    b1[...] = out[rows:]


def feed_out(hidden, down, after=()):
    rows = hidden.shape[0] // 2
    units, width = down.shape
    tile = tile_of(width, 512)
    part = ((rows, width), BF, (rows, tile), lambda d: (0, d))
    return call(
        feed_out_kernel,
        "feed_out",
        (width // tile,),
        [fixed(hidden), (down, (units, tile), lambda d: (0, d))],
        [part, part],
        flops=4 * rows * width * units,
        after=after,
    )


def back_local_kernel(
    width, g0, g1, w, pg_ref, pf_ref, state_ref, gain_ref, lb_ref, *refs
):
    mixed_ref, gpg_ref, loc_ref, cum_ref, tot_ref, term_ref = refs[-6:]
    groups, rows, tile = loc_ref.shape
    steps = rows // CHUNKS
    gain = gain_ref[...]
    lb = lb_ref[...]
    grads = dot_last(jnp.concatenate([g0[:rows], g1[:rows]], axis=0), w[...])
    term = jnp.zeros((1, tile), F32)
    for g in range(groups):
        extra = (g1 if g else g0)[rows:, :rows].astype(F32)
        scales = upright(extra[0:1] + extra[1:2])
        inners = upright(extra[2:3] + extra[3:4])
        for c in range(CHUNKS):
            at = pl.ds(c * steps, steps)
            part = slice(c * steps, (c + 1) * steps)
            scale = scales[part, :1]
            coef = scale * scale * scale * inners[part, :1] * (1.0 / width)
            pg = pg_ref[g, at, :]
            gm = grads[g * rows + c * steps : g * rows + (c + 1) * steps]
            st = state_ref[g, at, :]
            sig = sigmoid(pg)
            act = pg * sig
            unit = st * scale
            gact = gm * act
            mixed_ref[g, at, :] = (unit * gain * act).astype(BF)
            gpg_ref[g, at, :] = (gm * gain * unit * (sig * (1.0 + pg * (1.0 - sig)))).astype(BF)
            term = term + jnp.sum(gact * unit, axis=0, keepdims=True)
            loc_ref[g, at, :] = scale * (gact * gain) - st * coef
    term_ref[...] = term
    for g in range(groups):
        s = jnp.zeros((CHUNKS, tile), F32)
        q = jnp.ones_like(s)
        for t in range(steps - 1, -1, -1):
            at = pl.ds(t, CHUNKS, stride=steps)
            f = lb + (1.0 - lb) * sigmoid(pf_ref[g, at, :])
            adj = loc_ref[g, at, :] + s
            loc_ref[g, at, :] = adj
            cum_ref[g, at, :] = q
            s = f * adj
            q = q * f
        last = CHUNKS - 1
        a = q[last : last + 1]
        b = s[last : last + 1]
        for c in range(CHUNKS - 2, -1, -1):
            b = q[c : c + 1] * b + s[c : c + 1]
            a = a * q[c : c + 1]
        put_total(tot_ref, g, a, b, refs[:-6])


def back_local(g0, g1, out_proj, pg, pf, state, gain, lower, prior=(), after=()):
    rows, width = pg.shape[1], g0.shape[1]
    chans = out_proj.shape[0]
    tile = tile_of(chans, 128)
    piece = ((2, rows, tile), lambda c: (0, 0, c))
    row = ((1, tile), lambda c: (0, c))
    shape = (2, rows, chans)
    before, total = total_blocks(prior, chans, tile)
    return call(
        functools.partial(back_local_kernel, width),
        "back_local",
        (chans // tile,),
        [
            fixed(g0),
            fixed(g1),
            (out_proj, (tile, width), lambda c: (c, 0)),
            (pg, *piece),
            (pf, *piece),
            (state, *piece),
            (gain, *row),
            (lower, *row),
            *before,
        ],
        [
            (shape, BF, *piece),
            (shape, BF, *piece),
            (shape, F32, *piece),
            (shape, F32, *piece),
            total,
            ((1, chans), F32, *row),
        ],
        flops=4 * rows * width * chans,
        after=after,
    )


def back_mix_kernel(
    loc_ref, cum_ref, state_ref, pi_ref, pf_ref, gpg_ref, carry_ref, prior_ref, lb_ref, w,
    both_ref, b0, b1, term_ref,
):
    _, rows, chans = loc_ref.shape
    steps = rows // CHUNKS
    lb = lb_ref[...]
    rest = 1.0 - lb
    cin = carry_ref[0]
    term = jnp.zeros((1, loc_ref.shape[2]), F32)
    top = lax.broadcasted_iota(jnp.int32, (steps, loc_ref.shape[2]), 0) == 0
    for c in range(CHUNKS - 1, -1, -1):
        at = pl.ds(c * steps, steps)
        adj = loc_ref[0, at, :] + cum_ref[0, at, :] * cin
        pi = pi_ref[0, at, :]
        sig = sigmoid(pf_ref[0, at, :])
        cin = (lb + rest * sig[0:1]) * adj[0:1]
        st = state_ref[0, at, :]
        before = prior_ref[0] if c == 0 else state_ref[0, pl.ds(c * steps - 1, 1), :]
        prev = jnp.where(top, before, pltpu.roll(st, 1, 0))
        sig_in = sigmoid(pi)
        total = adj * (prev - pi * sig_in)
        left = 1.0 - sig
        slope = sig_in * (1.0 + pi * (1.0 - sig_in))
        both_ref[0, at, :chans] = (adj * (rest * left) * slope).astype(BF)
        both_ref[0, at, chans:] = (total * rest * sig * left).astype(BF)
        term = term + jnp.sum(total * left, axis=0, keepdims=True)
    term_ref[0] = term
    out = (
        dot_last(both_ref[0, :, :chans], w[0])
        + dot_last(both_ref[0, :, chans:], w[1])
        + dot_last(gpg_ref[0], w[2])
    ).astype(BF)
    first = pl.program_id(0) == 0

    @pl.when(first)
    def _():
        b0[...] = out

    @pl.when(jnp.logical_not(first))
    def _():
        b1[...] = out


def back_mix(loc, cum, state, pi, pf, gpg, carry, prior, shift, lower, in_proj, after=()):
    _, rows, chans = state.shape
    width = in_proj.shape[1]
    piece = ((1, rows, chans), lambda g: (g, 0, 0))
    per = ((1, 1, chans), lambda g: (g, 0, 0))
    moved = ((1, 1, chans), lambda g: (g + shift, 0, 0))
    whole = ((rows, width), BF, (rows, width), lambda g: (0, 0))
    return call(
        back_mix_kernel,
        "back_mix",
        (2,),
        [(v, *piece) for v in (loc, cum, state, pi, pf, gpg)]
        + [(carry, *moved), (prior, *moved), fixed(lower), fixed(in_proj)],
        [
            ((2, rows, 2 * chans), BF, (1, rows, 2 * chans), lambda g: (g, 0, 0)),
            whole,
            whole,
            ((2, 1, chans), F32, *per),
        ],
        flops=12 * rows * width * chans,
        after=after,
    )


def total_product(near_count, refs):
    lefts, (near, far) = refs[:-2], refs[-2:]
    return dot_first(stack(*lefts[:near_count]), near[...]) + dot_first(
        stack(*lefts[near_count:]), far[...]
    )


def product_kernel(near_count, me, *refs):
    refs[-1][...] = total_product(near_count, refs[:-1]).astype(BF)


def product_add_kernel(near_count, half, me, *refs):
    got, send, keep = refs[-3:]
    total = (total_product(near_count, refs[:-3]) + got[...].astype(F32)).astype(BF)
    early = pl.program_id(0) < half

    @pl.when(early)
    def _():
        send[...] = total

    @pl.when(jnp.logical_not(early))
    def _():
        keep[...] = total


def product(me, lefts, near, far, bits, size, got=None, after=()):
    levels = len(bits)
    count = 1 << (levels - 1)
    base = 0 if got is None else count
    top = 2 * count - 1 - base
    units = near.shape[1]
    near_count = len(lefts[0])
    lefts = [*lefts[0], *lefts[1]]

    def place(j, me):
        turned = top - j
        block = me[0]
        for n, bit in enumerate(bits):
            block = block ^ (((turned >> (levels - 1 - n)) & 1) * bit)
        return (0, block)

    if size % 128:
        def ordered(x, rows):
            parts = [
                lax.dynamic_slice_in_dim(x[:rows], place(j, me)[1] * size, size, 1)
                for j in range(count)
            ]
            return jnp.concatenate(parts, axis=1), rows

        lefts = [ordered(*x) for x in lefts]
        count, size = count * size // 128, 128
        position = lambda j, me: (0, j)
    else:
        position = place
    inputs = [(x, (rows, size), position) for x, rows in lefts]
    inputs += [fixed(near), fixed(far)]
    flops = 0
    if got is None:
        out = ((count * size, units), BF, (size, units), lambda j, me: (j, 0))
        return call(
            functools.partial(product_kernel, near_count),
            "product", (count,), inputs, [out], flops, after, blocks=me,
        )
    half = count // 2
    inputs.append((got, (size, units), lambda j, me: (j, 0)))
    shape = (half * size, units)
    send = (shape, BF, (size, units), lambda j, me: (jnp.minimum(j, half - 1), 0))
    keep = (shape, BF, (size, units), lambda j, me: (jnp.maximum(j - half, 0), 0))
    return call(
        functools.partial(product_add_kernel, near_count, half),
        "product_add",
        (count,),
        inputs,
        [send, keep],
        flops,
        after,
        blocks=me,
    )


def halve_kernel(half, one, two, send, keep):
    total = (one[...].astype(F32) + two[...].astype(F32)).astype(BF)
    early = pl.program_id(0) < half

    @pl.when(early)
    def _():
        send[...] = total

    @pl.when(jnp.logical_not(early))
    def _():
        keep[...] = total


def halve(one, two, size, after=()):
    count = one.shape[0] // size
    half = count // 2
    units = one.shape[1]
    block = ((size, units), lambda j: (j, 0))
    shape = (half * size, units)
    return call(
        functools.partial(halve_kernel, half),
        "halve",
        (count,),
        [(one, *block), (two, *block)],
        [
            (shape, BF, (size, units), lambda j: (jnp.minimum(j, half - 1), 0)),
            (shape, BF, (size, units), lambda j: (jnp.maximum(j - half, 0), 0)),
        ],
        after=after,
    )


def finish_kernel(turned, one, two, *refs):
    out = refs[-1]
    total = one[...].astype(F32) + two[...].astype(F32)
    if turned:
        out[...] = total.T
    else:
        parts, _, units = out.shape
        for part in range(parts):
            out[part] = total[:, part * units : (part + 1) * units]


def finish(one, two, turned=False, slot=0, parts=1, slots=1, into=None, after=()):
    rows, units = one.shape
    if turned:
        tile = 128 if rows % 128 == 0 else rows
        shape = (units, rows)
        out = pl.BlockSpec((units, tile), lambda n: (0, n))
    else:
        tile = 64 if rows % 64 == 0 else rows
        shape = (slots, rows, units // parts)
        out = pl.BlockSpec((parts, tile, units // parts), lambda n: (slot // parts, n, 0))
    block = pl.BlockSpec((tile, units), lambda n: (n, 0))
    held = [] if into is None else [into]
    waits = [*held, *after]
    count = len(waits)
    return pl.pallas_call(
        lambda one, two, *refs: finish_kernel(turned, one, two, *refs[count:]),
        grid=(rows // tile,),
        in_specs=[block, block] + [ANYWHERE] * count,
        out_specs=out,
        out_shape=sds(shape),
        input_output_aliases={2: 0} if held else {},
        compiler_params=pltpu.CompilerParams(vmem_limit_bytes=VMEM_LIMIT),
        cost_estimate=pl.CostEstimate(flops=0, bytes_accessed=0, transcendentals=0),
        name="finish",
    )(one, two, *waits)


def row_call(kernel, name, arrays, gains, outputs, sums=0, after=(), most=64, more=()):
    rows, width = arrays[0].shape[-2:]
    tile = most if rows % most == 0 else rows

    def block(shape):
        lead = len(shape) - 2
        return (*shape[:-2], tile, shape[-1]), lambda r: (*(0,) * lead, r, 0)

    inputs = [(a, *block(a.shape)) for a in arrays] + [fixed(g) for g in gains]
    results = [(shape, dtype, *block(shape)) for shape, dtype in outputs]
    results += [((1, width), F32, (1, width), lambda r: (0, 0))] * sums + list(more)
    return call(kernel, name, (rows // tile,), inputs, results, after=after)


def add_to(ref, term):
    first = pl.program_id(0) == 0

    @pl.when(first)
    def _():
        ref[...] = term

    @pl.when(jnp.logical_not(first))
    def _():
        ref[...] += term


def first_norm_kernel(x_ref, gain_ref, out):
    x = x_ref[...].astype(F32)
    out[...] = (x * rms_scale(x) * gain_ref[...]).astype(BF)


def plus_kernel(one, two, out):
    out[...] = (one[...].astype(F32) + two[...].astype(F32)).astype(BF)


def plus(one, two, after=()):
    return row_call(plus_kernel, "plus", [one, two], [], [(one.shape, BF)], after=after)


def join_kernel(one, two, top, bottom):
    half = bottom.shape[0]
    rows = 2 * half
    for out, at in ((top, 0), (bottom, half)):
        part = slice(at, at + half)
        out[:half] = (one[part].astype(F32) + two[part].astype(F32)).astype(BF)
    extra = one[rows:].astype(F32) + two[rows:].astype(F32)
    top[half:] = in_two(jnp.broadcast_to(extra[0:1] + extra[1:2], extra.shape))


def join(one, two, after=()):
    rows, width = one.shape[0] - EXTRA, one.shape[1]
    shapes = [(rows // 2 + EXTRA, width), (rows // 2, width)]
    return call(
        join_kernel, "join", (1,), [fixed(one), fixed(two)],
        [(s, BF, s, lambda i: (0, 0)) for s in shapes], after=after,
    )


def middle_kernel(half, x, own, core, hop, own_more, core_more, hop_more, gain, *refs):
    branch_ref, middle_ref, scale_ref, full, out = refs[-5:]
    rows, width = x.shape
    more = own_more[...].astype(F32) + core_more[...].astype(F32) + hop_more[...].astype(F32)
    squares = (more[0:1] + more[1:2])[:, half * rows : (half + 1) * rows]
    scale = lax.rsqrt(upright(squares) / width + EPS)
    branch = own[...].astype(F32) + core[...].astype(F32) + hop[...].astype(F32)
    middle = x[...].astype(F32) + branch * scale[:, :1]
    branch_ref[...] = branch
    scale_ref[...] = scale
    middle_ref[...] = middle
    low = (middle * rms_scale(middle) * gain[...]).astype(BF)
    full[...] = low
    out[...] = low


def middle_half(half, x, own, core, hop, top, gain, begun=(), after=()):
    total, width = x.shape
    rows = total // 2
    part = pl.BlockSpec((rows, width), lambda i: (half, 0))
    alone = pl.BlockSpec((rows, width), lambda i: (0, 0))
    more = pl.BlockSpec((EXTRA, width), lambda i: (total // EXTRA, 0))
    top_more = pl.BlockSpec((EXTRA, width), lambda i: (rows // EXTRA, 0))
    waits = [*begun, *after]
    return pl.pallas_call(
        functools.partial(middle_kernel, half),
        grid=(1,),
        in_specs=[part, part, part, alone, more, more, top_more, pl.BlockSpec((1, width), lambda i: (0, 0))]
        + [ANYWHERE] * len(waits),
        out_specs=[part, part, pl.BlockSpec((rows, 128), lambda i: (half, 0)), part, alone],
        out_shape=[
            sds((total, width)), sds((total, width)), sds((total, 128)), sds((total, width), BF),
            sds((rows + (16 if half == 0 else 0), width), BF),
        ],
        input_output_aliases={8 + n: n for n in range(len(begun))},
        compiler_params=pltpu.CompilerParams(vmem_limit_bytes=VMEM_LIMIT),
        cost_estimate=pl.CostEstimate(flops=0, bytes_accessed=0, transcendentals=0),
        name="middle",
    )(x, own, core, hop, own, core, top, gain, *waits)


def turn_kernel(up, own, core, hop, middle_ref, branch, scale_ref, gain, grad_ref, term, out):
    tile = up.shape[0]
    step = pl.program_id(0)
    rows = out.shape[0] - EXTRA
    grad = own[...].astype(F32) + core[...].astype(F32) + hop[...].astype(F32)
    middle = middle_ref[...]
    scale = rms_scale(middle)
    total = up[...].astype(F32) + norm_back(grad, middle, scale, gain[...])
    low = total.astype(BF)
    grad_ref[...] = total
    out[pl.ds(pl.multiple_of(step * tile, tile), tile), :] = low
    inner = wide(jnp.sum(low.astype(F32) * branch[...], axis=-1, keepdims=True)).T[:EXTRA]
    outer = scale_ref[...].T[:EXTRA]
    high_outer = outer.astype(BF).astype(F32)
    high_inner = inner.astype(BF).astype(F32)
    which = lax.broadcasted_iota(jnp.int32, inner.shape, 0)
    both = jnp.where(which < 2, outer, inner)
    high = jnp.where(which < 2, high_outer, high_inner)
    extra = jnp.where(which % 2 == 0, high, both - high)

    @pl.when(step == 0)
    def _():
        out[rows:, :] = jnp.zeros((EXTRA, out.shape[1]), BF)

    out[rows:, pl.ds(pl.multiple_of(step * tile, tile), tile)] = extra.astype(BF)
    add_to(term, jnp.sum(grad * middle * scale, axis=0, keepdims=True))


def turn(up, own, core, hop, middle, branch, scale, gain, after=()):
    rows, width = up.shape
    shape = (rows + EXTRA, width)
    return row_call(
        turn_kernel, "turn", [up, own, core, hop, middle, branch, scale], [gain],
        [(up.shape, F32)], sums=1, after=after, most=128,
        more=[(shape, BF, shape, lambda r: (0, 0))],
    )


def last_kernel(x_ref, own, core, hop, grad_middle, gain, out, term):
    grad = own[...].astype(F32) + core[...].astype(F32) + hop[...].astype(F32)
    x = x_ref[...].astype(F32)
    scale = rms_scale(x)
    out[...] = grad_middle[...] + norm_back(grad, x, scale, gain[...])
    add_to(term, jnp.sum(grad * x * scale, axis=0, keepdims=True))


def result_kernel(middle, own, core, hop, out):
    out[...] = (
        middle[...] + (own[...].astype(F32) + core[...].astype(F32) + hop[...].astype(F32))
    ).astype(BF)


def in_order(me, total, other):
    odd = (me[0] % 2) == 1
    return (
        odd,
        jnp.where(odd, other[0], total[0]),
        jnp.where(odd, other[1], total[1]),
        jnp.where(odd, total[0], other[0]),
        jnp.where(odd, total[1], other[1]),
    )


def pair_kernel(reverse, me, total, other, pair):
    odd, low_a, low_b, high_a, high_b = in_order(me, total, other)
    pair[0] = low_a * high_a
    pair[1] = low_a * high_b + low_b if reverse else high_a * low_b + high_b


def enter_kernel(reverse, me, total, other, *refs):
    odd, low_a, low_b, high_a, high_b = in_order(me, total, other)
    enter = jnp.zeros_like(low_a)
    for got in reversed(refs[:-1]):
        enter = got[0] * enter + got[1]
    if reverse:
        enter = jnp.where(odd, enter, high_a * enter + high_b)
    else:
        enter = jnp.where(odd, low_a * enter + low_b, enter)
    for g in range(enter.shape[0]):
        refs[-1][g] = enter[g : g + 1]


def chain(me, total, reverse, between=None, beside=None):
    size = lax.axis_size("seq")
    _, groups, chans = total.shape
    other = swap(total, "seq", 1)
    got = between() if between else ()
    whole = (total.shape, F32, total.shape, lambda i, me: (0, 0, 0))
    pair = call(
        functools.partial(pair_kernel, reverse), "pair", (1,), [fixed(total), fixed(other)], [whole],
        after=got, blocks=me,
    )
    sign = -1 if reverse else 1
    reached = [shift(pair, "seq", 2 * sign * d) for d in range(1, size // 2)]
    shape = (groups, 1, chans)
    got = beside(pair) if beside else ()
    return call(
        functools.partial(enter_kernel, reverse), "enter", (1,),
        [fixed(total), fixed(other), *[fixed(r) for r in reached]],
        [(shape, F32, shape, lambda i, me: (0, 0, 0))],
        after=got,
        blocks=me,
    )


def seq_bits():
    size = lax.axis_size("seq")
    bits = []
    bit = 1
    while bit < size:
        bits.append(bit)
        bit *= 2
    return bits


class Weight:
    def __init__(self, me, lefts, near, far, bits, size):
        self.me, self.lefts, self.near, self.far = me, lefts, near, far
        self.bits, self.size, self.level = bits, size, 0

    def begin(self, *earlier):
        self.send = product(
            self.me, self.lefts, self.near, self.far, self.bits, self.size, after=earlier
        )
        return self.send

    def go(self, *earlier):
        send = after(self.send, *earlier) if earlier else self.send
        self.got = swap(send, "seq", self.bits[self.level])
        self.level += 1

    def step(self, *earlier):
        if self.level == 1:
            self.send, self.keep = product(
                self.me, self.lefts, self.near, self.far, self.bits, self.size, self.got, after=earlier
            )
        else:
            self.send, self.keep = halve(self.keep, self.got, self.size, after=earlier)
        return self.send

    def last(self):
        return self.level == len(self.bits)


def gain_terms(norm1_term, norm2_term, mixer_term, bound_n, bound_f):
    wt = lax.axis_index("wt")
    span = norm1_term.shape[1] // lax.axis_size("wt")
    norm_terms = jnp.concatenate([norm1_term, norm2_term])

    def part(j):
        return lax.dynamic_slice_in_dim(norm_terms, (wt ^ j) * span, span, 1)

    norms = part(0)
    for j in (1, 2, 3):
        norms = norms + swap(part(j), "wt", j)
    bound_term = jnp.sum(bound_n, axis=(0, 1)) + jnp.sum(bound_f, axis=(0, 1))
    return jnp.stack([norms[0], mixer_term[0], norms[1], bound_term])


GATE_AT, LOWER_AT, UP_AT, LOWER_BITS = "before", "beside", "pair", "m"
ORDER = (
    ("-p", "-n", "gs", "bb", "us", "-l", "ob", "ls", "ab", "us", "-r", "gf", "bs")
    + ("os", "as", "lf", "bs", "uf", "as", "os", "bf", "-1", "af", "-2", "-3", "of")
)


def on_device(
    tokens,
    in_proj,
    out_proj,
    gate_up,
    down,
    norm1_gain,
    mixer_gain,
    norm2_gain,
    lower_bound,
    cotangent,
):
    width = in_proj.shape[1]
    chans = in_proj.shape[2]
    x = tokens[0]
    g0 = cotangent[0]
    rows = x.shape[0]
    bits = seq_bits()
    y_first = bits
    mixed_order = {"m": bits[1:2] + bits[:1] + bits[2:], "z": bits[1:] + bits[:1], "y": bits}[LOWER_BITS]
    block = width // lax.axis_size("seq")
    me = lax.axis_index("seq").reshape(1).astype(jnp.int32)

    offset = lax.axis_index("wt") * chans
    lower_use = lax.dynamic_slice_in_dim(lower_bound, offset, chans)[None]
    mixer_use = lax.dynamic_slice_in_dim(mixer_gain, offset, chans)[None]
    gain_one, gain_two = norm1_gain[None], norm2_gain[None]

    n0 = row_call(first_norm_kernel, "first_norm", [x], [gain_one], [(x.shape, BF)])
    hop = swap(n0, "wt", 2)
    n1 = swap(n0, "wt", 1)
    g1 = swap(g0, "wt", 1)
    grad_hop = swap(after(g0, n0), "wt", 2)
    pi_n, pf_n, pg_n, loc_n, cum_n, tot = project(n0, n1, in_proj, lower_use)
    gh_n = hidden_grad(g0, g1, down, after=(tot,))
    n2 = after(hop, gh_n)
    n3 = swap(n2, "wt", 1)
    pi_f, pf_f, pg_f, loc_f, cum_f, tot = project(n2, n3, in_proj, lower_use, (tot,))
    enter = chain(me, tot, False)
    state_f, bf0, bf1 = mix(loc_f, cum_f, pg_f, enter, 2, mixer_use, out_proj)
    g2 = after(grad_hop, bf0)
    g3 = swap(g2, "wt", 1)
    state_n, bn0, bn1 = mix(loc_n, cum_n, pg_n, enter, 0, mixer_use, out_proj, after=(bf0,))
    across = join(bf0, swap(bf1, "wt", 1), after=(bn0,))
    hops = [swap(part, "wt", 2) for part in across]
    core = swap(bn1, "wt", 1)
    gh_f = hidden_grad(g2, g3, down, after=(across[1],))
    *begun, half0 = middle_half(0, x, bn0, core, hops[0], hops[0], gain_two, after=(gh_f,))
    branch, middle, scale_two, t0, half1 = middle_half(
        1, x, bn0, core, hops[1], hops[0], gain_two, begun
    )

    hops = [swap(half, "wt", 2) for half in (half0, half1)]
    t1 = [swap(half, "wt", 1) for half in (half0, half1)]
    hid_n, gg_n, gu_n = feed((t0, *t1), gate_up, gh_n)
    kn0, kn1 = feed_back(gg_n, gu_n, gate_up)
    core = swap(kn1, "wt", 1)
    t2 = [after(hop, kn0) for hop in hops]
    t3 = [swap(half, "wt", 1) for half in t2]
    hid_f, gg_f, gu_f = feed((*t2, *t3), gate_up, gh_f)

    def pieces(*arrays):
        return [(v, min(rows, v.shape[0]) // 128 * 128) for v in arrays]

    twos = (pieces(t0, *t1), pieces(*t2, *t3))
    gate = Weight(me, twos, gg_n, gg_f, y_first, block)
    up = Weight(me, twos, gu_n, gu_f, y_first, block)
    lower = Weight(me, (pieces(g0, g1), pieces(g2, g3)), hid_n, hid_f, mixed_order, block)
    kf0, kf1 = feed_back(gg_f, gu_f, gate_up)
    gate.begin(kf0)
    gate.go()
    across = plus(kf0, swap(kf1, "wt", 1), after=(gate.send,))
    hop = swap(across, "wt", 2)
    lower.begin(across)
    lower.go()
    up.begin(lower.send, across)
    ff0, ff1 = feed_out(hid_f, down, after=(up.send,))
    grad_middle, norm2_term, b0 = turn(
        g0, kn0, core, hop, middle, branch, scale_two, gain_two, after=(ff0,)
    )

    hop = swap(b0, "wt", 2)
    b1 = swap(b0, "wt", 1)
    mixed_n, gpg_n, bloc_n, bcum_n, btot, mixer_n = back_local(
        b0, b1, out_proj, pg_n, pf_n, state_n, mixer_use, lower_use
    )
    ffn_across = plus(ff0, swap(ff1, "wt", 1), after=(btot,))
    fn0, fn1 = feed_out(hid_n, down, after=(ffn_across,))
    ffn_core = swap(fn1, "wt", 1)
    b2 = after(hop, fn0)
    b3 = swap(b2, "wt", 1)
    early = (gate.step(b2),) if GATE_AT == "before" else ()
    mixed_f, gpg_f, bloc_f, bcum_f, btot, mixer_f = back_local(
        b2, b3, out_proj, pg_f, pf_f, state_f, mixer_use, lower_use, (btot,), after=early
    )

    def beside(pair):
        if UP_AT == "pair":
            up.go(pair)
        for one, place in ((gate, GATE_AT), (lower, LOWER_AT)):
            if place == "beside":
                pair = one.step(pair)
        return (pair,)

    leave = chain(me, btot, True, None, beside)
    if UP_AT == "leave":
        up.go(leave)
    if GATE_AT == "after":
        gate.step(leave)
        gate.go()
    else:
        gate.go(leave)
    if LOWER_AT == "beside":
        if LOWER_BITS == "z":
            lower.go(leave)
        else:
            lower.go()
    both_f, df0, df1, bound_f = back_mix(
        bloc_f, bcum_f, state_f, pi_f, pf_f, gpg_f, leave, enter, 2, lower_use, in_proj
    )

    def flat(values):
        return values.reshape(2 * rows, values.shape[2])

    normals = (pieces(n0, n1), pieces(n2, n3))
    last_in = Weight(me, normals, flat(gpg_n), flat(gpg_f), y_first, block)
    out = Weight(me, (pieces(b0, b1), pieces(b2, b3)), flat(mixed_n), flat(mixed_f), y_first, block)
    both_n, dn0, dn1, bound_n = None, None, None, None
    token = df0
    weights = {"g": gate, "u": up, "l": lower, "a": last_in, "o": out}
    rounds = list(bits)
    gate_up_grad = in_grad = None
    for kind, act in ORDER:
        if kind in weights:
            one = weights[kind]
            if act == "b":
                token = one.begin(token)
                one.go()
            elif act == "s":
                token = one.step(token)
                one.go()
                while one.level > 2 and not one.last():
                    token = one.step(token)
                    one.go()
            elif kind in "gu":
                slot = "gu".index(kind)
                token = gate_up_grad = finish(
                    one.keep, one.got, slot=slot, slots=2, into=gate_up_grad,
                    after=() if token is gate_up_grad else (token,),
                )
            elif kind == "b":
                token = in_grad = finish(
                    one.keep, one.got, parts=2, slots=3, into=in_grad,
                    after=() if token is in_grad else (token,),
                )
            elif kind == "a":
                token = in_grad = finish(
                    one.keep, one.got, slot=2, slots=3, into=in_grad,
                    after=() if token is in_grad else (token,),
                )
            elif kind == "l":
                token = down_grad = finish(one.keep, one.got, True, after=(token,))
            else:
                token = out_grad = finish(one.keep, one.got, True, after=(token,))
        elif act == "p":
            token = plus(df0, swap(df1, "wt", 1), after=(token,))
            hop = swap(token, "wt", 2)
        elif act == "n":
            both_n, dn0, dn1, bound_n = back_mix(
                bloc_n, bcum_n, state_n, pi_n, pf_n, gpg_n, leave, enter, 0, lower_use, in_proj,
                after=(token,),
            )
            token = dn0
            core = swap(dn1, "wt", 1)
            weights["b"] = Weight(me, normals, flat(both_n), flat(both_f), y_first, block)
        elif act == "l":
            grad_inputs, norm1_term = row_call(
                last_kernel,
                "last",
                [x, dn0, core, hop, grad_middle],
                [gain_one],
                [(x.shape, F32)],
                sums=1,
                after=(token,),
            )
            token = grad_inputs
            ffn_hop = swap(after(ffn_across, token), "wt", 2)
            gains = gain_terms(norm1_term, norm2_term, mixer_n + mixer_f, bound_n, bound_f)
        elif act == "r":
            token = result = row_call(
                result_kernel, "result", [middle, fn0, ffn_core, ffn_hop], [], [(x.shape, BF)],
                after=(token,),
            )
        elif act in "123":
            for _ in range(len(rounds) if act == "3" else 1):
                gains = gains + after(swap(gains, "seq", rounds.pop(0)), token)

    return (
        result[None],
        grad_inputs[None],
        in_grad,
        out_grad,
        gate_up_grad,
        down_grad,
        gains[0],
        gains[1],
        gains[2],
        gains[3],
    )


def solution(mesh):
    placed = (
        P("wt", "seq", None),
        P(None, None, "wt"),
        P("wt", None),
        P(None, None, "wt"),
        P("wt", None),
        P(),
        P(),
        P(),
        P(),
        P("wt", "seq", None),
    )
    return jax.shard_map(
        on_device,
        mesh=mesh,
        in_specs=placed,
        out_specs=(
            P("wt", "seq", None),
            P("wt", "seq", None),
            P(None, "seq", "wt"),
            P("wt", "seq"),
            P(None, "seq", "wt"),
            P("wt", "seq"),
            P("wt"),
            P("wt"),
            P("wt"),
            P("wt"),
        ),
        check_vma=False,
    )
```

```python
import functools

import jax
import jax.numpy as jnp
from jax import lax
from jax.experimental import pallas as pl
from jax.experimental.pallas import tpu as pltpu
from jax.sharding import PartitionSpec as P

EPS = 1e-06
BF = jnp.bfloat16
F32 = jnp.float32
CHUNKS = 8


def swap(values, axis, bit):
    size = lax.axis_size(axis)
    return lax.ppermute(values, axis, [(i, i ^ bit) for i in range(size)])


def shift(values, axis, step):
    size = lax.axis_size(axis)
    pairs = [(i, i + step) for i in range(size) if 0 <= i + step < size]
    return lax.ppermute(values, axis, pairs)


def rms_scale(values):
    return lax.rsqrt(jnp.mean(values * values, axis=-1, keepdims=True) + EPS)


def norm_back(grad_normed, values, scale, weight):
    weighted = grad_normed * weight
    return scale * weighted - values * (scale * scale * scale) * jnp.mean(
        weighted * values, axis=-1, keepdims=True
    )


def sigmoid(v):
    return 0.5 * jnp.tanh(0.5 * v) + 0.5


ANYWHERE = pl.BlockSpec(memory_space=pl.ANY)
EXTRA = 16
VMEM_LIMIT = 63 * 1024 * 1024


def sds(shape, dtype=F32):
    return jax.ShapeDtypeStruct(shape, dtype)


def call(kernel, name, grid, inputs, outputs, flops=0, after=(), scratch=(), blocks=None):
    in_specs = [pl.BlockSpec(block, index) for _, block, index in inputs]
    in_specs += [ANYWHERE] * len(after)
    out_specs = [pl.BlockSpec(block, index) for _, _, block, index in outputs]
    count = len(inputs)
    skip = len(after)
    lead = 0 if blocks is None else 1

    def body(*refs):
        kernel(*refs[: lead + count], *refs[lead + count + skip :])

    settings = dict(
        out_shape=[sds(shape, dtype) for shape, dtype, _, _ in outputs],
        compiler_params=pltpu.CompilerParams(vmem_limit_bytes=VMEM_LIMIT),
        cost_estimate=pl.CostEstimate(flops=0, bytes_accessed=0, transcendentals=0),
        name=name,
    )
    operands = [a for a, _, _ in inputs] + list(after)
    if blocks is None:
        got = pl.pallas_call(
            body, grid=grid, in_specs=in_specs, out_specs=out_specs, scratch_shapes=list(scratch), **settings
        )(*operands)
    else:
        spec = pltpu.PrefetchScalarGridSpec(
            num_scalar_prefetch=1,
            grid=grid,
            in_specs=in_specs,
            out_specs=out_specs,
            scratch_shapes=list(scratch),
        )
        got = pl.pallas_call(body, grid_spec=spec, **settings)(blocks, *operands)
    return got[0] if len(outputs) == 1 else got


def fixed(array):
    zeros = (0,) * array.ndim
    return (array, array.shape, lambda *_: zeros)


def hold_kernel(*refs):
    pass


def after(value, *earlier):
    return pl.pallas_call(
        hold_kernel,
        in_specs=[ANYWHERE] * (1 + len(earlier)),
        out_specs=ANYWHERE,
        out_shape=jax.ShapeDtypeStruct(value.shape, value.dtype),
        input_output_aliases={0: 0},
        cost_estimate=pl.CostEstimate(flops=0, bytes_accessed=0, transcendentals=0),
        name="hold",
    )(value, *earlier)


def dot(left, right):
    return jnp.dot(left, right, preferred_element_type=F32)


def dot_last(left, right):
    return lax.dot_general(left, right, (((1,), (1,)), ((), ())), preferred_element_type=F32)


def dot_first(left, right):
    return lax.dot_general(left, right, (((0,), (0,)), ((), ())), preferred_element_type=F32)


def wide(column):
    return jnp.broadcast_to(column, (column.shape[0], 128))


def in_two(values):
    which = lax.broadcasted_iota(jnp.int32, values.shape, 0)
    high = values.astype(BF).astype(F32)
    return jnp.where(which == 0, high, jnp.where(which == 1, values - high, 0.0)).astype(BF)


def upright(row):
    return jnp.broadcast_to(row, (128, row.shape[1])).T


def stack(*refs):
    return jnp.concatenate([r[...] for r in refs], axis=0)


def tile_of(size, most):
    best = size
    for tile in range(128, most + 1, 128):
        if size % tile == 0:
            best = tile
    return best


def project_kernel(x0, x1, w, lb_ref, *refs):
    pi_ref, pf_ref, pg_ref, loc_ref, cum_ref, tot_ref = refs[-6:]
    groups, rows, tile = loc_ref.shape
    steps = rows // CHUNKS
    y = dot(stack(x0, x1), jnp.concatenate([w[0], w[1], w[2]], axis=1))
    lb = lb_ref[...]
    for g in range(groups):
        part = y[g * rows : (g + 1) * rows]
        pi_ref[g] = part[:, :tile]
        pf_ref[g] = part[:, tile : 2 * tile]
        pg_ref[g] = part[:, 2 * tile :]
    for g in range(groups):
        s = jnp.zeros((CHUNKS, tile), F32)
        p = jnp.ones_like(s)
        for t in range(steps):
            at = pl.ds(t, CHUNKS, stride=steps)
            pi = pi_ref[g, at, :]
            sig = sigmoid(pf_ref[g, at, :])
            f = lb + (1.0 - lb) * sig
            s = f * s + pi * sigmoid(pi) * ((1.0 - lb) * (1.0 - sig))
            p = p * f
            loc_ref[g, at, :] = s
            cum_ref[g, at, :] = p
        a = p[0:1]
        b = s[0:1]
        for c in range(1, CHUNKS):
            b = p[c : c + 1] * b + s[c : c + 1]
            a = a * p[c : c + 1]
        put_total(tot_ref, g, a, b, refs[:-6])


def put_total(tot_ref, g, a, b, prior):
    at = g
    if prior:
        at = g + prior[0].shape[1]
        if g == 0:
            tot_ref[:, : prior[0].shape[1], :] = prior[0][...]
    tot_ref[0, at : at + 1, :] = a
    tot_ref[1, at : at + 1, :] = b


def total_blocks(prior, chans, tile):
    count = 2 + sum(p.shape[1] for p in prior)
    inputs = [(p, (2, p.shape[1], tile), lambda c: (0, 0, c)) for p in prior]
    return inputs, ((2, count, chans), F32, (2, count, tile), lambda c: (0, 0, c))


def project(x0, x1, in_proj, lower, prior=(), after=()):
    rows, width = x0.shape
    chans = in_proj.shape[2]
    tile = tile_of(chans, 128)
    full = ((2, rows, chans), F32, (2, rows, tile), lambda c: (0, 0, c))
    before, total = total_blocks(prior, chans, tile)
    return call(
        project_kernel,
        "project",
        (chans // tile,),
        [
            fixed(x0),
            fixed(x1),
            (in_proj, (3, width, tile), lambda c: (0, 0, c)),
            (lower, (1, tile), lambda c: (0, c)),
            *before,
        ],
        [full] * 5 + [total],
        flops=12 * rows * width * chans,
        after=after,
    )


def mix_kernel(loc_ref, cum_ref, pg_ref, carry_ref, gain_ref, w_ref, state_ref, b0, b1, mix_ref, sq_ref):
    rows = loc_ref.shape[1]
    steps = rows // CHUNKS
    gain = gain_ref[...]
    cin = carry_ref[0]
    for c in range(CHUNKS):
        at = pl.ds(c * steps, steps)
        st = loc_ref[0, at, :] + cum_ref[0, at, :] * cin
        cin = st[steps - 1 : steps]
        pg = pg_ref[0, at, :]
        state_ref[0, at, :] = st
        mix_ref[at, :] = (st * gain * (pg * sigmoid(pg))).astype(BF)
        sq_ref[at, :] = wide(jnp.sum(st * st, axis=-1, keepdims=True))
    out = dot(mix_ref[...], w_ref[...]).astype(BF)
    first = pl.program_id(0) == 0

    def put(ref):
        ref[:rows] = out
        ref[rows:] = jnp.zeros((EXTRA, out.shape[1]), BF)
        ref[rows:, :rows] = in_two(sq_ref[...].T[:EXTRA])

    @pl.when(first)
    def _():
        put(b0)

    @pl.when(jnp.logical_not(first))
    def _():
        put(b1)


def mix(loc, cum, pg, carry, shift, gain, out_proj, after=()):
    _, rows, chans = loc.shape
    width = out_proj.shape[1]
    piece = ((1, rows, chans), lambda g: (g, 0, 0))
    shape = (rows + EXTRA, width)
    whole = (shape, BF, shape, lambda g: (0, 0))
    return call(
        mix_kernel,
        "mix",
        (2,),
        [
            (loc, *piece),
            (cum, *piece),
            (pg, *piece),
            (carry, (1, 1, chans), lambda g: (g + shift, 0, 0)),
            fixed(gain),
            fixed(out_proj),
        ],
        [
            (loc.shape, F32, *piece),
            whole,
            whole,
        ],
        flops=4 * rows * chans * width,
        after=after,
        scratch=[pltpu.VMEM((rows, chans), BF), pltpu.VMEM((rows, 128), F32)],
    )


def hidden_grad_kernel(g0, g1, w, out):
    out[...] = dot_last(stack(g0, g1), w[...])


def hidden_grad(g0, g1, down, after=()):
    rows, width = g0.shape
    units = down.shape[0]
    tile = min(512, units)
    return call(
        hidden_grad_kernel,
        "hidden_grad",
        (pl.cdiv(units, tile),),
        [fixed(g0), fixed(g1), (down, (tile, width), lambda n: (n, 0))],
        [((2 * rows, units), F32, (2 * rows, tile), lambda n: (0, n))],
        flops=4 * rows * width * units,
        after=after,
    )


def feed_kernel(*refs):
    w, gh_ref, hidden, gg, gu = refs[-5:]
    x = stack(*refs[:-5])
    gate = dot(x, w[0])
    up = dot(x, w[1])
    gh = gh_ref[...]
    sig = sigmoid(gate)
    act = gate * sig
    hidden[...] = (act * up).astype(BF)
    gg[...] = (gh * up * (sig * (1.0 + gate * (1.0 - sig)))).astype(BF)
    gu[...] = (gh * act).astype(BF)


def feed(pieces, gate_up, gh, after=()):
    rows, width = gh.shape[0] // 2, gate_up.shape[1]
    units = gate_up.shape[2]
    tile = min(512, units)
    col = ((2 * rows, tile), lambda n: (0, n))
    return call(
        feed_kernel,
        "feed",
        (pl.cdiv(units, tile),),
        [
            *[(x, (min(x.shape[0], rows) // 128 * 128, width), lambda n: (0, 0)) for x in pieces],
            (gate_up, (2, width, tile), lambda n: (0, 0, n)),
            (gh, *col),
        ],
        [((2 * rows, units), BF, *col)] * 3,
        flops=8 * rows * width * units,
        after=after,
    )


def feed_back_kernel(gg, gu, w, b0, b1):
    rows = b0.shape[0]
    out = (dot_last(gg[...], w[0]) + dot_last(gu[...], w[1])).astype(BF)
    b0[...] = out[:rows]
    b1[...] = out[rows:]


def feed_back(gg, gu, gate_up, after=()):
    rows = gg.shape[0] // 2
    _, width, units = gate_up.shape
    tile = tile_of(width, 512)
    part = ((rows, width), BF, (rows, tile), lambda d: (0, d))
    return call(
        feed_back_kernel,
        "feed_back",
        (width // tile,),
        [fixed(gg), fixed(gu), (gate_up, (2, tile, units), lambda d: (0, d, 0))],
        [part, part],
        flops=8 * rows * width * units,
        after=after,
    )


def feed_out_kernel(h, w, b0, b1):
    rows = b0.shape[0]
    out = dot(h[...], w[...]).astype(BF)
    b0[...] = out[:rows]
    b1[...] = out[rows:]


def feed_out(hidden, down, after=()):
    rows = hidden.shape[0] // 2
    units, width = down.shape
    tile = tile_of(width, 512)
    part = ((rows, width), BF, (rows, tile), lambda d: (0, d))
    return call(
        feed_out_kernel,
        "feed_out",
        (width // tile,),
        [fixed(hidden), (down, (units, tile), lambda d: (0, d))],
        [part, part],
        flops=4 * rows * width * units,
        after=after,
    )


def back_local_kernel(
    width, g0, g1, w, pg_ref, pf_ref, state_ref, gain_ref, lb_ref, *refs
):
    mixed_ref, gpg_ref, loc_ref, cum_ref, tot_ref, term_ref = refs[-6:]
    groups, rows, tile = loc_ref.shape
    steps = rows // CHUNKS
    gain = gain_ref[...]
    lb = lb_ref[...]
    grads = dot_last(jnp.concatenate([g0[:rows], g1[:rows]], axis=0), w[...])
    term = jnp.zeros((1, tile), F32)
    for g in range(groups):
        extra = (g1 if g else g0)[rows:, :rows].astype(F32)
        scales = upright(extra[0:1] + extra[1:2])
        inners = upright(extra[2:3] + extra[3:4])
        for c in range(CHUNKS):
            at = pl.ds(c * steps, steps)
            part = slice(c * steps, (c + 1) * steps)
            scale = scales[part, :1]
            coef = scale * scale * scale * inners[part, :1] * (1.0 / width)
            pg = pg_ref[g, at, :]
            gm = grads[g * rows + c * steps : g * rows + (c + 1) * steps]
            st = state_ref[g, at, :]
            sig = sigmoid(pg)
            act = pg * sig
            unit = st * scale
            gact = gm * act
            mixed_ref[g, at, :] = (unit * gain * act).astype(BF)
            gpg_ref[g, at, :] = (gm * gain * unit * (sig * (1.0 + pg * (1.0 - sig)))).astype(BF)
            term = term + jnp.sum(gact * unit, axis=0, keepdims=True)
            loc_ref[g, at, :] = scale * (gact * gain) - st * coef
    term_ref[...] = term
    for g in range(groups):
        s = jnp.zeros((CHUNKS, tile), F32)
        q = jnp.ones_like(s)
        for t in range(steps - 1, -1, -1):
            at = pl.ds(t, CHUNKS, stride=steps)
            f = lb + (1.0 - lb) * sigmoid(pf_ref[g, at, :])
            adj = loc_ref[g, at, :] + s
            loc_ref[g, at, :] = adj
            cum_ref[g, at, :] = q
            s = f * adj
            q = q * f
        last = CHUNKS - 1
        a = q[last : last + 1]
        b = s[last : last + 1]
        for c in range(CHUNKS - 2, -1, -1):
            b = q[c : c + 1] * b + s[c : c + 1]
            a = a * q[c : c + 1]
        put_total(tot_ref, g, a, b, refs[:-6])


def back_local(g0, g1, out_proj, pg, pf, state, gain, lower, prior=(), after=()):
    rows, width = pg.shape[1], g0.shape[1]
    chans = out_proj.shape[0]
    tile = tile_of(chans, 128)
    piece = ((2, rows, tile), lambda c: (0, 0, c))
    row = ((1, tile), lambda c: (0, c))
    shape = (2, rows, chans)
    before, total = total_blocks(prior, chans, tile)
    return call(
        functools.partial(back_local_kernel, width),
        "back_local",
        (chans // tile,),
        [
            fixed(g0),
            fixed(g1),
            (out_proj, (tile, width), lambda c: (c, 0)),
            (pg, *piece),
            (pf, *piece),
            (state, *piece),
            (gain, *row),
            (lower, *row),
            *before,
        ],
        [
            (shape, BF, *piece),
            (shape, BF, *piece),
            (shape, F32, *piece),
            (shape, F32, *piece),
            total,
            ((1, chans), F32, *row),
        ],
        flops=4 * rows * width * chans,
        after=after,
    )


def back_mix_kernel(
    loc_ref, cum_ref, state_ref, pi_ref, pf_ref, gpg_ref, carry_ref, prior_ref, lb_ref, w,
    both_ref, b0, b1, term_ref,
):
    _, rows, chans = loc_ref.shape
    steps = rows // CHUNKS
    lb = lb_ref[...]
    rest = 1.0 - lb
    cin = carry_ref[0]
    term = jnp.zeros((1, loc_ref.shape[2]), F32)
    top = lax.broadcasted_iota(jnp.int32, (steps, loc_ref.shape[2]), 0) == 0
    for c in range(CHUNKS - 1, -1, -1):
        at = pl.ds(c * steps, steps)
        adj = loc_ref[0, at, :] + cum_ref[0, at, :] * cin
        pi = pi_ref[0, at, :]
        sig = sigmoid(pf_ref[0, at, :])
        cin = (lb + rest * sig[0:1]) * adj[0:1]
        st = state_ref[0, at, :]
        before = prior_ref[0] if c == 0 else state_ref[0, pl.ds(c * steps - 1, 1), :]
        prev = jnp.where(top, before, pltpu.roll(st, 1, 0))
        sig_in = sigmoid(pi)
        total = adj * (prev - pi * sig_in)
        left = 1.0 - sig
        slope = sig_in * (1.0 + pi * (1.0 - sig_in))
        both_ref[0, at, :chans] = (adj * (rest * left) * slope).astype(BF)
        both_ref[0, at, chans:] = (total * rest * sig * left).astype(BF)
        term = term + jnp.sum(total * left, axis=0, keepdims=True)
    term_ref[0] = term
    out = (
        dot_last(both_ref[0, :, :chans], w[0])
        + dot_last(both_ref[0, :, chans:], w[1])
        + dot_last(gpg_ref[0], w[2])
    ).astype(BF)
    first = pl.program_id(0) == 0

    @pl.when(first)
    def _():
        b0[...] = out

    @pl.when(jnp.logical_not(first))
    def _():
        b1[...] = out


def back_mix(loc, cum, state, pi, pf, gpg, carry, prior, shift, lower, in_proj, after=()):
    _, rows, chans = state.shape
    width = in_proj.shape[1]
    piece = ((1, rows, chans), lambda g: (g, 0, 0))
    per = ((1, 1, chans), lambda g: (g, 0, 0))
    moved = ((1, 1, chans), lambda g: (g + shift, 0, 0))
    whole = ((rows, width), BF, (rows, width), lambda g: (0, 0))
    return call(
        back_mix_kernel,
        "back_mix",
        (2,),
        [(v, *piece) for v in (loc, cum, state, pi, pf, gpg)]
        + [(carry, *moved), (prior, *moved), fixed(lower), fixed(in_proj)],
        [
            ((2, rows, 2 * chans), BF, (1, rows, 2 * chans), lambda g: (g, 0, 0)),
            whole,
            whole,
            ((2, 1, chans), F32, *per),
        ],
        flops=12 * rows * width * chans,
        after=after,
    )


def total_product(near_count, refs):
    lefts, (near, far) = refs[:-2], refs[-2:]
    return dot_first(stack(*lefts[:near_count]), near[...]) + dot_first(
        stack(*lefts[near_count:]), far[...]
    )


def product_kernel(near_count, me, *refs):
    refs[-1][...] = total_product(near_count, refs[:-1]).astype(BF)


def product_add_kernel(near_count, half, me, *refs):
    got, send, keep = refs[-3:]
    total = (total_product(near_count, refs[:-3]) + got[...].astype(F32)).astype(BF)
    early = pl.program_id(0) < half

    @pl.when(early)
    def _():
        send[...] = total

    @pl.when(jnp.logical_not(early))
    def _():
        keep[...] = total


def product(me, lefts, near, far, bits, size, got=None, after=(), more=0):
    levels = len(bits)
    count = 1 << (levels - 1)
    base = 0 if got is None else count
    top = 2 * count - 1 - base
    units = near.shape[1]
    near_count = len(lefts[0])
    lefts = [*lefts[0], *lefts[1]]

    def place(j, me):
        turned = top - j
        block = me[0]
        for n, bit in enumerate(bits):
            block = block ^ (((turned >> (levels - 1 - n)) & 1) * bit)
        return (0, block)

    if size % 128:
        def ordered(x, rows):
            parts = [
                lax.dynamic_slice_in_dim(x[:rows], place(j, me)[1] * size, size, 1)
                for j in range(count)
            ]
            return jnp.concatenate(parts, axis=1), rows

        lefts = [ordered(*x) for x in lefts]
        count, size = count * size // 128, 128
        position = lambda j, me: (0, j)
    else:
        position = place
    inputs = [(x, (rows, size), position) for x, rows in lefts]
    inputs += [fixed(near), fixed(far)]
    flops = 0
    if got is None:
        out = ((count * size + more, units), BF, (size, units), lambda j, me: (j, 0))
        return call(
            functools.partial(product_kernel, near_count),
            "product", (count,), inputs, [out], flops, after, blocks=me,
        )
    half = count // 2
    inputs.append((got, (size, units), lambda j, me: (j, 0)))
    shape = (half * size, units)
    send = (shape, BF, (size, units), lambda j, me: (jnp.minimum(j, half - 1), 0))
    keep = (shape, BF, (size, units), lambda j, me: (jnp.maximum(j - half, 0), 0))
    return call(
        functools.partial(product_add_kernel, near_count, half),
        "product_add",
        (count,),
        inputs,
        [send, keep],
        flops,
        after,
        blocks=me,
    )


def halve_kernel(half, one, two, send, keep):
    total = (one[...].astype(F32) + two[...].astype(F32)).astype(BF)
    early = pl.program_id(0) < half

    @pl.when(early)
    def _():
        send[...] = total

    @pl.when(jnp.logical_not(early))
    def _():
        keep[...] = total


def halve(one, two, size, after=()):
    count = one.shape[0] // size
    half = count // 2
    units = one.shape[1]
    block = ((size, units), lambda j: (j, 0))
    shape = (half * size, units)
    return call(
        functools.partial(halve_kernel, half),
        "halve",
        (count,),
        [(one, *block), (two, *block)],
        [
            (shape, BF, (size, units), lambda j: (jnp.minimum(j, half - 1), 0)),
            (shape, BF, (size, units), lambda j: (jnp.maximum(j - half, 0), 0)),
        ],
        after=after,
    )


def finish_kernel(turned, one, two, *refs):
    out = refs[-1]
    total = one[...].astype(F32) + two[...].astype(F32)
    if turned:
        out[...] = total.T
    else:
        parts, _, units = out.shape
        for part in range(parts):
            out[part] = total[:, part * units : (part + 1) * units]


def finish(one, two, turned=False, slot=0, parts=1, slots=1, into=None, after=()):
    rows, units = one.shape
    if turned:
        tile = 128 if rows % 128 == 0 else rows
        shape = (units, rows)
        out = pl.BlockSpec((units, tile), lambda n: (0, n))
    else:
        tile = 64 if rows % 64 == 0 else rows
        shape = (slots, rows, units // parts)
        out = pl.BlockSpec((parts, tile, units // parts), lambda n: (slot // parts, n, 0))
    block = pl.BlockSpec((tile, units), lambda n: (n, 0))
    held = [] if into is None else [into]
    waits = [*held, *after]
    count = len(waits)
    return pl.pallas_call(
        lambda one, two, *refs: finish_kernel(turned, one, two, *refs[count:]),
        grid=(rows // tile,),
        in_specs=[block, block] + [ANYWHERE] * count,
        out_specs=out,
        out_shape=sds(shape),
        input_output_aliases={2: 0} if held else {},
        compiler_params=pltpu.CompilerParams(vmem_limit_bytes=VMEM_LIMIT),
        cost_estimate=pl.CostEstimate(flops=0, bytes_accessed=0, transcendentals=0),
        name="finish",
    )(one, two, *waits)


def row_call(kernel, name, arrays, gains, outputs, sums=0, after=(), most=64, more=()):
    rows, width = arrays[0].shape[-2:]
    tile = most if rows % most == 0 else rows

    def block(shape):
        lead = len(shape) - 2
        return (*shape[:-2], tile, shape[-1]), lambda r: (*(0,) * lead, r, 0)

    inputs = [(a, *block(a.shape)) for a in arrays] + [fixed(g) for g in gains]
    results = [(shape, dtype, *block(shape)) for shape, dtype in outputs]
    results += [((1, width), F32, (1, width), lambda r: (0, 0))] * sums + list(more)
    return call(kernel, name, (rows // tile,), inputs, results, after=after)


def add_to(ref, term):
    first = pl.program_id(0) == 0

    @pl.when(first)
    def _():
        ref[...] = term

    @pl.when(jnp.logical_not(first))
    def _():
        ref[...] += term


def first_norm_kernel(x_ref, gain_ref, out):
    x = x_ref[...].astype(F32)
    out[...] = (x * rms_scale(x) * gain_ref[...]).astype(BF)


def plus_kernel(one, two, out):
    out[...] = (one[...].astype(F32) + two[...].astype(F32)).astype(BF)


def plus(one, two, after=()):
    return row_call(plus_kernel, "plus", [one, two], [], [(one.shape, BF)], after=after)


def join_kernel(one, two, top, bottom):
    half = bottom.shape[0]
    rows = 2 * half
    for out, at in ((top, 0), (bottom, half)):
        part = slice(at, at + half)
        out[:half] = (one[part].astype(F32) + two[part].astype(F32)).astype(BF)
    extra = one[rows:].astype(F32) + two[rows:].astype(F32)
    top[half:] = in_two(jnp.broadcast_to(extra[0:1] + extra[1:2], extra.shape))


def join(one, two, after=()):
    rows, width = one.shape[0] - EXTRA, one.shape[1]
    shapes = [(rows // 2 + EXTRA, width), (rows // 2, width)]
    return call(
        join_kernel, "join", (1,), [fixed(one), fixed(two)],
        [(s, BF, s, lambda i: (0, 0)) for s in shapes], after=after,
    )


def middle_kernel(half, x, own, core, hop, own_more, core_more, hop_more, gain, *refs):
    branch_ref, middle_ref, scale_ref, full, out = refs[-5:]
    rows, width = x.shape
    more = own_more[...].astype(F32) + core_more[...].astype(F32) + hop_more[...].astype(F32)
    squares = (more[0:1] + more[1:2])[:, half * rows : (half + 1) * rows]
    scale = lax.rsqrt(upright(squares) / width + EPS)
    branch = own[...].astype(F32) + core[...].astype(F32) + hop[...].astype(F32)
    middle = x[...].astype(F32) + branch * scale[:, :1]
    branch_ref[...] = branch
    scale_ref[...] = scale
    middle_ref[...] = middle
    low = (middle * rms_scale(middle) * gain[...]).astype(BF)
    full[...] = low
    out[...] = low


def middle_half(half, x, own, core, hop, top, gain, begun=(), after=()):
    total, width = x.shape
    rows = total // 2
    part = pl.BlockSpec((rows, width), lambda i: (half, 0))
    alone = pl.BlockSpec((rows, width), lambda i: (0, 0))
    more = pl.BlockSpec((EXTRA, width), lambda i: (total // EXTRA, 0))
    top_more = pl.BlockSpec((EXTRA, width), lambda i: (rows // EXTRA, 0))
    waits = [*begun, *after]
    return pl.pallas_call(
        functools.partial(middle_kernel, half),
        grid=(1,),
        in_specs=[part, part, part, alone, more, more, top_more, pl.BlockSpec((1, width), lambda i: (0, 0))]
        + [ANYWHERE] * len(waits),
        out_specs=[part, part, pl.BlockSpec((rows, 128), lambda i: (half, 0)), part, alone],
        out_shape=[
            sds((total, width)), sds((total, width)), sds((total, 128)), sds((total, width), BF),
            sds((rows + (16 if half == 0 else 0), width), BF),
        ],
        input_output_aliases={8 + n: n for n in range(len(begun))},
        compiler_params=pltpu.CompilerParams(vmem_limit_bytes=VMEM_LIMIT),
        cost_estimate=pl.CostEstimate(flops=0, bytes_accessed=0, transcendentals=0),
        name="middle",
    )(x, own, core, hop, own, core, top, gain, *waits)


def turn_kernel(up, own, core, hop, middle_ref, branch, scale_ref, gain, grad_ref, term, out):
    tile = up.shape[0]
    step = pl.program_id(0)
    rows = out.shape[0] - EXTRA
    grad = own[...].astype(F32) + core[...].astype(F32) + hop[...].astype(F32)
    middle = middle_ref[...]
    scale = rms_scale(middle)
    total = up[...].astype(F32) + norm_back(grad, middle, scale, gain[...])
    low = total.astype(BF)
    grad_ref[...] = total
    out[pl.ds(pl.multiple_of(step * tile, tile), tile), :] = low
    inner = wide(jnp.sum(low.astype(F32) * branch[...], axis=-1, keepdims=True)).T[:EXTRA]
    outer = scale_ref[...].T[:EXTRA]
    high_outer = outer.astype(BF).astype(F32)
    high_inner = inner.astype(BF).astype(F32)
    which = lax.broadcasted_iota(jnp.int32, inner.shape, 0)
    both = jnp.where(which < 2, outer, inner)
    high = jnp.where(which < 2, high_outer, high_inner)
    extra = jnp.where(which % 2 == 0, high, both - high)

    @pl.when(step == 0)
    def _():
        out[rows:, :] = jnp.zeros((EXTRA, out.shape[1]), BF)

    out[rows:, pl.ds(pl.multiple_of(step * tile, tile), tile)] = extra.astype(BF)
    add_to(term, jnp.sum(grad * middle * scale, axis=0, keepdims=True))


def turn(up, own, core, hop, middle, branch, scale, gain, after=()):
    rows, width = up.shape
    shape = (rows + EXTRA, width)
    return row_call(
        turn_kernel, "turn", [up, own, core, hop, middle, branch, scale], [gain],
        [(up.shape, F32)], sums=1, after=after, most=128,
        more=[(shape, BF, shape, lambda r: (0, 0))],
    )


def last_kernel(x_ref, own, core, hop, grad_middle, gain, out, term):
    grad = own[...].astype(F32) + core[...].astype(F32) + hop[...].astype(F32)
    x = x_ref[...].astype(F32)
    scale = rms_scale(x)
    out[...] = grad_middle[...] + norm_back(grad, x, scale, gain[...])
    add_to(term, jnp.sum(grad * x * scale, axis=0, keepdims=True))


def result_kernel(middle, own, core, hop, out):
    out[...] = (
        middle[...] + (own[...].astype(F32) + core[...].astype(F32) + hop[...].astype(F32))
    ).astype(BF)


def in_order(me, total, other):
    odd = (me[0] % 2) == 1
    return (
        odd,
        jnp.where(odd, other[0], total[0]),
        jnp.where(odd, other[1], total[1]),
        jnp.where(odd, total[0], other[0]),
        jnp.where(odd, total[1], other[1]),
    )


def pair_kernel(reverse, me, total, other, pair):
    odd, low_a, low_b, high_a, high_b = in_order(me, total, other)
    pair[0] = low_a * high_a
    pair[1] = low_a * high_b + low_b if reverse else high_a * low_b + high_b


def enter_kernel(reverse, me, total, other, *refs):
    odd, low_a, low_b, high_a, high_b = in_order(me, total, other)
    enter = jnp.zeros_like(low_a)
    for got in reversed(refs[:-1]):
        enter = got[0] * enter + got[1]
    if reverse:
        enter = jnp.where(odd, enter, high_a * enter + high_b)
    else:
        enter = jnp.where(odd, low_a * enter + low_b, enter)
    for g in range(enter.shape[0]):
        refs[-1][g] = enter[g : g + 1]


def chain(me, total, reverse, between=None, beside=None):
    size = lax.axis_size("seq")
    _, groups, chans = total.shape
    other = swap(total, "seq", 1)
    got = between() if between else ()
    whole = (total.shape, F32, total.shape, lambda i, me: (0, 0, 0))
    pair = call(
        functools.partial(pair_kernel, reverse), "pair", (1,), [fixed(total), fixed(other)], [whole],
        after=got, blocks=me,
    )
    sign = -1 if reverse else 1
    reached = [shift(pair, "seq", 2 * sign * d) for d in range(1, size // 2)]
    shape = (groups, 1, chans)
    got = beside(pair) if beside else ()
    return call(
        functools.partial(enter_kernel, reverse), "enter", (1,),
        [fixed(total), fixed(other), *[fixed(r) for r in reached]],
        [(shape, F32, shape, lambda i, me: (0, 0, 0))],
        after=got,
        blocks=me,
    )


def seq_bits():
    size = lax.axis_size("seq")
    bits = []
    bit = 1
    while bit < size:
        bits.append(bit)
        bit *= 2
    return bits


class Weight:
    def __init__(self, me, lefts, near, far, bits, size):
        self.me, self.lefts, self.near, self.far = me, lefts, near, far
        self.bits, self.size, self.level = bits, size, 0

    def begin(self, *earlier, more=0):
        self.send = product(
            self.me, self.lefts, self.near, self.far, self.bits, self.size, after=earlier, more=more
        )
        return self.send

    def go(self, *earlier):
        send = after(self.send, *earlier) if earlier else self.send
        self.got = swap(send, "seq", self.bits[self.level])
        self.level += 1

    def step(self, *earlier):
        if self.level == 1:
            self.send, self.keep = product(
                self.me, self.lefts, self.near, self.far, self.bits, self.size, self.got, after=earlier
            )
        else:
            self.send, self.keep = halve(self.keep, self.got, self.size, after=earlier)
        return self.send

    def last(self):
        return self.level == len(self.bits)


def gain_terms(norm1_term, norm2_term, mixer_term, bound_n, bound_f):
    wt = lax.axis_index("wt")
    span = norm1_term.shape[1] // lax.axis_size("wt")
    norm_terms = jnp.concatenate([norm1_term, norm2_term])

    def part(j):
        return lax.dynamic_slice_in_dim(norm_terms, (wt ^ j) * span, span, 1)

    norms = part(0)
    for j in (1, 2, 3):
        norms = norms + swap(part(j), "wt", j)
    bound_term = jnp.sum(bound_n, axis=(0, 1)) + jnp.sum(bound_f, axis=(0, 1))
    return jnp.stack([norms[0], mixer_term[0], norms[1], bound_term])


GATE_AT, LOWER_AT, UP_AT, LOWER_BITS = "beside", "beside", "pair", "m"
ORDER = (
    ("-p", "-n", "gs", "bb", "us", "-l", "ob", "ls", "ab", "-r", "us", "gf", "bs")
    + ("os", "as", "bs", "lf", "uf", "as", "os", "-1", "bf", "af", "-2", "-3", "of")
)


def on_device(
    tokens,
    in_proj,
    out_proj,
    gate_up,
    down,
    norm1_gain,
    mixer_gain,
    norm2_gain,
    lower_bound,
    cotangent,
):
    width = in_proj.shape[1]
    chans = in_proj.shape[2]
    x = tokens[0]
    g0 = cotangent[0]
    rows = x.shape[0]
    bits = seq_bits()
    y_first = bits
    mixed_order = {"m": bits[1:2] + bits[:1] + bits[2:], "z": bits[1:] + bits[:1], "y": bits}[LOWER_BITS]
    block = width // lax.axis_size("seq")
    me = lax.axis_index("seq").reshape(1).astype(jnp.int32)

    offset = lax.axis_index("wt") * chans
    lower_use = lax.dynamic_slice_in_dim(lower_bound, offset, chans)[None]
    mixer_use = lax.dynamic_slice_in_dim(mixer_gain, offset, chans)[None]
    gain_one, gain_two = norm1_gain[None], norm2_gain[None]

    n0 = row_call(first_norm_kernel, "first_norm", [x], [gain_one], [(x.shape, BF)])
    hop = swap(n0, "wt", 2)
    n1 = swap(n0, "wt", 1)
    g1 = swap(g0, "wt", 1)
    grad_hop = swap(after(g0, n0), "wt", 2)
    pi_n, pf_n, pg_n, loc_n, cum_n, tot = project(n0, n1, in_proj, lower_use)
    gh_n = hidden_grad(g0, g1, down, after=(tot,))
    n2 = after(hop, gh_n)
    n3 = swap(n2, "wt", 1)
    pi_f, pf_f, pg_f, loc_f, cum_f, tot = project(n2, n3, in_proj, lower_use, (tot,))
    enter = chain(me, tot, False)
    state_f, bf0, bf1 = mix(loc_f, cum_f, pg_f, enter, 2, mixer_use, out_proj)
    g2 = after(grad_hop, bf0)
    g3 = swap(g2, "wt", 1)
    state_n, bn0, bn1 = mix(loc_n, cum_n, pg_n, enter, 0, mixer_use, out_proj, after=(bf0,))
    across = join(bf0, swap(bf1, "wt", 1), after=(bn0,))
    hops = [swap(part, "wt", 2) for part in across]
    core = swap(bn1, "wt", 1)
    gh_f = hidden_grad(g2, g3, down, after=(across[1],))
    *begun, half0 = middle_half(0, x, bn0, core, hops[0], hops[0], gain_two, after=(gh_f,))
    branch, middle, scale_two, t0, half1 = middle_half(
        1, x, bn0, core, hops[1], hops[0], gain_two, begun
    )

    hops = [swap(half, "wt", 2) for half in (half0, half1)]
    t1 = [swap(half, "wt", 1) for half in (half0, half1)]
    hid_n, gg_n, gu_n = feed((t0, *t1), gate_up, gh_n)
    kn0, kn1 = feed_back(gg_n, gu_n, gate_up)
    core = swap(kn1, "wt", 1)
    t2 = [after(hop, kn0) for hop in hops]
    t3 = [swap(half, "wt", 1) for half in t2]
    hid_f, gg_f, gu_f = feed((*t2, *t3), gate_up, gh_f)

    def pieces(*arrays):
        return [(v, min(rows, v.shape[0]) // 128 * 128) for v in arrays]

    twos = (pieces(t0, *t1), pieces(*t2, *t3))
    gate = Weight(me, twos, gg_n, gg_f, y_first, block)
    up = Weight(me, twos, gu_n, gu_f, y_first, block)
    lower = Weight(me, (pieces(g0, g1), pieces(g2, g3)), hid_n, hid_f, mixed_order, block)
    kf0, kf1 = feed_back(gg_f, gu_f, gate_up)
    gate.begin(kf0, more=128)
    gate.go()
    across = plus(kf0, swap(kf1, "wt", 1), after=(gate.send,))
    hop = swap(across, "wt", 2)
    lower.begin(across, more=128)
    lower.go()
    up.begin(lower.send, across, more=0)
    ff0, ff1 = feed_out(hid_f, down, after=(up.send,))
    grad_middle, norm2_term, b0 = turn(
        g0, kn0, core, hop, middle, branch, scale_two, gain_two, after=(ff0,)
    )

    hop = swap(b0, "wt", 2)
    b1 = swap(b0, "wt", 1)
    mixed_n, gpg_n, bloc_n, bcum_n, btot, mixer_n = back_local(
        b0, b1, out_proj, pg_n, pf_n, state_n, mixer_use, lower_use
    )
    ffn_across = plus(ff0, swap(ff1, "wt", 1), after=(btot,))
    fn0, fn1 = feed_out(hid_n, down, after=(ffn_across,))
    ffn_core = swap(fn1, "wt", 1)
    b2 = after(hop, fn0)
    b3 = swap(b2, "wt", 1)
    early = (gate.step(b2),) if GATE_AT == "before" else ()
    mixed_f, gpg_f, bloc_f, bcum_f, btot, mixer_f = back_local(
        b2, b3, out_proj, pg_f, pf_f, state_f, mixer_use, lower_use, (btot,), after=early
    )

    def beside(pair):
        if UP_AT == "pair":
            up.go(pair)
        for one, place in ((gate, GATE_AT), (lower, LOWER_AT)):
            if place == "beside":
                pair = one.step(pair)
        return (pair,)

    leave = chain(me, btot, True, None, beside)
    if UP_AT == "leave":
        up.go(leave)
    if GATE_AT == "after":
        gate.step(leave)
        gate.go()
    else:
        gate.go(leave)
    if LOWER_AT == "beside":
        if LOWER_BITS == "z":
            lower.go(leave)
        else:
            lower.go()
    both_f, df0, df1, bound_f = back_mix(
        bloc_f, bcum_f, state_f, pi_f, pf_f, gpg_f, leave, enter, 2, lower_use, in_proj
    )

    def flat(values):
        return values.reshape(2 * rows, values.shape[2])

    normals = (pieces(n0, n1), pieces(n2, n3))
    last_in = Weight(me, normals, flat(gpg_n), flat(gpg_f), y_first, block)
    out = Weight(me, (pieces(b0, b1), pieces(b2, b3)), flat(mixed_n), flat(mixed_f), y_first, block)
    both_n, dn0, dn1, bound_n = None, None, None, None
    token = df0
    weights = {"g": gate, "u": up, "l": lower, "a": last_in, "o": out}
    rounds = list(bits)
    gate_up_grad = in_grad = None
    for kind, act in ORDER:
        if kind in weights:
            one = weights[kind]
            if act == "b":
                token = one.begin(token)
                one.go()
            elif act == "s":
                token = one.step(token)
                one.go()
                while one.level > 2 and not one.last():
                    token = one.step(token)
                    one.go()
            elif kind in "gu":
                slot = "gu".index(kind)
                token = gate_up_grad = finish(
                    one.keep, one.got, slot=slot, slots=2, into=gate_up_grad,
                    after=() if token is gate_up_grad else (token,),
                )
            elif kind == "b":
                token = in_grad = finish(
                    one.keep, one.got, parts=2, slots=3, into=in_grad,
                    after=() if token is in_grad else (token,),
                )
            elif kind == "a":
                token = in_grad = finish(
                    one.keep, one.got, slot=2, slots=3, into=in_grad,
                    after=() if token is in_grad else (token,),
                )
            elif kind == "l":
                token = down_grad = finish(one.keep, one.got, True, after=(token,))
            else:
                token = out_grad = finish(one.keep, one.got, True, after=(token,))
        elif act == "p":
            token = plus(df0, swap(df1, "wt", 1), after=(token,))
            hop = swap(token, "wt", 2)
        elif act == "n":
            both_n, dn0, dn1, bound_n = back_mix(
                bloc_n, bcum_n, state_n, pi_n, pf_n, gpg_n, leave, enter, 0, lower_use, in_proj,
                after=(token,),
            )
            token = dn0
            core = swap(dn1, "wt", 1)
            weights["b"] = Weight(me, normals, flat(both_n), flat(both_f), y_first, block)
        elif act == "l":
            grad_inputs, norm1_term = row_call(
                last_kernel,
                "last",
                [x, dn0, core, hop, grad_middle],
                [gain_one],
                [(x.shape, F32)],
                sums=1,
                after=(token,),
            )
            token = grad_inputs
            ffn_hop = swap(after(ffn_across, token), "wt", 2)
            gains = gain_terms(norm1_term, norm2_term, mixer_n + mixer_f, bound_n, bound_f)
        elif act == "r":
            token = result = row_call(
                result_kernel, "result", [middle, fn0, ffn_core, ffn_hop], [], [(x.shape, BF)],
                after=(token,),
            )
        elif act in "123":
            for _ in range(len(rounds) if act == "3" else 1):
                gains = gains + after(swap(gains, "seq", rounds.pop(0)), token)

    return (
        result[None],
        grad_inputs[None],
        in_grad,
        out_grad,
        gate_up_grad,
        down_grad,
        gains[0],
        gains[1],
        gains[2],
        gains[3],
    )


def solution(mesh):
    placed = (
        P("wt", "seq", None),
        P(None, None, "wt"),
        P("wt", None),
        P(None, None, "wt"),
        P("wt", None),
        P(),
        P(),
        P(),
        P(),
        P("wt", "seq", None),
    )
    return jax.shard_map(
        on_device,
        mesh=mesh,
        in_specs=placed,
        out_specs=(
            P("wt", "seq", None),
            P("wt", "seq", None),
            P(None, "seq", "wt"),
            P("wt", "seq"),
            P(None, "seq", "wt"),
            P("wt", "seq"),
            P("wt"),
            P("wt"),
            P("wt"),
            P("wt"),
        ),
        check_vma=False,
    )
```

```python
import functools

import jax
import jax.numpy as jnp
from jax import lax
from jax.experimental import pallas as pl
from jax.experimental.pallas import tpu as pltpu
from jax.sharding import PartitionSpec as P

EPS = 1e-06
BF = jnp.bfloat16
F32 = jnp.float32
CHUNKS = 8


def swap(values, axis, bit):
    size = lax.axis_size(axis)
    return lax.ppermute(values, axis, [(i, i ^ bit) for i in range(size)])


def shift(values, axis, step):
    size = lax.axis_size(axis)
    pairs = [(i, i + step) for i in range(size) if 0 <= i + step < size]
    return lax.ppermute(values, axis, pairs)


def rms_scale(values):
    return lax.rsqrt(jnp.mean(values * values, axis=-1, keepdims=True) + EPS)


def norm_back(grad_normed, values, scale, weight):
    weighted = grad_normed * weight
    return scale * weighted - values * (scale * scale * scale) * jnp.mean(
        weighted * values, axis=-1, keepdims=True
    )


def sigmoid(v):
    return 0.5 * jnp.tanh(0.5 * v) + 0.5


ANYWHERE = pl.BlockSpec(memory_space=pl.ANY)
EXTRA = 16
VMEM_LIMIT = 63 * 1024 * 1024


def sds(shape, dtype=F32):
    return jax.ShapeDtypeStruct(shape, dtype)


def call(kernel, name, grid, inputs, outputs, flops=0, after=(), scratch=(), blocks=None):
    in_specs = [pl.BlockSpec(block, index) for _, block, index in inputs]
    in_specs += [ANYWHERE] * len(after)
    out_specs = [pl.BlockSpec(block, index) for _, _, block, index in outputs]
    count = len(inputs)
    skip = len(after)
    lead = 0 if blocks is None else 1

    def body(*refs):
        kernel(*refs[: lead + count], *refs[lead + count + skip :])

    settings = dict(
        out_shape=[sds(shape, dtype) for shape, dtype, _, _ in outputs],
        compiler_params=pltpu.CompilerParams(vmem_limit_bytes=VMEM_LIMIT),
        cost_estimate=pl.CostEstimate(flops=0, bytes_accessed=0, transcendentals=0),
        name=name,
    )
    operands = [a for a, _, _ in inputs] + list(after)
    if blocks is None:
        got = pl.pallas_call(
            body, grid=grid, in_specs=in_specs, out_specs=out_specs, scratch_shapes=list(scratch), **settings
        )(*operands)
    else:
        spec = pltpu.PrefetchScalarGridSpec(
            num_scalar_prefetch=1,
            grid=grid,
            in_specs=in_specs,
            out_specs=out_specs,
            scratch_shapes=list(scratch),
        )
        got = pl.pallas_call(body, grid_spec=spec, **settings)(blocks, *operands)
    return got[0] if len(outputs) == 1 else got


def fixed(array):
    zeros = (0,) * array.ndim
    return (array, array.shape, lambda *_: zeros)


def hold_kernel(*refs):
    pass


def after(value, *earlier):
    return pl.pallas_call(
        hold_kernel,
        in_specs=[ANYWHERE] * (1 + len(earlier)),
        out_specs=ANYWHERE,
        out_shape=jax.ShapeDtypeStruct(value.shape, value.dtype),
        input_output_aliases={0: 0},
        cost_estimate=pl.CostEstimate(flops=0, bytes_accessed=0, transcendentals=0),
        name="hold",
    )(value, *earlier)


def dot(left, right):
    return jnp.dot(left, right, preferred_element_type=F32)


def dot_last(left, right):
    return lax.dot_general(left, right, (((1,), (1,)), ((), ())), preferred_element_type=F32)


def dot_first(left, right):
    return lax.dot_general(left, right, (((0,), (0,)), ((), ())), preferred_element_type=F32)


def wide(column):
    return jnp.broadcast_to(column, (column.shape[0], 128))


def in_two(values):
    which = lax.broadcasted_iota(jnp.int32, values.shape, 0)
    high = values.astype(BF).astype(F32)
    return jnp.where(which == 0, high, jnp.where(which == 1, values - high, 0.0)).astype(BF)


def upright(row):
    return jnp.broadcast_to(row, (128, row.shape[1])).T


def stack(*refs):
    return jnp.concatenate([r[...] for r in refs], axis=0)


def tile_of(size, most):
    best = size
    for tile in range(128, most + 1, 128):
        if size % tile == 0:
            best = tile
    return best


def project_kernel(x0, x1, w, lb_ref, *refs):
    pi_ref, pf_ref, pg_ref, loc_ref, cum_ref, tot_ref = refs[-6:]
    groups, rows, tile = loc_ref.shape
    steps = rows // CHUNKS
    y = dot(stack(x0, x1), jnp.concatenate([w[0], w[1], w[2]], axis=1))
    lb = lb_ref[...]
    for g in range(groups):
        part = y[g * rows : (g + 1) * rows]
        pi_ref[g] = part[:, :tile]
        pf_ref[g] = part[:, tile : 2 * tile]
        pg_ref[g] = part[:, 2 * tile :]
    for g in range(groups):
        s = jnp.zeros((CHUNKS, tile), F32)
        p = jnp.ones_like(s)
        for t in range(steps):
            at = pl.ds(t, CHUNKS, stride=steps)
            pi = pi_ref[g, at, :]
            sig = sigmoid(pf_ref[g, at, :])
            f = lb + (1.0 - lb) * sig
            s = f * s + pi * sigmoid(pi) * ((1.0 - lb) * (1.0 - sig))
            p = p * f
            loc_ref[g, at, :] = s
            cum_ref[g, at, :] = p
        a = p[0:1]
        b = s[0:1]
        for c in range(1, CHUNKS):
            b = p[c : c + 1] * b + s[c : c + 1]
            a = a * p[c : c + 1]
        put_total(tot_ref, g, a, b, refs[:-6])


def put_total(tot_ref, g, a, b, prior):
    at = g
    if prior:
        at = g + prior[0].shape[1]
        if g == 0:
            tot_ref[:, : prior[0].shape[1], :] = prior[0][...]
    tot_ref[0, at : at + 1, :] = a
    tot_ref[1, at : at + 1, :] = b


def total_blocks(prior, chans, tile):
    count = 2 + sum(p.shape[1] for p in prior)
    inputs = [(p, (2, p.shape[1], tile), lambda c: (0, 0, c)) for p in prior]
    return inputs, ((2, count, chans), F32, (2, count, tile), lambda c: (0, 0, c))


def project(x0, x1, in_proj, lower, prior=(), after=()):
    rows, width = x0.shape
    chans = in_proj.shape[2]
    tile = tile_of(chans, 128)
    full = ((2, rows, chans), F32, (2, rows, tile), lambda c: (0, 0, c))
    before, total = total_blocks(prior, chans, tile)
    return call(
        project_kernel,
        "project",
        (chans // tile,),
        [
            fixed(x0),
            fixed(x1),
            (in_proj, (3, width, tile), lambda c: (0, 0, c)),
            (lower, (1, tile), lambda c: (0, c)),
            *before,
        ],
        [full] * 5 + [total],
        flops=12 * rows * width * chans,
        after=after,
    )


def mix_kernel(loc_ref, cum_ref, pg_ref, carry_ref, gain_ref, w_ref, state_ref, b0, b1, mix_ref, sq_ref):
    rows = loc_ref.shape[1]
    steps = rows // CHUNKS
    gain = gain_ref[...]
    cin = carry_ref[0]
    for c in range(CHUNKS):
        at = pl.ds(c * steps, steps)
        st = loc_ref[0, at, :] + cum_ref[0, at, :] * cin
        cin = st[steps - 1 : steps]
        pg = pg_ref[0, at, :]
        state_ref[0, at, :] = st
        mix_ref[at, :] = (st * gain * (pg * sigmoid(pg))).astype(BF)
        sq_ref[at, :] = wide(jnp.sum(st * st, axis=-1, keepdims=True))
    out = dot(mix_ref[...], w_ref[...]).astype(BF)
    first = pl.program_id(0) == 0

    def put(ref):
        ref[:rows] = out
        ref[rows:] = jnp.zeros((EXTRA, out.shape[1]), BF)
        ref[rows:, :rows] = in_two(sq_ref[...].T[:EXTRA])

    @pl.when(first)
    def _():
        put(b0)

    @pl.when(jnp.logical_not(first))
    def _():
        put(b1)


def mix(loc, cum, pg, carry, shift, gain, out_proj, after=()):
    _, rows, chans = loc.shape
    width = out_proj.shape[1]
    piece = ((1, rows, chans), lambda g: (g, 0, 0))
    shape = (rows + EXTRA, width)
    whole = (shape, BF, shape, lambda g: (0, 0))
    return call(
        mix_kernel,
        "mix",
        (2,),
        [
            (loc, *piece),
            (cum, *piece),
            (pg, *piece),
            (carry, (1, 1, chans), lambda g: (g + shift, 0, 0)),
            fixed(gain),
            fixed(out_proj),
        ],
        [
            (loc.shape, F32, *piece),
            whole,
            whole,
        ],
        flops=4 * rows * chans * width,
        after=after,
        scratch=[pltpu.VMEM((rows, chans), BF), pltpu.VMEM((rows, 128), F32)],
    )


def hidden_grad_kernel(g0, g1, w, out):
    out[...] = dot_last(stack(g0, g1), w[...])


def hidden_grad(g0, g1, down, after=()):
    rows, width = g0.shape
    units = down.shape[0]
    tile = min(512, units)
    return call(
        hidden_grad_kernel,
        "hidden_grad",
        (pl.cdiv(units, tile),),
        [fixed(g0), fixed(g1), (down, (tile, width), lambda n: (n, 0))],
        [((2 * rows, units), F32, (2 * rows, tile), lambda n: (0, n))],
        flops=4 * rows * width * units,
        after=after,
    )


def feed_kernel(*refs):
    w, gh_ref, hidden, gg, gu = refs[-5:]
    x = stack(*refs[:-5])
    gate = dot(x, w[0])
    up = dot(x, w[1])
    gh = gh_ref[...]
    sig = sigmoid(gate)
    act = gate * sig
    hidden[...] = (act * up).astype(BF)
    gg[...] = (gh * up * (sig * (1.0 + gate * (1.0 - sig)))).astype(BF)
    gu[...] = (gh * act).astype(BF)


def feed(pieces, gate_up, gh, after=()):
    rows, width = gh.shape[0] // 2, gate_up.shape[1]
    units = gate_up.shape[2]
    tile = min(512, units)
    col = ((2 * rows, tile), lambda n: (0, n))
    return call(
        feed_kernel,
        "feed",
        (pl.cdiv(units, tile),),
        [
            *[(x, (min(x.shape[0], rows) // 128 * 128, width), lambda n: (0, 0)) for x in pieces],
            (gate_up, (2, width, tile), lambda n: (0, 0, n)),
            (gh, *col),
        ],
        [((2 * rows, units), BF, *col)] * 3,
        flops=8 * rows * width * units,
        after=after,
    )


def feed_back_kernel(gg, gu, w, b0, b1):
    rows = b0.shape[0]
    out = (dot_last(gg[...], w[0]) + dot_last(gu[...], w[1])).astype(BF)
    b0[...] = out[:rows]
    b1[...] = out[rows:]


def feed_back(gg, gu, gate_up, after=()):
    rows = gg.shape[0] // 2
    _, width, units = gate_up.shape
    tile = tile_of(width, 512)
    part = ((rows, width), BF, (rows, tile), lambda d: (0, d))
    return call(
        feed_back_kernel,
        "feed_back",
        (width // tile,),
        [fixed(gg), fixed(gu), (gate_up, (2, tile, units), lambda d: (0, d, 0))],
        [part, part],
        flops=8 * rows * width * units,
        after=after,
    )


def feed_out_kernel(h, w, b0, b1):
    rows = b0.shape[0]
    out = dot(h[...], w[...]).astype(BF)
    b0[...] = out[:rows]
    b1[...] = out[rows:]


def feed_out(hidden, down, after=()):
    rows = hidden.shape[0] // 2
    units, width = down.shape
    tile = tile_of(width, 512)
    part = ((rows, width), BF, (rows, tile), lambda d: (0, d))
    return call(
        feed_out_kernel,
        "feed_out",
        (width // tile,),
        [fixed(hidden), (down, (units, tile), lambda d: (0, d))],
        [part, part],
        flops=4 * rows * width * units,
        after=after,
    )


def back_local_kernel(
    width, g0, g1, w, pg_ref, pf_ref, state_ref, gain_ref, lb_ref, *refs
):
    mixed_ref, gpg_ref, loc_ref, cum_ref, tot_ref, term_ref = refs[-6:]
    groups, rows, tile = loc_ref.shape
    steps = rows // CHUNKS
    gain = gain_ref[...]
    lb = lb_ref[...]
    grads = dot_last(jnp.concatenate([g0[:rows], g1[:rows]], axis=0), w[...])
    term = jnp.zeros((1, tile), F32)
    for g in range(groups):
        extra = (g1 if g else g0)[rows:, :rows].astype(F32)
        scales = upright(extra[0:1] + extra[1:2])
        inners = upright(extra[2:3] + extra[3:4])
        for c in range(CHUNKS):
            at = pl.ds(c * steps, steps)
            part = slice(c * steps, (c + 1) * steps)
            scale = scales[part, :1]
            coef = scale * scale * scale * inners[part, :1] * (1.0 / width)
            pg = pg_ref[g, at, :]
            gm = grads[g * rows + c * steps : g * rows + (c + 1) * steps]
            st = state_ref[g, at, :]
            sig = sigmoid(pg)
            act = pg * sig
            unit = st * scale
            gact = gm * act
            mixed_ref[g, at, :] = (unit * gain * act).astype(BF)
            gpg_ref[g, at, :] = (gm * gain * unit * (sig * (1.0 + pg * (1.0 - sig)))).astype(BF)
            term = term + jnp.sum(gact * unit, axis=0, keepdims=True)
            loc_ref[g, at, :] = scale * (gact * gain) - st * coef
    term_ref[...] = term
    for g in range(groups):
        s = jnp.zeros((CHUNKS, tile), F32)
        q = jnp.ones_like(s)
        for t in range(steps - 1, -1, -1):
            at = pl.ds(t, CHUNKS, stride=steps)
            f = lb + (1.0 - lb) * sigmoid(pf_ref[g, at, :])
            adj = loc_ref[g, at, :] + s
            loc_ref[g, at, :] = adj
            cum_ref[g, at, :] = q
            s = f * adj
            q = q * f
        last = CHUNKS - 1
        a = q[last : last + 1]
        b = s[last : last + 1]
        for c in range(CHUNKS - 2, -1, -1):
            b = q[c : c + 1] * b + s[c : c + 1]
            a = a * q[c : c + 1]
        put_total(tot_ref, g, a, b, refs[:-6])


def back_local(g0, g1, out_proj, pg, pf, state, gain, lower, prior=(), after=()):
    rows, width = pg.shape[1], g0.shape[1]
    chans = out_proj.shape[0]
    tile = tile_of(chans, 128)
    piece = ((2, rows, tile), lambda c: (0, 0, c))
    row = ((1, tile), lambda c: (0, c))
    shape = (2, rows, chans)
    before, total = total_blocks(prior, chans, tile)
    return call(
        functools.partial(back_local_kernel, width),
        "back_local",
        (chans // tile,),
        [
            fixed(g0),
            fixed(g1),
            (out_proj, (tile, width), lambda c: (c, 0)),
            (pg, *piece),
            (pf, *piece),
            (state, *piece),
            (gain, *row),
            (lower, *row),
            *before,
        ],
        [
            (shape, BF, *piece),
            (shape, BF, *piece),
            (shape, F32, *piece),
            (shape, F32, *piece),
            total,
            ((1, chans), F32, *row),
        ],
        flops=4 * rows * width * chans,
        after=after,
    )


def back_mix_kernel(
    loc_ref, cum_ref, state_ref, pi_ref, pf_ref, gpg_ref, carry_ref, prior_ref, lb_ref, w,
    both_ref, b0, b1, term_ref,
):
    _, rows, chans = loc_ref.shape
    steps = rows // CHUNKS
    lb = lb_ref[...]
    rest = 1.0 - lb
    cin = carry_ref[0]
    term = jnp.zeros((1, loc_ref.shape[2]), F32)
    top = lax.broadcasted_iota(jnp.int32, (steps, loc_ref.shape[2]), 0) == 0
    for c in range(CHUNKS - 1, -1, -1):
        at = pl.ds(c * steps, steps)
        adj = loc_ref[0, at, :] + cum_ref[0, at, :] * cin
        pi = pi_ref[0, at, :]
        sig = sigmoid(pf_ref[0, at, :])
        cin = (lb + rest * sig[0:1]) * adj[0:1]
        st = state_ref[0, at, :]
        before = prior_ref[0] if c == 0 else state_ref[0, pl.ds(c * steps - 1, 1), :]
        prev = jnp.where(top, before, pltpu.roll(st, 1, 0))
        sig_in = sigmoid(pi)
        total = adj * (prev - pi * sig_in)
        left = 1.0 - sig
        slope = sig_in * (1.0 + pi * (1.0 - sig_in))
        both_ref[0, at, :chans] = (adj * (rest * left) * slope).astype(BF)
        both_ref[0, at, chans:] = (total * rest * sig * left).astype(BF)
        term = term + jnp.sum(total * left, axis=0, keepdims=True)
    term_ref[0] = term
    out = (
        dot_last(both_ref[0, :, :chans], w[0])
        + dot_last(both_ref[0, :, chans:], w[1])
        + dot_last(gpg_ref[0], w[2])
    ).astype(BF)
    first = pl.program_id(0) == 0

    @pl.when(first)
    def _():
        b0[...] = out

    @pl.when(jnp.logical_not(first))
    def _():
        b1[...] = out


def back_mix(loc, cum, state, pi, pf, gpg, carry, prior, shift, lower, in_proj, after=()):
    _, rows, chans = state.shape
    width = in_proj.shape[1]
    piece = ((1, rows, chans), lambda g: (g, 0, 0))
    per = ((1, 1, chans), lambda g: (g, 0, 0))
    moved = ((1, 1, chans), lambda g: (g + shift, 0, 0))
    whole = ((rows, width), BF, (rows, width), lambda g: (0, 0))
    return call(
        back_mix_kernel,
        "back_mix",
        (2,),
        [(v, *piece) for v in (loc, cum, state, pi, pf, gpg)]
        + [(carry, *moved), (prior, *moved), fixed(lower), fixed(in_proj)],
        [
            ((2, rows, 2 * chans), BF, (1, rows, 2 * chans), lambda g: (g, 0, 0)),
            whole,
            whole,
            ((2, 1, chans), F32, *per),
        ],
        flops=12 * rows * width * chans,
        after=after,
    )


def total_product(near_count, refs):
    lefts, (near, far) = refs[:-2], refs[-2:]
    return dot_first(stack(*lefts[:near_count]), near[...]) + dot_first(
        stack(*lefts[near_count:]), far[...]
    )


def product_kernel(near_count, me, *refs):
    refs[-1][...] = total_product(near_count, refs[:-1]).astype(BF)


def product_add_kernel(near_count, half, me, *refs):
    got, send, keep = refs[-3:]
    total = (total_product(near_count, refs[:-3]) + got[...].astype(F32)).astype(BF)
    early = pl.program_id(0) < half

    @pl.when(early)
    def _():
        send[...] = total

    @pl.when(jnp.logical_not(early))
    def _():
        keep[...] = total


def product(me, lefts, near, far, bits, size, got=None, after=(), more=0):
    levels = len(bits)
    count = 1 << (levels - 1)
    base = 0 if got is None else count
    top = 2 * count - 1 - base
    units = near.shape[1]
    near_count = len(lefts[0])
    lefts = [*lefts[0], *lefts[1]]

    def place(j, me):
        turned = top - j
        block = me[0]
        for n, bit in enumerate(bits):
            block = block ^ (((turned >> (levels - 1 - n)) & 1) * bit)
        return (0, block)

    if size % 128:
        def ordered(x, rows):
            parts = [
                lax.dynamic_slice_in_dim(x[:rows], place(j, me)[1] * size, size, 1)
                for j in range(count)
            ]
            return jnp.concatenate(parts, axis=1), rows

        lefts = [ordered(*x) for x in lefts]
        count, size = count * size // 128, 128
        position = lambda j, me: (0, j)
    else:
        position = place
    inputs = [(x, (rows, size), position) for x, rows in lefts]
    inputs += [fixed(near), fixed(far)]
    flops = 0
    if got is None:
        out = ((count * size + more, units), BF, (size, units), lambda j, me: (j, 0))
        return call(
            functools.partial(product_kernel, near_count),
            "product", (count,), inputs, [out], flops, after, blocks=me,
        )
    half = count // 2
    inputs.append((got, (size, units), lambda j, me: (j, 0)))
    shape = (half * size, units)
    send = (shape, BF, (size, units), lambda j, me: (jnp.minimum(j, half - 1), 0))
    keep = (shape, BF, (size, units), lambda j, me: (jnp.maximum(j - half, 0), 0))
    return call(
        functools.partial(product_add_kernel, near_count, half),
        "product_add",
        (count,),
        inputs,
        [send, keep],
        flops,
        after,
        blocks=me,
    )


def halve_kernel(half, one, two, send, keep):
    total = (one[...].astype(F32) + two[...].astype(F32)).astype(BF)
    early = pl.program_id(0) < half

    @pl.when(early)
    def _():
        send[...] = total

    @pl.when(jnp.logical_not(early))
    def _():
        keep[...] = total


def halve(one, two, size, after=()):
    count = one.shape[0] // size
    half = count // 2
    units = one.shape[1]
    block = ((size, units), lambda j: (j, 0))
    shape = (half * size, units)
    return call(
        functools.partial(halve_kernel, half),
        "halve",
        (count,),
        [(one, *block), (two, *block)],
        [
            (shape, BF, (size, units), lambda j: (jnp.minimum(j, half - 1), 0)),
            (shape, BF, (size, units), lambda j: (jnp.maximum(j - half, 0), 0)),
        ],
        after=after,
    )


def finish_kernel(turned, one, two, *refs):
    out = refs[-1]
    total = one[...].astype(F32) + two[...].astype(F32)
    if turned:
        out[...] = total.T
    else:
        parts, _, units = out.shape
        for part in range(parts):
            out[part] = total[:, part * units : (part + 1) * units]


def finish(one, two, turned=False, slot=0, parts=1, slots=1, into=None, after=()):
    rows, units = one.shape
    if turned:
        tile = 128 if rows % 128 == 0 else rows
        shape = (units, rows)
        out = pl.BlockSpec((units, tile), lambda n: (0, n))
    else:
        tile = 64 if rows % 64 == 0 else rows
        shape = (slots, rows, units // parts)
        out = pl.BlockSpec((parts, tile, units // parts), lambda n: (slot // parts, n, 0))
    block = pl.BlockSpec((tile, units), lambda n: (n, 0))
    held = [] if into is None else [into]
    waits = [*held, *after]
    count = len(waits)
    return pl.pallas_call(
        lambda one, two, *refs: finish_kernel(turned, one, two, *refs[count:]),
        grid=(rows // tile,),
        in_specs=[block, block] + [ANYWHERE] * count,
        out_specs=out,
        out_shape=sds(shape),
        input_output_aliases={2: 0} if held else {},
        compiler_params=pltpu.CompilerParams(vmem_limit_bytes=VMEM_LIMIT),
        cost_estimate=pl.CostEstimate(flops=0, bytes_accessed=0, transcendentals=0),
        name="finish",
    )(one, two, *waits)


def row_call(kernel, name, arrays, gains, outputs, sums=0, after=(), most=64, more=()):
    rows, width = arrays[0].shape[-2:]
    tile = most if rows % most == 0 else rows

    def block(shape):
        lead = len(shape) - 2
        return (*shape[:-2], tile, shape[-1]), lambda r: (*(0,) * lead, r, 0)

    inputs = [(a, *block(a.shape)) for a in arrays] + [fixed(g) for g in gains]
    results = [(shape, dtype, *block(shape)) for shape, dtype in outputs]
    results += [((1, width), F32, (1, width), lambda r: (0, 0))] * sums + list(more)
    return call(kernel, name, (rows // tile,), inputs, results, after=after)


def add_to(ref, term):
    first = pl.program_id(0) == 0

    @pl.when(first)
    def _():
        ref[...] = term

    @pl.when(jnp.logical_not(first))
    def _():
        ref[...] += term


def first_norm_kernel(x_ref, gain_ref, out):
    x = x_ref[...].astype(F32)
    out[...] = (x * rms_scale(x) * gain_ref[...]).astype(BF)


def plus_kernel(one, two, out):
    out[...] = (one[...].astype(F32) + two[...].astype(F32)).astype(BF)


def plus(one, two, after=()):
    return row_call(plus_kernel, "plus", [one, two], [], [(one.shape, BF)], after=after)


def join_kernel(one, two, top, bottom):
    half = bottom.shape[0]
    rows = 2 * half
    for out, at in ((top, 0), (bottom, half)):
        part = slice(at, at + half)
        out[:half] = (one[part].astype(F32) + two[part].astype(F32)).astype(BF)
    extra = one[rows:].astype(F32) + two[rows:].astype(F32)
    top[half:] = in_two(jnp.broadcast_to(extra[0:1] + extra[1:2], extra.shape))


def join(one, two, after=()):
    rows, width = one.shape[0] - EXTRA, one.shape[1]
    shapes = [(rows // 2 + EXTRA, width), (rows // 2, width)]
    return call(
        join_kernel, "join", (1,), [fixed(one), fixed(two)],
        [(s, BF, s, lambda i: (0, 0)) for s in shapes], after=after,
    )


def middle_kernel(half, x, own, core, hop, own_more, core_more, hop_more, gain, *refs):
    branch_ref, middle_ref, scale_ref, full, out = refs[-5:]
    rows, width = x.shape
    more = own_more[...].astype(F32) + core_more[...].astype(F32) + hop_more[...].astype(F32)
    squares = (more[0:1] + more[1:2])[:, half * rows : (half + 1) * rows]
    scale = lax.rsqrt(upright(squares) / width + EPS)
    branch = own[...].astype(F32) + core[...].astype(F32) + hop[...].astype(F32)
    middle = x[...].astype(F32) + branch * scale[:, :1]
    branch_ref[...] = branch
    scale_ref[...] = scale
    middle_ref[...] = middle
    low = (middle * rms_scale(middle) * gain[...]).astype(BF)
    full[...] = low
    out[...] = low


def middle_half(half, x, own, core, hop, top, gain, begun=(), after=()):
    total, width = x.shape
    rows = total // 2
    part = pl.BlockSpec((rows, width), lambda i: (half, 0))
    alone = pl.BlockSpec((rows, width), lambda i: (0, 0))
    more = pl.BlockSpec((EXTRA, width), lambda i: (total // EXTRA, 0))
    top_more = pl.BlockSpec((EXTRA, width), lambda i: (rows // EXTRA, 0))
    waits = [*begun, *after]
    return pl.pallas_call(
        functools.partial(middle_kernel, half),
        grid=(1,),
        in_specs=[part, part, part, alone, more, more, top_more, pl.BlockSpec((1, width), lambda i: (0, 0))]
        + [ANYWHERE] * len(waits),
        out_specs=[part, part, pl.BlockSpec((rows, 128), lambda i: (half, 0)), part, alone],
        out_shape=[
            sds((total, width)), sds((total, width)), sds((total, 128)), sds((total, width), BF),
            sds((rows + (16 if half == 0 else 0), width), BF),
        ],
        input_output_aliases={8 + n: n for n in range(len(begun))},
        compiler_params=pltpu.CompilerParams(vmem_limit_bytes=VMEM_LIMIT),
        cost_estimate=pl.CostEstimate(flops=0, bytes_accessed=0, transcendentals=0),
        name="middle",
    )(x, own, core, hop, own, core, top, gain, *waits)


def turn_kernel(up, own, core, hop, middle_ref, branch, scale_ref, gain, grad_ref, term, out):
    tile = up.shape[0]
    step = pl.program_id(0)
    rows = out.shape[0] - EXTRA
    grad = own[...].astype(F32) + core[...].astype(F32) + hop[...].astype(F32)
    middle = middle_ref[...]
    scale = rms_scale(middle)
    total = up[...].astype(F32) + norm_back(grad, middle, scale, gain[...])
    low = total.astype(BF)
    grad_ref[...] = total
    out[pl.ds(pl.multiple_of(step * tile, tile), tile), :] = low
    inner = wide(jnp.sum(low.astype(F32) * branch[...], axis=-1, keepdims=True)).T[:EXTRA]
    outer = scale_ref[...].T[:EXTRA]
    high_outer = outer.astype(BF).astype(F32)
    high_inner = inner.astype(BF).astype(F32)
    which = lax.broadcasted_iota(jnp.int32, inner.shape, 0)
    both = jnp.where(which < 2, outer, inner)
    high = jnp.where(which < 2, high_outer, high_inner)
    extra = jnp.where(which % 2 == 0, high, both - high)

    @pl.when(step == 0)
    def _():
        out[rows:, :] = jnp.zeros((EXTRA, out.shape[1]), BF)

    out[rows:, pl.ds(pl.multiple_of(step * tile, tile), tile)] = extra.astype(BF)
    add_to(term, jnp.sum(grad * middle * scale, axis=0, keepdims=True))


def turn(up, own, core, hop, middle, branch, scale, gain, after=()):
    rows, width = up.shape
    shape = (rows + EXTRA, width)
    return row_call(
        turn_kernel, "turn", [up, own, core, hop, middle, branch, scale], [gain],
        [(up.shape, F32)], sums=1, after=after, most=128,
        more=[(shape, BF, shape, lambda r: (0, 0))],
    )


def last_kernel(x_ref, own, core, hop, grad_middle, gain, out, term):
    grad = own[...].astype(F32) + core[...].astype(F32) + hop[...].astype(F32)
    x = x_ref[...].astype(F32)
    scale = rms_scale(x)
    out[...] = grad_middle[...] + norm_back(grad, x, scale, gain[...])
    add_to(term, jnp.sum(grad * x * scale, axis=0, keepdims=True))


def result_kernel(middle, own, core, hop, out):
    out[...] = (
        middle[...] + (own[...].astype(F32) + core[...].astype(F32) + hop[...].astype(F32))
    ).astype(BF)


def in_order(me, total, other):
    odd = (me[0] % 2) == 1
    return (
        odd,
        jnp.where(odd, other[0], total[0]),
        jnp.where(odd, other[1], total[1]),
        jnp.where(odd, total[0], other[0]),
        jnp.where(odd, total[1], other[1]),
    )


def pair_kernel(reverse, me, total, other, pair):
    odd, low_a, low_b, high_a, high_b = in_order(me, total, other)
    pair[0] = low_a * high_a
    pair[1] = low_a * high_b + low_b if reverse else high_a * low_b + high_b


def enter_kernel(reverse, me, total, other, *refs):
    odd, low_a, low_b, high_a, high_b = in_order(me, total, other)
    enter = jnp.zeros_like(low_a)
    for got in reversed(refs[:-1]):
        enter = got[0] * enter + got[1]
    if reverse:
        enter = jnp.where(odd, enter, high_a * enter + high_b)
    else:
        enter = jnp.where(odd, low_a * enter + low_b, enter)
    for g in range(enter.shape[0]):
        refs[-1][g] = enter[g : g + 1]


def chain(me, total, reverse, between=None, beside=None):
    size = lax.axis_size("seq")
    _, groups, chans = total.shape
    other = swap(total, "seq", 1)
    got = between() if between else ()
    whole = (total.shape, F32, total.shape, lambda i, me: (0, 0, 0))
    pair = call(
        functools.partial(pair_kernel, reverse), "pair", (1,), [fixed(total), fixed(other)], [whole],
        after=got, blocks=me,
    )
    sign = -1 if reverse else 1
    reached = [shift(pair, "seq", 2 * sign * d) for d in range(1, size // 2)]
    shape = (groups, 1, chans)
    got = beside(pair) if beside else ()
    return call(
        functools.partial(enter_kernel, reverse), "enter", (1,),
        [fixed(total), fixed(other), *[fixed(r) for r in reached]],
        [(shape, F32, shape, lambda i, me: (0, 0, 0))],
        after=got,
        blocks=me,
    )


def seq_bits():
    size = lax.axis_size("seq")
    bits = []
    bit = 1
    while bit < size:
        bits.append(bit)
        bit *= 2
    return bits


class Weight:
    def __init__(self, me, lefts, near, far, bits, size):
        self.me, self.lefts, self.near, self.far = me, lefts, near, far
        self.bits, self.size, self.level = bits, size, 0

    def begin(self, *earlier, more=0):
        self.send = product(
            self.me, self.lefts, self.near, self.far, self.bits, self.size, after=earlier, more=more
        )
        return self.send

    def go(self, *earlier):
        send = after(self.send, *earlier) if earlier else self.send
        self.got = swap(send, "seq", self.bits[self.level])
        self.level += 1

    def step(self, *earlier):
        if self.level == 1:
            self.send, self.keep = product(
                self.me, self.lefts, self.near, self.far, self.bits, self.size, self.got, after=earlier
            )
        else:
            self.send, self.keep = halve(self.keep, self.got, self.size, after=earlier)
        return self.send

    def last(self):
        return self.level == len(self.bits)


def gain_terms(norm1_term, norm2_term, mixer_term, bound_n, bound_f):
    wt = lax.axis_index("wt")
    span = norm1_term.shape[1] // lax.axis_size("wt")
    norm_terms = jnp.concatenate([norm1_term, norm2_term])

    def part(j):
        return lax.dynamic_slice_in_dim(norm_terms, (wt ^ j) * span, span, 1)

    norms = part(0)
    for j in (1, 2, 3):
        norms = norms + swap(part(j), "wt", j)
    bound_term = jnp.sum(bound_n, axis=(0, 1)) + jnp.sum(bound_f, axis=(0, 1))
    return jnp.stack([norms[0], mixer_term[0], norms[1], bound_term])


GATE_AT, LOWER_AT, UP_AT, LOWER_BITS = "beside", "beside", "pair", "m"
ORDER = (
    ("-p", "-n", "gs", "bb", "us", "-l", "ob", "ls", "ab", "-r", "us", "gf", "bs")
    + ("lf", "as", "os", "bs", "uf", "as", "os", "-1", "bf", "af", "-2", "-3", "of")
)


def on_device(
    tokens,
    in_proj,
    out_proj,
    gate_up,
    down,
    norm1_gain,
    mixer_gain,
    norm2_gain,
    lower_bound,
    cotangent,
):
    width = in_proj.shape[1]
    chans = in_proj.shape[2]
    x = tokens[0]
    g0 = cotangent[0]
    rows = x.shape[0]
    bits = seq_bits()
    y_first = bits
    mixed_order = {"m": bits[1:2] + bits[:1] + bits[2:], "z": bits[1:] + bits[:1], "y": bits}[LOWER_BITS]
    block = width // lax.axis_size("seq")
    me = lax.axis_index("seq").reshape(1).astype(jnp.int32)

    offset = lax.axis_index("wt") * chans
    lower_use = lax.dynamic_slice_in_dim(lower_bound, offset, chans)[None]
    mixer_use = lax.dynamic_slice_in_dim(mixer_gain, offset, chans)[None]
    gain_one, gain_two = norm1_gain[None], norm2_gain[None]

    n0 = row_call(first_norm_kernel, "first_norm", [x], [gain_one], [(x.shape, BF)])
    hop = swap(n0, "wt", 2)
    n1 = swap(n0, "wt", 1)
    g1 = swap(g0, "wt", 1)
    grad_hop = swap(after(g0, n0), "wt", 2)
    pi_n, pf_n, pg_n, loc_n, cum_n, tot = project(n0, n1, in_proj, lower_use)
    gh_n = hidden_grad(g0, g1, down, after=(tot,))
    n2 = after(hop, gh_n)
    n3 = swap(n2, "wt", 1)
    pi_f, pf_f, pg_f, loc_f, cum_f, tot = project(n2, n3, in_proj, lower_use, (tot,))
    enter = chain(me, tot, False)
    state_f, bf0, bf1 = mix(loc_f, cum_f, pg_f, enter, 2, mixer_use, out_proj)
    g2 = after(grad_hop, bf0)
    g3 = swap(g2, "wt", 1)
    state_n, bn0, bn1 = mix(loc_n, cum_n, pg_n, enter, 0, mixer_use, out_proj, after=(bf0,))
    across = join(bf0, swap(bf1, "wt", 1), after=(bn0,))
    hops = [swap(part, "wt", 2) for part in across]
    core = swap(bn1, "wt", 1)
    gh_f = hidden_grad(g2, g3, down, after=(across[1],))
    *begun, half0 = middle_half(0, x, bn0, core, hops[0], hops[0], gain_two, after=(gh_f,))
    branch, middle, scale_two, t0, half1 = middle_half(
        1, x, bn0, core, hops[1], hops[0], gain_two, begun
    )

    hops = [swap(half, "wt", 2) for half in (half0, half1)]
    t1 = [swap(half, "wt", 1) for half in (half0, half1)]
    hid_n, gg_n, gu_n = feed((t0, *t1), gate_up, gh_n)
    kn0, kn1 = feed_back(gg_n, gu_n, gate_up)
    core = swap(kn1, "wt", 1)
    t2 = [after(hop, kn0) for hop in hops]
    t3 = [swap(half, "wt", 1) for half in t2]
    hid_f, gg_f, gu_f = feed((*t2, *t3), gate_up, gh_f)

    def pieces(*arrays):
        return [(v, min(rows, v.shape[0]) // 128 * 128) for v in arrays]

    twos = (pieces(t0, *t1), pieces(*t2, *t3))
    gate = Weight(me, twos, gg_n, gg_f, y_first, block)
    up = Weight(me, twos, gu_n, gu_f, y_first, block)
    lower = Weight(me, (pieces(g0, g1), pieces(g2, g3)), hid_n, hid_f, mixed_order, block)
    kf0, kf1 = feed_back(gg_f, gu_f, gate_up)
    gate.begin(kf0, more=128)
    gate.go()
    across = plus(kf0, swap(kf1, "wt", 1), after=(gate.send,))
    hop = swap(across, "wt", 2)
    lower.begin(across, more=128)
    lower.go()
    up.begin(lower.send, across, more=0)
    ff0, ff1 = feed_out(hid_f, down, after=(up.send,))
    grad_middle, norm2_term, b0 = turn(
        g0, kn0, core, hop, middle, branch, scale_two, gain_two, after=(ff0,)
    )

    hop = swap(b0, "wt", 2)
    b1 = swap(b0, "wt", 1)
    mixed_n, gpg_n, bloc_n, bcum_n, btot, mixer_n = back_local(
        b0, b1, out_proj, pg_n, pf_n, state_n, mixer_use, lower_use
    )
    ffn_across = plus(ff0, swap(ff1, "wt", 1), after=(btot,))
    fn0, fn1 = feed_out(hid_n, down, after=(ffn_across,))
    ffn_core = swap(fn1, "wt", 1)
    b2 = after(hop, fn0)
    b3 = swap(b2, "wt", 1)
    early = (gate.step(b2),) if GATE_AT == "before" else ()
    mixed_f, gpg_f, bloc_f, bcum_f, btot, mixer_f = back_local(
        b2, b3, out_proj, pg_f, pf_f, state_f, mixer_use, lower_use, (btot,), after=early
    )

    def beside(pair):
        if UP_AT == "pair":
            up.go(pair)
        for one, place in ((gate, GATE_AT), (lower, LOWER_AT)):
            if place == "beside":
                pair = one.step(pair)
        return (pair,)

    leave = chain(me, btot, True, None, beside)
    if UP_AT == "leave":
        up.go(leave)
    if GATE_AT == "after":
        gate.step(leave)
        gate.go()
    else:
        gate.go(leave)
    if LOWER_AT == "beside":
        if LOWER_BITS == "z":
            lower.go(leave)
        else:
            lower.go()
    both_f, df0, df1, bound_f = back_mix(
        bloc_f, bcum_f, state_f, pi_f, pf_f, gpg_f, leave, enter, 2, lower_use, in_proj
    )

    def flat(values):
        return values.reshape(2 * rows, values.shape[2])

    normals = (pieces(n0, n1), pieces(n2, n3))
    last_in = Weight(me, normals, flat(gpg_n), flat(gpg_f), y_first, block)
    out = Weight(me, (pieces(b0, b1), pieces(b2, b3)), flat(mixed_n), flat(mixed_f), y_first, block)
    both_n, dn0, dn1, bound_n = None, None, None, None
    token = df0
    weights = {"g": gate, "u": up, "l": lower, "a": last_in, "o": out}
    rounds = list(bits)
    gate_up_grad = in_grad = None
    for kind, act in ORDER:
        if kind in weights:
            one = weights[kind]
            if act == "b":
                token = one.begin(token)
                one.go()
            elif act == "s":
                token = one.step(token)
                one.go()
                while one.level > 2 and not one.last():
                    token = one.step(token)
                    one.go()
            elif kind in "gu":
                slot = "gu".index(kind)
                token = gate_up_grad = finish(
                    one.keep, one.got, slot=slot, slots=2, into=gate_up_grad,
                    after=() if token is gate_up_grad else (token,),
                )
            elif kind == "b":
                token = in_grad = finish(
                    one.keep, one.got, parts=2, slots=3, into=in_grad,
                    after=() if token is in_grad else (token,),
                )
            elif kind == "a":
                token = in_grad = finish(
                    one.keep, one.got, slot=2, slots=3, into=in_grad,
                    after=() if token is in_grad else (token,),
                )
            elif kind == "l":
                token = down_grad = finish(one.keep, one.got, True, after=(token,))
            else:
                token = out_grad = finish(one.keep, one.got, True, after=(token,))
        elif act == "p":
            token = plus(df0, swap(df1, "wt", 1), after=(token,))
            hop = swap(token, "wt", 2)
        elif act == "n":
            both_n, dn0, dn1, bound_n = back_mix(
                bloc_n, bcum_n, state_n, pi_n, pf_n, gpg_n, leave, enter, 0, lower_use, in_proj,
                after=(token,),
            )
            token = dn0
            core = swap(dn1, "wt", 1)
            weights["b"] = Weight(me, normals, flat(both_n), flat(both_f), y_first, block)
        elif act == "l":
            grad_inputs, norm1_term = row_call(
                last_kernel,
                "last",
                [x, dn0, core, hop, grad_middle],
                [gain_one],
                [(x.shape, F32)],
                sums=1,
                after=(token,),
            )
            token = grad_inputs
            ffn_hop = swap(after(ffn_across, token), "wt", 2)
            gains = gain_terms(norm1_term, norm2_term, mixer_n + mixer_f, bound_n, bound_f)
        elif act == "r":
            token = result = row_call(
                result_kernel, "result", [middle, fn0, ffn_core, ffn_hop], [], [(x.shape, BF)],
                after=(token,),
            )
        elif act in "123":
            for _ in range(len(rounds) if act == "3" else 1):
                gains = gains + after(swap(gains, "seq", rounds.pop(0)), token)

    return (
        result[None],
        grad_inputs[None],
        in_grad,
        out_grad,
        gate_up_grad,
        down_grad,
        gains[0],
        gains[1],
        gains[2],
        gains[3],
    )


def solution(mesh):
    placed = (
        P("wt", "seq", None),
        P(None, None, "wt"),
        P("wt", None),
        P(None, None, "wt"),
        P("wt", None),
        P(),
        P(),
        P(),
        P(),
        P("wt", "seq", None),
    )
    return jax.shard_map(
        on_device,
        mesh=mesh,
        in_specs=placed,
        out_specs=(
            P("wt", "seq", None),
            P("wt", "seq", None),
            P(None, "seq", "wt"),
            P("wt", "seq"),
            P(None, "seq", "wt"),
            P("wt", "seq"),
            P("wt"),
            P("wt"),
            P("wt"),
            P("wt"),
        ),
        check_vma=False,
    )
```

```python
import functools

import jax
import jax.numpy as jnp
from jax import lax
from jax.experimental import pallas as pl
from jax.experimental.pallas import tpu as pltpu
from jax.sharding import PartitionSpec as P

EPS = 1e-06
BF = jnp.bfloat16
F32 = jnp.float32
CHUNKS = 8


def swap(values, axis, bit):
    size = lax.axis_size(axis)
    return lax.ppermute(values, axis, [(i, i ^ bit) for i in range(size)])


def shift(values, axis, step):
    size = lax.axis_size(axis)
    pairs = [(i, i + step) for i in range(size) if 0 <= i + step < size]
    return lax.ppermute(values, axis, pairs)


def rms_scale(values):
    return lax.rsqrt(jnp.mean(values * values, axis=-1, keepdims=True) + EPS)


def norm_back(grad_normed, values, scale, weight):
    weighted = grad_normed * weight
    return scale * weighted - values * (scale * scale * scale) * jnp.mean(
        weighted * values, axis=-1, keepdims=True
    )


def sigmoid(v):
    return 0.5 * jnp.tanh(0.5 * v) + 0.5


ANYWHERE = pl.BlockSpec(memory_space=pl.ANY)
EXTRA = 16
VMEM_LIMIT = 63 * 1024 * 1024


def sds(shape, dtype=F32):
    return jax.ShapeDtypeStruct(shape, dtype)


def call(kernel, name, grid, inputs, outputs, flops=0, after=(), scratch=(), blocks=None):
    in_specs = [pl.BlockSpec(block, index) for _, block, index in inputs]
    in_specs += [ANYWHERE] * len(after)
    out_specs = [pl.BlockSpec(block, index) for _, _, block, index in outputs]
    count = len(inputs)
    skip = len(after)
    lead = 0 if blocks is None else 1

    def body(*refs):
        kernel(*refs[: lead + count], *refs[lead + count + skip :])

    settings = dict(
        out_shape=[sds(shape, dtype) for shape, dtype, _, _ in outputs],
        compiler_params=pltpu.CompilerParams(vmem_limit_bytes=VMEM_LIMIT),
        cost_estimate=pl.CostEstimate(flops=0, bytes_accessed=0, transcendentals=0),
        name=name,
    )
    operands = [a for a, _, _ in inputs] + list(after)
    if blocks is None:
        got = pl.pallas_call(
            body, grid=grid, in_specs=in_specs, out_specs=out_specs, scratch_shapes=list(scratch), **settings
        )(*operands)
    else:
        spec = pltpu.PrefetchScalarGridSpec(
            num_scalar_prefetch=1,
            grid=grid,
            in_specs=in_specs,
            out_specs=out_specs,
            scratch_shapes=list(scratch),
        )
        got = pl.pallas_call(body, grid_spec=spec, **settings)(blocks, *operands)
    return got[0] if len(outputs) == 1 else got


def fixed(array):
    zeros = (0,) * array.ndim
    return (array, array.shape, lambda *_: zeros)


def hold_kernel(*refs):
    pass


def after(value, *earlier):
    return pl.pallas_call(
        hold_kernel,
        in_specs=[ANYWHERE] * (1 + len(earlier)),
        out_specs=ANYWHERE,
        out_shape=jax.ShapeDtypeStruct(value.shape, value.dtype),
        input_output_aliases={0: 0},
        cost_estimate=pl.CostEstimate(flops=0, bytes_accessed=0, transcendentals=0),
        name="hold",
    )(value, *earlier)


def dot(left, right):
    return jnp.dot(left, right, preferred_element_type=F32)


def dot_last(left, right):
    return lax.dot_general(left, right, (((1,), (1,)), ((), ())), preferred_element_type=F32)


def dot_first(left, right):
    return lax.dot_general(left, right, (((0,), (0,)), ((), ())), preferred_element_type=F32)


def wide(column):
    return jnp.broadcast_to(column, (column.shape[0], 128))


def in_two(values):
    which = lax.broadcasted_iota(jnp.int32, values.shape, 0)
    high = values.astype(BF).astype(F32)
    return jnp.where(which == 0, high, jnp.where(which == 1, values - high, 0.0)).astype(BF)


def upright(row):
    return jnp.broadcast_to(row, (128, row.shape[1])).T


def stack(*refs):
    return jnp.concatenate([r[...] for r in refs], axis=0)


def tile_of(size, most):
    best = size
    for tile in range(128, most + 1, 128):
        if size % tile == 0:
            best = tile
    return best


def project_kernel(x0, x1, w, lb_ref, *refs):
    pi_ref, pf_ref, pg_ref, loc_ref, cum_ref, tot_ref = refs[-6:]
    groups, rows, tile = loc_ref.shape
    steps = rows // CHUNKS
    y = dot(stack(x0, x1), jnp.concatenate([w[0], w[1], w[2]], axis=1))
    lb = lb_ref[...]
    for g in range(groups):
        part = y[g * rows : (g + 1) * rows]
        pi_ref[g] = part[:, :tile]
        pf_ref[g] = part[:, tile : 2 * tile]
        pg_ref[g] = part[:, 2 * tile :]
    for g in range(groups):
        s = jnp.zeros((CHUNKS, tile), F32)
        p = jnp.ones_like(s)
        for t in range(steps):
            at = pl.ds(t, CHUNKS, stride=steps)
            pi = pi_ref[g, at, :]
            sig = sigmoid(pf_ref[g, at, :])
            f = lb + (1.0 - lb) * sig
            s = f * s + pi * sigmoid(pi) * ((1.0 - lb) * (1.0 - sig))
            p = p * f
            loc_ref[g, at, :] = s
            cum_ref[g, at, :] = p
        a = p[0:1]
        b = s[0:1]
        for c in range(1, CHUNKS):
            b = p[c : c + 1] * b + s[c : c + 1]
            a = a * p[c : c + 1]
        put_total(tot_ref, g, a, b, refs[:-6])


def put_total(tot_ref, g, a, b, prior):
    at = g
    if prior:
        at = g + prior[0].shape[1]
        if g == 0:
            tot_ref[:, : prior[0].shape[1], :] = prior[0][...]
    tot_ref[0, at : at + 1, :] = a
    tot_ref[1, at : at + 1, :] = b


def total_blocks(prior, chans, tile):
    count = 2 + sum(p.shape[1] for p in prior)
    inputs = [(p, (2, p.shape[1], tile), lambda c: (0, 0, c)) for p in prior]
    return inputs, ((2, count, chans), F32, (2, count, tile), lambda c: (0, 0, c))


def project(x0, x1, in_proj, lower, prior=(), after=()):
    rows, width = x0.shape
    chans = in_proj.shape[2]
    tile = tile_of(chans, 128)
    full = ((2, rows, chans), F32, (2, rows, tile), lambda c: (0, 0, c))
    before, total = total_blocks(prior, chans, tile)
    return call(
        project_kernel,
        "project",
        (chans // tile,),
        [
            fixed(x0),
            fixed(x1),
            (in_proj, (3, width, tile), lambda c: (0, 0, c)),
            (lower, (1, tile), lambda c: (0, c)),
            *before,
        ],
        [full] * 5 + [total],
        flops=12 * rows * width * chans,
        after=after,
    )


def mix_kernel(loc_ref, cum_ref, pg_ref, carry_ref, gain_ref, w_ref, state_ref, b0, b1, mix_ref, sq_ref):
    rows = loc_ref.shape[1]
    steps = rows // CHUNKS
    gain = gain_ref[...]
    cin = carry_ref[0]
    for c in range(CHUNKS):
        at = pl.ds(c * steps, steps)
        st = loc_ref[0, at, :] + cum_ref[0, at, :] * cin
        cin = st[steps - 1 : steps]
        pg = pg_ref[0, at, :]
        state_ref[0, at, :] = st
        mix_ref[at, :] = (st * gain * (pg * sigmoid(pg))).astype(BF)
        sq_ref[at, :] = wide(jnp.sum(st * st, axis=-1, keepdims=True))
    out = dot(mix_ref[...], w_ref[...]).astype(BF)
    first = pl.program_id(0) == 0

    def put(ref):
        ref[:rows] = out
        ref[rows:] = jnp.zeros((EXTRA, out.shape[1]), BF)
        ref[rows:, :rows] = in_two(sq_ref[...].T[:EXTRA])

    @pl.when(first)
    def _():
        put(b0)

    @pl.when(jnp.logical_not(first))
    def _():
        put(b1)


def mix(loc, cum, pg, carry, shift, gain, out_proj, after=()):
    _, rows, chans = loc.shape
    width = out_proj.shape[1]
    piece = ((1, rows, chans), lambda g: (g, 0, 0))
    shape = (rows + EXTRA, width)
    whole = (shape, BF, shape, lambda g: (0, 0))
    return call(
        mix_kernel,
        "mix",
        (2,),
        [
            (loc, *piece),
            (cum, *piece),
            (pg, *piece),
            (carry, (1, 1, chans), lambda g: (g + shift, 0, 0)),
            fixed(gain),
            fixed(out_proj),
        ],
        [
            (loc.shape, F32, *piece),
            whole,
            whole,
        ],
        flops=4 * rows * chans * width,
        after=after,
        scratch=[pltpu.VMEM((rows, chans), BF), pltpu.VMEM((rows, 128), F32)],
    )


def hidden_grad_kernel(g0, g1, w, out):
    out[...] = dot_last(stack(g0, g1), w[...])


def hidden_grad(g0, g1, down, after=()):
    rows, width = g0.shape
    units = down.shape[0]
    tile = min(512, units)
    return call(
        hidden_grad_kernel,
        "hidden_grad",
        (pl.cdiv(units, tile),),
        [fixed(g0), fixed(g1), (down, (tile, width), lambda n: (n, 0))],
        [((2 * rows, units), F32, (2 * rows, tile), lambda n: (0, n))],
        flops=4 * rows * width * units,
        after=after,
    )


def feed_kernel(*refs):
    w, gh_ref, hidden, gg, gu = refs[-5:]
    x = stack(*refs[:-5])
    gate = dot(x, w[0])
    up = dot(x, w[1])
    gh = gh_ref[...]
    sig = sigmoid(gate)
    act = gate * sig
    hidden[...] = (act * up).astype(BF)
    gg[...] = (gh * up * (sig * (1.0 + gate * (1.0 - sig)))).astype(BF)
    gu[...] = (gh * act).astype(BF)


def feed(pieces, gate_up, gh, after=()):
    rows, width = gh.shape[0] // 2, gate_up.shape[1]
    units = gate_up.shape[2]
    tile = min(512, units)
    col = ((2 * rows, tile), lambda n: (0, n))
    return call(
        feed_kernel,
        "feed",
        (pl.cdiv(units, tile),),
        [
            *[(x, (min(x.shape[0], rows) // 128 * 128, width), lambda n: (0, 0)) for x in pieces],
            (gate_up, (2, width, tile), lambda n: (0, 0, n)),
            (gh, *col),
        ],
        [((2 * rows, units), BF, *col)] * 3,
        flops=8 * rows * width * units,
        after=after,
    )


def feed_back_kernel(gg, gu, w, b0, b1):
    rows = b0.shape[0]
    out = (dot_last(gg[...], w[0]) + dot_last(gu[...], w[1])).astype(BF)
    b0[...] = out[:rows]
    b1[...] = out[rows:]


def feed_back(gg, gu, gate_up, after=()):
    rows = gg.shape[0] // 2
    _, width, units = gate_up.shape
    tile = tile_of(width, 512)
    part = ((rows, width), BF, (rows, tile), lambda d: (0, d))
    return call(
        feed_back_kernel,
        "feed_back",
        (width // tile,),
        [fixed(gg), fixed(gu), (gate_up, (2, tile, units), lambda d: (0, d, 0))],
        [part, part],
        flops=8 * rows * width * units,
        after=after,
    )


def feed_out_kernel(h, w, b0, b1):
    rows = b0.shape[0]
    out = dot(h[...], w[...]).astype(BF)
    b0[...] = out[:rows]
    b1[...] = out[rows:]


def feed_out(hidden, down, after=()):
    rows = hidden.shape[0] // 2
    units, width = down.shape
    tile = tile_of(width, 512)
    part = ((rows, width), BF, (rows, tile), lambda d: (0, d))
    return call(
        feed_out_kernel,
        "feed_out",
        (width // tile,),
        [fixed(hidden), (down, (units, tile), lambda d: (0, d))],
        [part, part],
        flops=4 * rows * width * units,
        after=after,
    )


def back_local_kernel(
    width, g0, g1, w, pg_ref, pf_ref, state_ref, gain_ref, lb_ref, *refs
):
    mixed_ref, gpg_ref, loc_ref, cum_ref, tot_ref, term_ref = refs[-6:]
    groups, rows, tile = loc_ref.shape
    steps = rows // CHUNKS
    gain = gain_ref[...]
    lb = lb_ref[...]
    grads = dot_last(jnp.concatenate([g0[:rows], g1[:rows]], axis=0), w[...])
    term = jnp.zeros((1, tile), F32)
    for g in range(groups):
        extra = (g1 if g else g0)[rows:, :rows].astype(F32)
        scales = upright(extra[0:1] + extra[1:2])
        inners = upright(extra[2:3] + extra[3:4])
        for c in range(CHUNKS):
            at = pl.ds(c * steps, steps)
            part = slice(c * steps, (c + 1) * steps)
            scale = scales[part, :1]
            coef = scale * scale * scale * inners[part, :1] * (1.0 / width)
            pg = pg_ref[g, at, :]
            gm = grads[g * rows + c * steps : g * rows + (c + 1) * steps]
            st = state_ref[g, at, :]
            sig = sigmoid(pg)
            act = pg * sig
            unit = st * scale
            gact = gm * act
            mixed_ref[g, at, :] = (unit * gain * act).astype(BF)
            gpg_ref[g, at, :] = (gm * gain * unit * (sig * (1.0 + pg * (1.0 - sig)))).astype(BF)
            term = term + jnp.sum(gact * unit, axis=0, keepdims=True)
            loc_ref[g, at, :] = scale * (gact * gain) - st * coef
    term_ref[...] = term
    for g in range(groups):
        s = jnp.zeros((CHUNKS, tile), F32)
        q = jnp.ones_like(s)
        for t in range(steps - 1, -1, -1):
            at = pl.ds(t, CHUNKS, stride=steps)
            f = lb + (1.0 - lb) * sigmoid(pf_ref[g, at, :])
            adj = loc_ref[g, at, :] + s
            loc_ref[g, at, :] = adj
            cum_ref[g, at, :] = q
            s = f * adj
            q = q * f
        last = CHUNKS - 1
        a = q[last : last + 1]
        b = s[last : last + 1]
        for c in range(CHUNKS - 2, -1, -1):
            b = q[c : c + 1] * b + s[c : c + 1]
            a = a * q[c : c + 1]
        put_total(tot_ref, g, a, b, refs[:-6])


def back_local(g0, g1, out_proj, pg, pf, state, gain, lower, prior=(), after=()):
    rows, width = pg.shape[1], g0.shape[1]
    chans = out_proj.shape[0]
    tile = tile_of(chans, 128)
    piece = ((2, rows, tile), lambda c: (0, 0, c))
    row = ((1, tile), lambda c: (0, c))
    shape = (2, rows, chans)
    before, total = total_blocks(prior, chans, tile)
    return call(
        functools.partial(back_local_kernel, width),
        "back_local",
        (chans // tile,),
        [
            fixed(g0),
            fixed(g1),
            (out_proj, (tile, width), lambda c: (c, 0)),
            (pg, *piece),
            (pf, *piece),
            (state, *piece),
            (gain, *row),
            (lower, *row),
            *before,
        ],
        [
            (shape, BF, *piece),
            (shape, BF, *piece),
            (shape, F32, *piece),
            (shape, F32, *piece),
            total,
            ((1, chans), F32, *row),
        ],
        flops=4 * rows * width * chans,
        after=after,
    )


def back_mix_kernel(
    loc_ref, cum_ref, state_ref, pi_ref, pf_ref, gpg_ref, carry_ref, prior_ref, lb_ref, w,
    both_ref, b0, b1, term_ref,
):
    _, rows, chans = loc_ref.shape
    steps = rows // CHUNKS
    lb = lb_ref[...]
    rest = 1.0 - lb
    cin = carry_ref[0]
    term = jnp.zeros((1, loc_ref.shape[2]), F32)
    top = lax.broadcasted_iota(jnp.int32, (steps, loc_ref.shape[2]), 0) == 0
    for c in range(CHUNKS - 1, -1, -1):
        at = pl.ds(c * steps, steps)
        adj = loc_ref[0, at, :] + cum_ref[0, at, :] * cin
        pi = pi_ref[0, at, :]
        sig = sigmoid(pf_ref[0, at, :])
        cin = (lb + rest * sig[0:1]) * adj[0:1]
        st = state_ref[0, at, :]
        before = prior_ref[0] if c == 0 else state_ref[0, pl.ds(c * steps - 1, 1), :]
        prev = jnp.where(top, before, pltpu.roll(st, 1, 0))
        sig_in = sigmoid(pi)
        total = adj * (prev - pi * sig_in)
        left = 1.0 - sig
        slope = sig_in * (1.0 + pi * (1.0 - sig_in))
        both_ref[0, at, :chans] = (adj * (rest * left) * slope).astype(BF)
        both_ref[0, at, chans:] = (total * rest * sig * left).astype(BF)
        term = term + jnp.sum(total * left, axis=0, keepdims=True)
    term_ref[0] = term
    out = (
        dot_last(both_ref[0, :, :chans], w[0])
        + dot_last(both_ref[0, :, chans:], w[1])
        + dot_last(gpg_ref[0], w[2])
    ).astype(BF)
    first = pl.program_id(0) == 0

    @pl.when(first)
    def _():
        b0[...] = out

    @pl.when(jnp.logical_not(first))
    def _():
        b1[...] = out


def back_mix(loc, cum, state, pi, pf, gpg, carry, prior, shift, lower, in_proj, after=()):
    _, rows, chans = state.shape
    width = in_proj.shape[1]
    piece = ((1, rows, chans), lambda g: (g, 0, 0))
    per = ((1, 1, chans), lambda g: (g, 0, 0))
    moved = ((1, 1, chans), lambda g: (g + shift, 0, 0))
    whole = ((rows, width), BF, (rows, width), lambda g: (0, 0))
    return call(
        back_mix_kernel,
        "back_mix",
        (2,),
        [(v, *piece) for v in (loc, cum, state, pi, pf, gpg)]
        + [(carry, *moved), (prior, *moved), fixed(lower), fixed(in_proj)],
        [
            ((2, rows, 2 * chans), BF, (1, rows, 2 * chans), lambda g: (g, 0, 0)),
            whole,
            whole,
            ((2, 1, chans), F32, *per),
        ],
        flops=12 * rows * width * chans,
        after=after,
    )


def total_product(near_count, refs):
    lefts, (near, far) = refs[:-2], refs[-2:]
    return dot_first(stack(*lefts[:near_count]), near[...]) + dot_first(
        stack(*lefts[near_count:]), far[...]
    )


def product_kernel(near_count, me, *refs):
    refs[-1][...] = total_product(near_count, refs[:-1]).astype(BF)


def product_add_kernel(near_count, half, me, *refs):
    got, send, keep = refs[-3:]
    total = (total_product(near_count, refs[:-3]) + got[...].astype(F32)).astype(BF)
    early = pl.program_id(0) < half

    @pl.when(early)
    def _():
        send[...] = total

    @pl.when(jnp.logical_not(early))
    def _():
        keep[...] = total


def product(me, lefts, near, far, bits, size, got=None, after=(), more=0):
    levels = len(bits)
    count = 1 << (levels - 1)
    base = 0 if got is None else count
    top = 2 * count - 1 - base
    units = near.shape[1]
    near_count = len(lefts[0])
    lefts = [*lefts[0], *lefts[1]]

    def place(j, me):
        turned = top - j
        block = me[0]
        for n, bit in enumerate(bits):
            block = block ^ (((turned >> (levels - 1 - n)) & 1) * bit)
        return (0, block)

    if size % 128:
        def ordered(x, rows):
            parts = [
                lax.dynamic_slice_in_dim(x[:rows], place(j, me)[1] * size, size, 1)
                for j in range(count)
            ]
            return jnp.concatenate(parts, axis=1), rows

        lefts = [ordered(*x) for x in lefts]
        count, size = count * size // 128, 128
        position = lambda j, me: (0, j)
    else:
        position = place
    inputs = [(x, (rows, size), position) for x, rows in lefts]
    inputs += [fixed(near), fixed(far)]
    flops = 0
    if got is None:
        out = ((count * size + more, units), BF, (size, units), lambda j, me: (j, 0))
        return call(
            functools.partial(product_kernel, near_count),
            "product", (count,), inputs, [out], flops, after, blocks=me,
        )
    half = count // 2
    inputs.append((got, (size, units), lambda j, me: (j, 0)))
    shape = (half * size, units)
    send = (shape, BF, (size, units), lambda j, me: (jnp.minimum(j, half - 1), 0))
    keep = (shape, BF, (size, units), lambda j, me: (jnp.maximum(j - half, 0), 0))
    return call(
        functools.partial(product_add_kernel, near_count, half),
        "product_add",
        (count,),
        inputs,
        [send, keep],
        flops,
        after,
        blocks=me,
    )


def halve_kernel(half, one, two, send, keep):
    total = (one[...].astype(F32) + two[...].astype(F32)).astype(BF)
    early = pl.program_id(0) < half

    @pl.when(early)
    def _():
        send[...] = total

    @pl.when(jnp.logical_not(early))
    def _():
        keep[...] = total


def halve(one, two, size, after=()):
    count = one.shape[0] // size
    half = count // 2
    units = one.shape[1]
    block = ((size, units), lambda j: (j, 0))
    shape = (half * size, units)
    return call(
        functools.partial(halve_kernel, half),
        "halve",
        (count,),
        [(one, *block), (two, *block)],
        [
            (shape, BF, (size, units), lambda j: (jnp.minimum(j, half - 1), 0)),
            (shape, BF, (size, units), lambda j: (jnp.maximum(j - half, 0), 0)),
        ],
        after=after,
    )


def finish_kernel(turned, one, two, *refs):
    out = refs[-1]
    total = one[...].astype(F32) + two[...].astype(F32)
    if turned:
        out[...] = total.T
    else:
        parts, _, units = out.shape
        for part in range(parts):
            out[part] = total[:, part * units : (part + 1) * units]


def finish(one, two, turned=False, slot=0, parts=1, slots=1, into=None, after=()):
    rows, units = one.shape
    if turned:
        tile = 128 if rows % 128 == 0 else rows
        shape = (units, rows)
        out = pl.BlockSpec((units, tile), lambda n: (0, n))
    else:
        tile = 64 if rows % 64 == 0 else rows
        shape = (slots, rows, units // parts)
        out = pl.BlockSpec((parts, tile, units // parts), lambda n: (slot // parts, n, 0))
    block = pl.BlockSpec((tile, units), lambda n: (n, 0))
    held = [] if into is None else [into]
    waits = [*held, *after]
    count = len(waits)
    return pl.pallas_call(
        lambda one, two, *refs: finish_kernel(turned, one, two, *refs[count:]),
        grid=(rows // tile,),
        in_specs=[block, block] + [ANYWHERE] * count,
        out_specs=out,
        out_shape=sds(shape),
        input_output_aliases={2: 0} if held else {},
        compiler_params=pltpu.CompilerParams(vmem_limit_bytes=VMEM_LIMIT),
        cost_estimate=pl.CostEstimate(flops=0, bytes_accessed=0, transcendentals=0),
        name="finish",
    )(one, two, *waits)


def row_call(kernel, name, arrays, gains, outputs, sums=0, after=(), most=64, more=()):
    rows, width = arrays[0].shape[-2:]
    tile = most if rows % most == 0 else rows

    def block(shape):
        lead = len(shape) - 2
        return (*shape[:-2], tile, shape[-1]), lambda r: (*(0,) * lead, r, 0)

    inputs = [(a, *block(a.shape)) for a in arrays] + [fixed(g) for g in gains]
    results = [(shape, dtype, *block(shape)) for shape, dtype in outputs]
    results += [((1, width), F32, (1, width), lambda r: (0, 0))] * sums + list(more)
    return call(kernel, name, (rows // tile,), inputs, results, after=after)


def add_to(ref, term):
    first = pl.program_id(0) == 0

    @pl.when(first)
    def _():
        ref[...] = term

    @pl.when(jnp.logical_not(first))
    def _():
        ref[...] += term


def first_norm_kernel(x_ref, gain_ref, out):
    x = x_ref[...].astype(F32)
    out[...] = (x * rms_scale(x) * gain_ref[...]).astype(BF)


def plus_kernel(one, two, out):
    out[...] = (one[...].astype(F32) + two[...].astype(F32)).astype(BF)


def plus(one, two, after=()):
    return row_call(plus_kernel, "plus", [one, two], [], [(one.shape, BF)], after=after)


def join_kernel(one, two, top, bottom):
    half = bottom.shape[0]
    rows = 2 * half
    for out, at in ((top, 0), (bottom, half)):
        part = slice(at, at + half)
        out[:half] = (one[part].astype(F32) + two[part].astype(F32)).astype(BF)
    extra = one[rows:].astype(F32) + two[rows:].astype(F32)
    top[half:] = in_two(jnp.broadcast_to(extra[0:1] + extra[1:2], extra.shape))


def join(one, two, after=()):
    rows, width = one.shape[0] - EXTRA, one.shape[1]
    shapes = [(rows // 2 + EXTRA, width), (rows // 2, width)]
    return call(
        join_kernel, "join", (1,), [fixed(one), fixed(two)],
        [(s, BF, s, lambda i: (0, 0)) for s in shapes], after=after,
    )


def middle_kernel(half, x, own, core, hop, own_more, core_more, hop_more, gain, *refs):
    branch_ref, middle_ref, scale_ref, full, out = refs[-5:]
    rows, width = x.shape
    more = own_more[...].astype(F32) + core_more[...].astype(F32) + hop_more[...].astype(F32)
    squares = (more[0:1] + more[1:2])[:, half * rows : (half + 1) * rows]
    scale = lax.rsqrt(upright(squares) / width + EPS)
    branch = own[...].astype(F32) + core[...].astype(F32) + hop[...].astype(F32)
    middle = x[...].astype(F32) + branch * scale[:, :1]
    branch_ref[...] = branch
    scale_ref[...] = scale
    middle_ref[...] = middle
    low = (middle * rms_scale(middle) * gain[...]).astype(BF)
    full[...] = low
    out[...] = low


def middle_half(half, x, own, core, hop, top, gain, begun=(), after=()):
    total, width = x.shape
    rows = total // 2
    part = pl.BlockSpec((rows, width), lambda i: (half, 0))
    alone = pl.BlockSpec((rows, width), lambda i: (0, 0))
    more = pl.BlockSpec((EXTRA, width), lambda i: (total // EXTRA, 0))
    top_more = pl.BlockSpec((EXTRA, width), lambda i: (rows // EXTRA, 0))
    waits = [*begun, *after]
    return pl.pallas_call(
        functools.partial(middle_kernel, half),
        grid=(1,),
        in_specs=[part, part, part, alone, more, more, top_more, pl.BlockSpec((1, width), lambda i: (0, 0))]
        + [ANYWHERE] * len(waits),
        out_specs=[part, part, pl.BlockSpec((rows, 128), lambda i: (half, 0)), part, alone],
        out_shape=[
            sds((total, width)), sds((total, width)), sds((total, 128)), sds((total, width), BF),
            sds((rows + (16 if half == 0 else 0), width), BF),
        ],
        input_output_aliases={8 + n: n for n in range(len(begun))},
        compiler_params=pltpu.CompilerParams(vmem_limit_bytes=VMEM_LIMIT),
        cost_estimate=pl.CostEstimate(flops=0, bytes_accessed=0, transcendentals=0),
        name="middle",
    )(x, own, core, hop, own, core, top, gain, *waits)


def turn_kernel(up, own, core, hop, middle_ref, branch, scale_ref, gain, grad_ref, term, out):
    tile = up.shape[0]
    step = pl.program_id(0)
    rows = out.shape[0] - EXTRA
    grad = own[...].astype(F32) + core[...].astype(F32) + hop[...].astype(F32)
    middle = middle_ref[...]
    scale = rms_scale(middle)
    total = up[...].astype(F32) + norm_back(grad, middle, scale, gain[...])
    low = total.astype(BF)
    grad_ref[...] = total
    out[pl.ds(pl.multiple_of(step * tile, tile), tile), :] = low
    inner = wide(jnp.sum(low.astype(F32) * branch[...], axis=-1, keepdims=True)).T[:EXTRA]
    outer = scale_ref[...].T[:EXTRA]
    high_outer = outer.astype(BF).astype(F32)
    high_inner = inner.astype(BF).astype(F32)
    which = lax.broadcasted_iota(jnp.int32, inner.shape, 0)
    both = jnp.where(which < 2, outer, inner)
    high = jnp.where(which < 2, high_outer, high_inner)
    extra = jnp.where(which % 2 == 0, high, both - high)

    @pl.when(step == 0)
    def _():
        out[rows:, :] = jnp.zeros((EXTRA, out.shape[1]), BF)

    out[rows:, pl.ds(pl.multiple_of(step * tile, tile), tile)] = extra.astype(BF)
    add_to(term, jnp.sum(grad * middle * scale, axis=0, keepdims=True))


def turn(up, own, core, hop, middle, branch, scale, gain, after=()):
    rows, width = up.shape
    shape = (rows + EXTRA, width)
    return row_call(
        turn_kernel, "turn", [up, own, core, hop, middle, branch, scale], [gain],
        [(up.shape, F32)], sums=1, after=after, most=128,
        more=[(shape, BF, shape, lambda r: (0, 0))],
    )


def last_kernel(x_ref, own, core, hop, grad_middle, gain, out, term):
    grad = own[...].astype(F32) + core[...].astype(F32) + hop[...].astype(F32)
    x = x_ref[...].astype(F32)
    scale = rms_scale(x)
    out[...] = grad_middle[...] + norm_back(grad, x, scale, gain[...])
    add_to(term, jnp.sum(grad * x * scale, axis=0, keepdims=True))


def result_kernel(middle, own, core, hop, out):
    out[...] = (
        middle[...] + (own[...].astype(F32) + core[...].astype(F32) + hop[...].astype(F32))
    ).astype(BF)


def in_order(me, total, other):
    odd = (me[0] % 2) == 1
    return (
        odd,
        jnp.where(odd, other[0], total[0]),
        jnp.where(odd, other[1], total[1]),
        jnp.where(odd, total[0], other[0]),
        jnp.where(odd, total[1], other[1]),
    )


def pair_kernel(reverse, me, total, other, pair):
    odd, low_a, low_b, high_a, high_b = in_order(me, total, other)
    pair[0] = low_a * high_a
    pair[1] = low_a * high_b + low_b if reverse else high_a * low_b + high_b


def enter_kernel(reverse, me, total, other, *refs):
    odd, low_a, low_b, high_a, high_b = in_order(me, total, other)
    enter = jnp.zeros_like(low_a)
    for got in reversed(refs[:-1]):
        enter = got[0] * enter + got[1]
    if reverse:
        enter = jnp.where(odd, enter, high_a * enter + high_b)
    else:
        enter = jnp.where(odd, low_a * enter + low_b, enter)
    for g in range(enter.shape[0]):
        refs[-1][g] = enter[g : g + 1]


def chain(me, total, reverse, between=None, beside=None):
    size = lax.axis_size("seq")
    _, groups, chans = total.shape
    other = swap(total, "seq", 1)
    got = between() if between else ()
    whole = (total.shape, F32, total.shape, lambda i, me: (0, 0, 0))
    pair = call(
        functools.partial(pair_kernel, reverse), "pair", (1,), [fixed(total), fixed(other)], [whole],
        after=got, blocks=me,
    )
    sign = -1 if reverse else 1
    reached = [shift(pair, "seq", 2 * sign * d) for d in range(1, size // 2)]
    shape = (groups, 1, chans)
    got = beside(pair) if beside else ()
    return call(
        functools.partial(enter_kernel, reverse), "enter", (1,),
        [fixed(total), fixed(other), *[fixed(r) for r in reached]],
        [(shape, F32, shape, lambda i, me: (0, 0, 0))],
        after=got,
        blocks=me,
    )


def seq_bits():
    size = lax.axis_size("seq")
    bits = []
    bit = 1
    while bit < size:
        bits.append(bit)
        bit *= 2
    return bits


class Weight:
    def __init__(self, me, lefts, near, far, bits, size):
        self.me, self.lefts, self.near, self.far = me, lefts, near, far
        self.bits, self.size, self.level = bits, size, 0

    def begin(self, *earlier, more=0):
        self.send = product(
            self.me, self.lefts, self.near, self.far, self.bits, self.size, after=earlier, more=more
        )
        return self.send

    def go(self, *earlier):
        send = after(self.send, *earlier) if earlier else self.send
        self.got = swap(send, "seq", self.bits[self.level])
        self.level += 1

    def step(self, *earlier):
        if self.level == 1:
            self.send, self.keep = product(
                self.me, self.lefts, self.near, self.far, self.bits, self.size, self.got, after=earlier
            )
        else:
            self.send, self.keep = halve(self.keep, self.got, self.size, after=earlier)
        return self.send

    def last(self):
        return self.level == len(self.bits)


def gain_terms(norm1_term, norm2_term, mixer_term, bound_n, bound_f):
    wt = lax.axis_index("wt")
    span = norm1_term.shape[1] // lax.axis_size("wt")
    norm_terms = jnp.concatenate([norm1_term, norm2_term])

    def part(j):
        return lax.dynamic_slice_in_dim(norm_terms, (wt ^ j) * span, span, 1)

    norms = part(0)
    for j in (1, 2, 3):
        norms = norms + swap(part(j), "wt", j)
    bound_term = jnp.sum(bound_n, axis=(0, 1)) + jnp.sum(bound_f, axis=(0, 1))
    return jnp.stack([norms[0], mixer_term[0], norms[1], bound_term])


GATE_AT, LOWER_AT, UP_AT, LOWER_BITS = "beside", "beside", "pair", "m"
ORDER = (
    ("-p", "-n", "gs", "bb", "us", "-l", "ob", "ls", "ab", "-r", "us", "gf", "bs")
    + ("lf", "as", "os", "bs", "uf", "as", "os", "-1", "bf", "af", "-2", "-3", "of")
)


def on_device(
    tokens,
    in_proj,
    out_proj,
    gate_up,
    down,
    norm1_gain,
    mixer_gain,
    norm2_gain,
    lower_bound,
    cotangent,
):
    width = in_proj.shape[1]
    chans = in_proj.shape[2]
    x = tokens[0]
    g0 = cotangent[0]
    rows = x.shape[0]
    bits = seq_bits()
    y_first = bits
    mixed_order = {"m": bits[1:2] + bits[:1] + bits[2:], "z": bits[1:] + bits[:1], "y": bits}[LOWER_BITS]
    block = width // lax.axis_size("seq")
    me = lax.axis_index("seq").reshape(1).astype(jnp.int32)

    offset = lax.axis_index("wt") * chans
    lower_use = lax.dynamic_slice_in_dim(lower_bound, offset, chans)[None]
    mixer_use = lax.dynamic_slice_in_dim(mixer_gain, offset, chans)[None]
    gain_one, gain_two = norm1_gain[None], norm2_gain[None]

    n0 = row_call(first_norm_kernel, "first_norm", [x], [gain_one], [(x.shape, BF)])
    hop = swap(n0, "wt", 2)
    n1 = swap(n0, "wt", 1)
    g1 = swap(g0, "wt", 1)
    grad_hop = swap(after(g0, n0), "wt", 2)
    pi_n, pf_n, pg_n, loc_n, cum_n, tot = project(n0, n1, in_proj, lower_use)
    gh_n = hidden_grad(g0, g1, down, after=(tot,))
    n2 = after(hop, gh_n)
    n3 = swap(n2, "wt", 1)
    pi_f, pf_f, pg_f, loc_f, cum_f, tot = project(n2, n3, in_proj, lower_use, (tot,))
    enter = chain(me, tot, False)
    state_f, bf0, bf1 = mix(loc_f, cum_f, pg_f, enter, 2, mixer_use, out_proj)
    g2 = after(grad_hop, bf0)
    g3 = swap(g2, "wt", 1)
    state_n, bn0, bn1 = mix(loc_n, cum_n, pg_n, enter, 0, mixer_use, out_proj, after=(bf0,))
    across = join(bf0, swap(bf1, "wt", 1), after=(bn0,))
    hops = [swap(part, "wt", 2) for part in across]
    core = swap(bn1, "wt", 1)
    gh_f = hidden_grad(g2, g3, down, after=(across[1],))
    *begun, half0 = middle_half(0, x, bn0, core, hops[0], hops[0], gain_two, after=(gh_f,))
    branch, middle, scale_two, t0, half1 = middle_half(
        1, x, bn0, core, hops[1], hops[0], gain_two, begun
    )

    hops = [swap(half, "wt", 2) for half in (half0, half1)]
    t1 = [swap(half, "wt", 1) for half in (half0, half1)]
    hid_n, gg_n, gu_n = feed((t0, *t1), gate_up, gh_n)
    kn0, kn1 = feed_back(gg_n, gu_n, gate_up)
    core = swap(kn1, "wt", 1)
    t2 = [after(hop, kn0) for hop in hops]
    t3 = [swap(half, "wt", 1) for half in t2]
    hid_f, gg_f, gu_f = feed((*t2, *t3), gate_up, gh_f)

    def pieces(*arrays):
        return [(v, min(rows, v.shape[0]) // 128 * 128) for v in arrays]

    twos = (pieces(t0, *t1), pieces(*t2, *t3))
    gate = Weight(me, twos, gg_n, gg_f, y_first, block)
    up = Weight(me, twos, gu_n, gu_f, y_first, block)
    lower = Weight(me, (pieces(g0, g1), pieces(g2, g3)), hid_n, hid_f, mixed_order, block)
    kf0, kf1 = feed_back(gg_f, gu_f, gate_up)
    gate.begin(kf0, more=96)
    gate.go()
    across = plus(kf0, swap(kf1, "wt", 1), after=(gate.send,))
    hop = swap(across, "wt", 2)
    lower.begin(across, more=96)
    lower.go()
    up.begin(lower.send, across, more=0)
    ff0, ff1 = feed_out(hid_f, down, after=(up.send,))
    grad_middle, norm2_term, b0 = turn(
        g0, kn0, core, hop, middle, branch, scale_two, gain_two, after=(ff0,)
    )

    hop = swap(b0, "wt", 2)
    b1 = swap(b0, "wt", 1)
    mixed_n, gpg_n, bloc_n, bcum_n, btot, mixer_n = back_local(
        b0, b1, out_proj, pg_n, pf_n, state_n, mixer_use, lower_use
    )
    ffn_across = plus(ff0, swap(ff1, "wt", 1), after=(btot,))
    fn0, fn1 = feed_out(hid_n, down, after=(ffn_across,))
    ffn_core = swap(fn1, "wt", 1)
    b2 = after(hop, fn0)
    b3 = swap(b2, "wt", 1)
    early = (gate.step(b2),) if GATE_AT == "before" else ()
    mixed_f, gpg_f, bloc_f, bcum_f, btot, mixer_f = back_local(
        b2, b3, out_proj, pg_f, pf_f, state_f, mixer_use, lower_use, (btot,), after=early
    )

    def beside(pair):
        if UP_AT == "pair":
            up.go(pair)
        for one, place in ((gate, GATE_AT), (lower, LOWER_AT)):
            if place == "beside":
                pair = one.step(pair)
        return (pair,)

    leave = chain(me, btot, True, None, beside)
    if UP_AT == "leave":
        up.go(leave)
    if GATE_AT == "after":
        gate.step(leave)
        gate.go()
    else:
        gate.go(leave)
    if LOWER_AT == "beside":
        if LOWER_BITS == "z":
            lower.go(leave)
        else:
            lower.go()
    both_f, df0, df1, bound_f = back_mix(
        bloc_f, bcum_f, state_f, pi_f, pf_f, gpg_f, leave, enter, 2, lower_use, in_proj
    )

    def flat(values):
        return values.reshape(2 * rows, values.shape[2])

    normals = (pieces(n0, n1), pieces(n2, n3))
    last_in = Weight(me, normals, flat(gpg_n), flat(gpg_f), y_first, block)
    out = Weight(me, (pieces(b0, b1), pieces(b2, b3)), flat(mixed_n), flat(mixed_f), y_first, block)
    both_n, dn0, dn1, bound_n = None, None, None, None
    token = df0
    weights = {"g": gate, "u": up, "l": lower, "a": last_in, "o": out}
    rounds = list(bits)
    gate_up_grad = in_grad = None
    for kind, act in ORDER:
        if kind in weights:
            one = weights[kind]
            if act == "b":
                token = one.begin(token)
                one.go()
            elif act == "s":
                token = one.step(token)
                one.go()
                while one.level > 2 and not one.last():
                    token = one.step(token)
                    one.go()
            elif kind in "gu":
                slot = "gu".index(kind)
                token = gate_up_grad = finish(
                    one.keep, one.got, slot=slot, slots=2, into=gate_up_grad,
                    after=() if token is gate_up_grad else (token,),
                )
            elif kind == "b":
                token = in_grad = finish(
                    one.keep, one.got, parts=2, slots=3, into=in_grad,
                    after=() if token is in_grad else (token,),
                )
            elif kind == "a":
                token = in_grad = finish(
                    one.keep, one.got, slot=2, slots=3, into=in_grad,
                    after=() if token is in_grad else (token,),
                )
            elif kind == "l":
                token = down_grad = finish(one.keep, one.got, True, after=(token,))
            else:
                token = out_grad = finish(one.keep, one.got, True, after=(token,))
        elif act == "p":
            token = plus(df0, swap(df1, "wt", 1), after=(token,))
            hop = swap(token, "wt", 2)
        elif act == "n":
            both_n, dn0, dn1, bound_n = back_mix(
                bloc_n, bcum_n, state_n, pi_n, pf_n, gpg_n, leave, enter, 0, lower_use, in_proj,
                after=(token,),
            )
            token = dn0
            core = swap(dn1, "wt", 1)
            weights["b"] = Weight(me, normals, flat(both_n), flat(both_f), y_first, block)
        elif act == "l":
            grad_inputs, norm1_term = row_call(
                last_kernel,
                "last",
                [x, dn0, core, hop, grad_middle],
                [gain_one],
                [(x.shape, F32)],
                sums=1,
                after=(token,),
            )
            token = grad_inputs
            ffn_hop = swap(after(ffn_across, token), "wt", 2)
            gains = gain_terms(norm1_term, norm2_term, mixer_n + mixer_f, bound_n, bound_f)
        elif act == "r":
            token = result = row_call(
                result_kernel, "result", [middle, fn0, ffn_core, ffn_hop], [], [(x.shape, BF)],
                after=(token,),
            )
        elif act in "123":
            for _ in range(len(rounds) if act == "3" else 1):
                gains = gains + after(swap(gains, "seq", rounds.pop(0)), token)

    return (
        result[None],
        grad_inputs[None],
        in_grad,
        out_grad,
        gate_up_grad,
        down_grad,
        gains[0],
        gains[1],
        gains[2],
        gains[3],
    )


def solution(mesh):
    placed = (
        P("wt", "seq", None),
        P(None, None, "wt"),
        P("wt", None),
        P(None, None, "wt"),
        P("wt", None),
        P(),
        P(),
        P(),
        P(),
        P("wt", "seq", None),
    )
    return jax.shard_map(
        on_device,
        mesh=mesh,
        in_specs=placed,
        out_specs=(
            P("wt", "seq", None),
            P("wt", "seq", None),
            P(None, "seq", "wt"),
            P("wt", "seq"),
            P(None, "seq", "wt"),
            P("wt", "seq"),
            P("wt"),
            P("wt"),
            P("wt"),
            P("wt"),
        ),
        check_vma=False,
    )
```
